32 devices in a mesh: seq: 8 (over y, x, core), tp: 4 (over z).
Axes of the slice: x: 2, y: 2, z: 4, core: 2. Of those that a mesh axis runs over, the one named last changes fastest.
Arguments:
- tokens: bfloat16 [32768, 512], P(('seq', 'tp')), may hold values from -6 to 6
- ln_gain: float32 [512], replicated, may hold values from 0.25 to 1.75
- in_proj: bfloat16 [2, 512, 256], P(None, None, 'tp'), may hold values from -0.25 to 0.25
- decay_log: float32 [256], P('tp'), as said below
- angle: float32 [256], P('tp'), may hold values from -3.140625 to 3.140625
- out_proj: bfloat16 [2, 256, 512], P(None, 'tp'), may hold values from -0.375 to 0.375
- skip: bfloat16 [512], replicated, may hold values from -4 to 4
- glu_proj: bfloat16 [2, 512, 1024], P(None, None, 'tp'), may hold values from -0.25 to 0.25
- down_proj: bfloat16 [1024, 512], P('tp'), may hold values from -0.5 to 0.5
- lengths: int32 [6], replicated, may hold values from 1 to 28672, as said below
- cotangent: bfloat16 [32768, 512], P(('seq', 'tp')), may hold values from -6 to 6
Outputs:
- result: bfloat16 [32768, 512], P(('seq', 'tp'))
- grad_tokens: float32 [32768, 512], P(('seq', 'tp'))
- grad_gain: float32 [512], replicated
- grad_in_proj: float32 [2, 512, 256], P(None, None, 'tp')
- grad_decay: float32 [256], P('tp')
- grad_angle: float32 [256], P('tp')
- grad_out_proj: float32 [2, 256, 512], P(None, 'tp')
- grad_skip: float32 [512], replicated
- grad_glu: float32 [2, 512, 1024], P(None, None, 'tp')
- grad_down: float32 [1024, 512], P('tp')
The draws below stay inside these ranges and needn't reach their ends.
Inputs may be any that keep to these rules, and one draw needn't show every extreme that they name: 6 positive lengths that sum to 32768; the tokens are packed one sequence after another in this order; the second sequence has exactly 28672 tokens, and the first together with all after the second have 4096. exp(decay_log) lies between 0.2 / 32768 and 1 / 25.
All inputs are finite; a program needn't handle non-finite values.
Results may differ from the reference program's by a relative error of at most 0.025.
Values may be sent and summed in bfloat16 or wider, within the bound.
A program may use at most 256 MiB of HBM per device.

```python
import math
from functools import partial
import jax
import jax.numpy as jnp
from jax import lax

D = 512
N = 256
H = 1024
TOK_DEV = 4096
SHORTS = 4
TOKENS = 32768


def draw_decay_log(key, part):
    key = jax.random.fold_in(key, 5)
    key_pick, key_slow, key_fast = jax.random.split(key, 3)
    slow_share = 0.5
    picked = jax.random.uniform(key_pick, (N,), dtype=jnp.float32) < slow_share
    slow_rates = jax.random.uniform(key_slow, (N,), dtype=jnp.float32, minval=math.log(0.2), maxval=math.log(2.0)) - math.log(TOKENS)
    fast_rates = jax.random.uniform(key_fast, (N,), dtype=jnp.float32, minval=math.log(1.0 / 50.0), maxval=math.log(1.0 / 25.0))
    return jnp.where(picked, slow_rates, fast_rates).astype(jnp.float32)


def draw_lengths(key, part):
    key = jax.random.fold_in(key, 11)
    key_head, key_parts = jax.random.split(key, 2)
    head_len = jax.random.randint(key_head, (), 1, TOK_DEV - SHORTS + 1, dtype=jnp.int32)
    tail_len = (TOK_DEV - head_len).astype(jnp.int32)
    weights = jax.random.randint(key_parts, (SHORTS,), 1, 9, dtype=jnp.int32)
    spare = tail_len - SHORTS
    running = jnp.cumsum(weights).astype(jnp.int32)
    bounds = spare * running // running[-1]
    pieces = 1 + jnp.diff(jnp.concatenate([jnp.zeros((1,), jnp.int32), bounds]))
    long_len = jnp.full((1,), TOKENS - TOK_DEV, jnp.int32)
    return jnp.concatenate([head_len[None], long_len, pieces.astype(jnp.int32)]).astype(jnp.int32)


def block_scale(own_key, extent, cuts, low, top_value):
    gain = 1.0
    for axis_at, parts in cuts:
        draws = jax.random.uniform(jax.random.fold_in(jax.random.fold_in(own_key, 6), axis_at), (parts,), jnp.float32, low / len(cuts), top_value / len(cuts))
        gain = gain * jnp.repeat(jnp.exp(draws), extent[axis_at] // parts).reshape((-1,) + (1,) * (len(extent) - 1 - axis_at))
    return gain


def gaussian(own_key, dims, scale, reach, shards=(), kind=jnp.bfloat16):
    entries = scale * jax.random.normal(own_key, dims, jnp.float32)
    if shards:
        entries = entries * block_scale(own_key, dims, shards, -0.22, 0.18)
    return jnp.clip(entries, -reach, reach).astype(kind)


def setup_inputs(seed: int = 0) -> dict:
    streams_of = jax.random.split(jax.random.key(seed), 12)
    tokens = gaussian(streams_of[0], (TOKENS, D), 1.0, 6.0, ((0, 32),))
    ln_gain = jnp.clip(1.0 + 0.15 * jax.random.normal(streams_of[1], (D,), jnp.float32), 0.25, 1.75)
    in_proj = gaussian(streams_of[2], (2, D, N), D ** -0.5, 0.25, ((2, 4),))
    decay_log = draw_decay_log(jax.random.fold_in(streams_of[11], 71), 0)
    angle = jnp.clip(jax.random.uniform(streams_of[4], (N,), jnp.float32, -3.140625, 3.140625), -3.140625, 3.140625)
    out_proj = gaussian(streams_of[5], (2, N, D), N ** -0.5, 0.375, ((1, 4),))
    skip = gaussian(streams_of[6], (D,), 0.7, 4.0)
    glu_proj = gaussian(streams_of[7], (2, D, H), D ** -0.5, 0.25, ((2, 4),))
    down_proj = gaussian(streams_of[8], (H, D), (H // 8) ** -0.5, 0.5, ((0, 4),))
    lengths = draw_lengths(jax.random.fold_in(streams_of[11], 71), 0)
    cotangent = gaussian(streams_of[10], (TOKENS, D), 1.0, 6.0, ((0, 32),))
    return dict(tokens=tokens, ln_gain=ln_gain, in_proj=in_proj, decay_log=decay_log, angle=angle, out_proj=out_proj, skip=skip, glu_proj=glu_proj, down_proj=down_proj, lengths=lengths, cotangent=cotangent)


epsilon = 1e-05

@jax.custom_vjp
def low(v):
    return lax.optimization_barrier(v.astype(jnp.bfloat16)).astype(jnp.float32)

@jax.custom_vjp
def low_back(v):
    return v

def low_keep(v):
    return (low(v), None)

def low_pass(kept, grad):
    return (grad,)

def back_keep(v):
    return (v, None)

def back_low(kept, grad):
    return (low(grad),)
low.defvjp(low_keep, low_pass)
low_back.defvjp(back_keep, back_low)

def complex_mul(left_re, left_im, right_re, right_im):
    return (left_re * right_re - left_im * right_im, left_re * right_im + left_im * right_re)

def compose(earlier, latter):
    scaled = complex_mul(latter[0], latter[1], earlier[0], earlier[1])
    moved = complex_mul(latter[0], latter[1], earlier[2], earlier[3])
    return (scaled[0], scaled[1], moved[0] + latter[2], moved[1] + latter[3])

def decay_terms(decay_log, angle):
    rate_step = jnp.exp(decay_log)
    radius = jnp.exp(-rate_step)
    return (radius * jnp.cos(angle), radius * jnp.sin(angle), jnp.sqrt(-jnp.expm1(-2.0 * rate_step)))

def layer(keep_mask, tokens, ln_gain, in_proj, decay_log, angle, out_proj, skip, glu_proj, down_proj):
    highest = lax.Precision.HIGHEST
    row_mean = lax.optimization_barrier(jnp.mean(tokens, axis=-1, keepdims=True))
    row_var = lax.optimization_barrier(jnp.mean(tokens * tokens, axis=-1, keepdims=True)) - row_mean * row_mean
    centred = (tokens - row_mean) * lax.rsqrt(row_var + epsilon)
    normed = low(centred * ln_gain)
    proj_re = low_back(jnp.dot(normed, in_proj[0], precision=highest))
    proj_im = low_back(jnp.dot(normed, in_proj[1], precision=highest))
    lam_re, lam_im, gamma = decay_terms(decay_log, angle)
    scanned = lax.associative_scan(compose, (lam_re * keep_mask, lam_im * keep_mask, gamma * proj_re, gamma * proj_im), axis=0)
    state_re = low(scanned[2])
    state_im = low(scanned[3])
    mixed = jnp.dot(state_re, out_proj[0], precision=highest) - jnp.dot(state_im, out_proj[1], precision=highest) + skip * normed
    mixed = low_back(mixed)
    act = low(jax.nn.gelu(mixed))
    value = low_back(jnp.dot(act, glu_proj[0], precision=highest))
    gate = low_back(jnp.dot(act, glu_proj[1], precision=highest))
    hidden = low(value * jax.nn.sigmoid(gate))
    return tokens + jnp.dot(hidden, down_proj, precision=highest)

def reference(tokens, ln_gain, in_proj, decay_log, angle, out_proj, skip, glu_proj, down_proj, lengths, cotangent):
    starts = (jnp.cumsum(lengths) - lengths).astype(jnp.int32)
    positions = jnp.arange(TOKENS, dtype=jnp.int32)
    keep_mask = 1.0 - jnp.any(positions[:, None] == starts[None, :], axis=1).astype(jnp.float32)
    keep_mask = keep_mask[:, None]
    outputs, pullback = jax.vjp(partial(layer, keep_mask), tokens.astype(jnp.float32), ln_gain, in_proj.astype(jnp.float32), decay_log, angle, out_proj.astype(jnp.float32), skip.astype(jnp.float32), glu_proj.astype(jnp.float32), down_proj.astype(jnp.float32))
    grads = pullback(cotangent.astype(jnp.float32))
    return (outputs.astype(jnp.bfloat16), grads[0], grads[1], grads[2], grads[3], grads[4], grads[5], grads[6], grads[7], grads[8])
```

```python
import functools
import jax
import jax.numpy as jnp
from jax import lax
from jax.experimental import pallas as pl
from jax.experimental.pallas import tpu as pltpu
from jax.sharding import PartitionSpec as P

epsilon = 1e-05
MESH = pl.DeviceIdType.MESH
F32 = jnp.float32
BF16 = jnp.bfloat16
GROUPS = 2


def dot(left, right):
    return jnp.dot(left, right, preferred_element_type=F32)


def dot_nt(left, right):
    return lax.dot_general(left, right, (((1,), (1,)), ((), ())), preferred_element_type=F32)


def complex_mul(left_re, left_im, right_re, right_im):
    return (left_re * right_re - left_im * right_im, left_re * right_im + left_im * right_re)


def load(ref, rows):
    return jnp.concatenate([ref[tile, rows, :] for tile in range(ref.shape[0])], 1)


def save(ref, rows, value):
    for tile in range(ref.shape[0]):
        ref[tile, rows, :] = value[:, tile * 128 : tile * 128 + 128]


def power(base, exponent):
    result = None
    square = base
    while exponent:
        if exponent & 1:
            result = square if result is None else complex_mul(*result, *square)
        exponent >>= 1
        if exponent:
            square = complex_mul(*square, *square)
    return result


def layer_kernel(
    S,
    T,
    lengths,
    tokens,
    cot,
    gain,
    skip,
    rates,
    w_in,
    w_out,
    glu,
    down,
    result,
    grad_tokens,
    small,
    grad_in,
    grad_out,
    grad_glu,
    grad_down,
    centred,
    inv_std,
    normed,
    normed_t,
    cot_t,
    proj,
    keep,
    keep_next,
    state,
    state_t,
    act,
    act_t,
    d_gelu,
    d_act,
    summed,
    d_mixed,
    adjoint,
    d_proj,
    hidden,
    d_value,
    d_gate,
    seg_carry,
    sums,
    state_tp,
    state_seq,
    adj_tp,
    adj_seq,
    send_sem,
    recv_sem,
):
    R, D = tokens.shape
    N = w_in.shape[1] // 2
    segments = 8 * GROUPS
    L = R // segments
    s = lax.axis_index("seq")
    t = lax.axis_index("tp")
    first = (s * T + t) * R

    peers_tp = [lax.rem(t + k, T) for k in range(1, T)]
    peers_seq = [lax.rem(s + k, S) for k in range(1, S)]
    barrier = pltpu.get_barrier_semaphore()
    for peer in peers_tp:
        pl.semaphore_signal(barrier, inc=1, device_id=(s, peer), device_id_type=MESH)
    for peer in peers_seq:
        pl.semaphore_signal(barrier, inc=1, device_id=(peer, t), device_id_type=MESH)

    starts = []
    total = jnp.int32(0)
    for index in range(lengths.shape[0]):
        starts.append(total)
        total = total + lengths[index]

    def keeps(position):
        hit = position == starts[0]
        for start in starts[1:]:
            hit = hit | (position == start)
        return jnp.where(hit, 0.0, 1.0)

    def clear(low, high):
        hit = (starts[0] >= low) & (starts[0] < high)
        for start in starts[1:]:
            hit = hit | ((start >= low) & (start < high))
        return jnp.where(hit, 0.0, 1.0)

    lam_re = rates[0:1, :N]
    lam_im = rates[0:1, N:]
    gamma = rates[1:2, :N]
    gamma_signed = jnp.concatenate([gamma, -gamma], 1)
    gain_row = gain[...]
    skip_row = skip[...].astype(F32)

    NORM_ROWS = 128

    @pl.loop(0, R // NORM_ROWS)
    def _(tile):
        at = pl.multiple_of(tile * NORM_ROWS, NORM_ROWS)
        rows = pl.ds(at, NORM_ROWS)
        x = tokens[rows, :].astype(F32)
        mean = jnp.mean(x, 1, keepdims=True)
        inv = lax.rsqrt(jnp.mean(x * x, 1, keepdims=True) - mean * mean + epsilon)
        c = (x - mean) * inv
        centred[rows, :] = c
        inv_std[rows, :] = jnp.broadcast_to(inv, (NORM_ROWS, 128))
        n = (c * gain_row).astype(BF16)
        normed[rows, :] = n
        normed_t[:, rows] = n.T
        cot_t[:, rows] = cot[rows, :].T
        position = first + at + lax.broadcasted_iota(jnp.int32, (NORM_ROWS, 128), 0)
        keep[rows, :] = keeps(position)
        keep_next[rows, :] = keeps(position + 1)
        save(proj, rows, dot(n, w_in[...]) * gamma_signed)

    low8_re = jnp.broadcast_to(lam_re, (8, N))
    low8_im = jnp.broadcast_to(lam_im, (8, N))

    def rows_of(group, step):
        return pl.ds(group * 8 * L + step, 8, stride=L)

    def spread(row):
        return jnp.concatenate([row] * (N // 128), 1)

    def scan_step(values, mask, add, sign):
        new_re, new_im = complex_mul(low8_re, sign * low8_im, *(value * mask for value in values))
        return (new_re + add[:, :N], new_im + add[:, N:])

    zero8 = jnp.zeros((8, N), F32)
    none = tuple((zero8, zero8) for _ in range(GROUPS))

    def forward_step(step, carry):
        return tuple(
            scan_step(
                carry[group],
                spread(keep[rows_of(group, step), :]),
                load(proj, rows_of(group, step)),
                -1.0,
            )
            for group in range(GROUPS)
        )

    def segment_rows(finals):
        return [
            (finals[group][0][lane : lane + 1], finals[group][1][lane : lane + 1])
            for group in range(GROUPS)
            for lane in range(8)
        ]

    def fold(start, factor, items, masks, taken):
        before = []
        carry = start
        for (item_re, item_im), mask, take in zip(items, masks, taken):
            before.append(carry)
            moved = complex_mul(*factor, *carry)
            longer = (moved[0] * mask + item_re, moved[1] * mask + item_im)
            if take is None:
                carry = longer
            else:
                carry = tuple(jnp.where(take, new, old) for new, old in zip(longer, carry))
        return carry, before

    zero1 = (jnp.zeros((1, N), F32), jnp.zeros((1, N), F32))
    lam = (lam_re, lam_im)
    conj = (lam_re, -lam_im)

    def unpack(row):
        return (row[:, :N], row[:, N:])

    def exchange(own, factor, tp_buf, seq_buf, base, forward):
        shift = 0 if forward else 1
        factor_tp = power(factor, R)
        factor_seq = power(factor_tp, T)
        order = (lambda items: items) if forward else (lambda items: items[::-1])
        tp_buf[t] = jnp.broadcast_to(jnp.concatenate(own, 1), tp_buf.shape[1:])
        copies = [
            pltpu.make_async_remote_copy(
                src_ref=tp_buf.at[t],
                dst_ref=tp_buf.at[t],
                send_sem=send_sem.at[base + k],
                recv_sem=recv_sem.at[base + k],
                device_id=(s, peer),
                device_id_type=MESH,
            )
            for k, peer in enumerate(peers_tp)
        ]
        for copy in copies:
            copy.start()
        for copy in copies:
            copy.wait()
        items = order([unpack(tp_buf[z, 0:1, :]) for z in range(T)])

        def masks_tp(row):
            return order(
                [clear(row + z * R + shift, row + (z + 1) * R + shift) for z in range(T)]
            )

        masks = masks_tp(s * T * R)
        block, _ = fold(zero1, factor_tp, items, masks, [None] * T)
        seq_buf[s] = jnp.broadcast_to(jnp.concatenate(block, 1), seq_buf.shape[1:])
        copies = [
            pltpu.make_async_remote_copy(
                src_ref=seq_buf.at[s],
                dst_ref=seq_buf.at[s],
                send_sem=send_sem.at[base + T - 1 + k],
                recv_sem=recv_sem.at[base + T - 1 + k],
                device_id=(peer, t),
                device_id_type=MESH,
            )
            for k, peer in enumerate(peers_seq)
        ]
        for copy in copies:
            copy.start()
        return copies, items, masks, factor_tp, factor_seq

    def arrived(pending, seq_buf, forward):
        copies, items, masks, factor_tp, factor_seq = pending
        shift = 0 if forward else 1
        for copy in copies:
            copy.wait()
        order = (lambda items: items) if forward else (lambda items: items[::-1])

        def before(other, mine):
            return other < mine if forward else other > mine

        blocks = order(list(range(S)))
        carry, _ = fold(
            zero1,
            factor_seq,
            [unpack(seq_buf[block, 0:1, :]) for block in blocks],
            [clear(block * T * R + shift, (block + 1) * T * R + shift) for block in blocks],
            [before(block, s) for block in blocks],
        )
        carry, _ = fold(carry, factor_tp, items, masks, [before(z, t) for z in order(list(range(T)))])
        return carry

    finals = segment_rows(lax.fori_loop(0, L, forward_step, none))
    seg_masks = [clear(first + index * L, first + (index + 1) * L) for index in range(segments)]
    factor_seg = power(conj, L)
    own, _ = fold(zero1, factor_seg, finals, seg_masks, [None] * segments)
    pl.semaphore_wait(barrier, T - 1 + S - 1)
    pending = exchange(own, conj, state_tp, state_seq, 0, True)
    carry = arrived(pending, state_seq, True)
    _, entering = fold(carry, factor_seg, finals, seg_masks, [None] * segments)
    for index, (row_re, row_im) in enumerate(entering):
        seg_carry[index : index + 1, :] = jnp.concatenate([row_re, row_im], 1)

    def write_state(step, carry):
        new = forward_step(step, carry)
        for group in range(GROUPS):
            save(state, rows_of(group, step), jnp.concatenate(new[group], 1))
        return new

    def entering_groups():
        return tuple(
            unpack(seg_carry[group * 8 : group * 8 + 8, :]) for group in range(GROUPS)
        )

    lax.fori_loop(0, L, write_state, entering_groups())

    MIX_ROWS = 128

    @pl.loop(0, R // MIX_ROWS)
    def _(tile):
        rows = pl.ds(pl.multiple_of(tile * MIX_ROWS, MIX_ROWS), MIX_ROWS)
        low = load(state, rows).astype(BF16)
        state_t[:, rows] = low.T
        x = dot(low, w_out[...]) + skip_row * normed[rows, :].astype(F32)
        scale = 0.7978845608028654
        th = jnp.tanh(scale * (x + 0.044715 * x * x * x))
        half = 0.5 * (1.0 + th)
        a = (x * half).astype(BF16)
        act[rows, :] = a
        act_t[:, rows] = a.T
        d_gelu[rows, :] = half + 0.5 * x * (1.0 - th * th) * scale * (1.0 + 0.134145 * x * x)

    UNIT_ROWS = 256
    for offset in range(T):
        c = lax.rem(t + offset, T)

        @pl.loop(0, R // UNIT_ROWS)
        def _(tile):
            rows = pl.ds(pl.multiple_of(tile * UNIT_ROWS, UNIT_ROWS), UNIT_ROWS)
            a = act[rows, :]
            value = dot(a, glu[c, 0])
            gate = dot(a, glu[c, 1])
            sigma = 0.5 * jnp.tanh(0.5 * gate) + 0.5
            gated = value * sigma
            h = gated.astype(BF16)
            hidden[rows, :] = h
            d_h = dot_nt(cot[rows, :], down[c])
            d_v = (d_h * sigma).astype(BF16)
            d_g = (d_h * gated * (1.0 - sigma)).astype(BF16)
            d_value[rows, :] = d_v
            d_gate[rows, :] = d_g
            added = dot(h, down[c])
            d_a = dot_nt(d_v, glu[c, 0]) + dot_nt(d_g, glu[c, 1])
            if offset > 0:
                added = added + summed[rows, :]
                d_a = d_a + d_act[rows, :]
            if offset < T - 1:
                summed[rows, :] = added
                d_act[rows, :] = d_a
            else:
                result[rows, :] = (tokens[rows, :].astype(F32) + added).astype(BF16)
                d_m = (d_gelu[rows, :] * d_a).astype(BF16)
                d_mixed[rows, :] = d_m
                save(adjoint, rows, dot_nt(d_m, w_out[...]))

        @pl.loop(0, D // 128)
        def _(tile):
            rows = pl.ds(pl.multiple_of(tile * 128, 128), 128)
            grad_down[c, rows, :] = dot(cot_t[rows, :], hidden[...]).astype(BF16)
            grad_glu[c, 0, rows, :] = dot(act_t[rows, :], d_value[...]).astype(BF16)
            grad_glu[c, 1, rows, :] = dot(act_t[rows, :], d_gate[...]).astype(BF16)

    def backward_step(index, carry):
        step = L - 1 - index
        return tuple(
            scan_step(
                carry[group],
                spread(keep_next[rows_of(group, step), :]),
                load(adjoint, rows_of(group, step)),
                1.0,
            )
            for group in range(GROUPS)
        )

    finals = segment_rows(lax.fori_loop(0, L, backward_step, none))[::-1]
    seg_masks = [
        clear(first + index * L + 1, first + (index + 1) * L + 1) for index in range(segments)
    ][::-1]
    factor_seg = power(lam, L)
    own, _ = fold(zero1, factor_seg, finals, seg_masks, [None] * segments)
    pending = exchange(own, lam, adj_tp, adj_seq, T + S - 2, False)

    @pl.loop(0, 2 * N // 128)
    def _(tile):
        rows = pl.ds(pl.multiple_of(tile * 128, 128), 128)
        grad_out[rows, :] = dot(state_t[rows, :], d_mixed[...]).astype(BF16)

    carry = arrived(pending, adj_seq, False)
    _, entering = fold(carry, factor_seg, finals, seg_masks, [None] * segments)
    entering = entering[::-1]
    groups = tuple(
        tuple(
            jnp.concatenate([entering[group * 8 + lane][part] for lane in range(8)], 0)
            for part in range(2)
        )
        for group in range(GROUPS)
    )
    sums[...] = jnp.zeros_like(sums)

    def adjoint_step(step, carry, previous):
        new = []
        add_re = zero8
        add_im = zero8
        add_gamma = zero8
        for group in range(GROUPS):
            rows = rows_of(group, step)
            b = scan_step(carry[group], spread(keep_next[rows, :]), load(adjoint, rows), 1.0)
            new.append(b)
            save(adjoint, rows, jnp.concatenate(b, 1))
            u = unpack(load(proj, rows))
            v = previous(group, step)
            mask = spread(keep[rows, :])
            add_re = add_re + mask * (b[0] * v[0] + b[1] * v[1])
            add_im = add_im + mask * (b[0] * v[1] - b[1] * v[0])
            add_gamma = add_gamma + b[0] * u[0] + b[1] * u[1]
        return tuple(new), (add_re, add_im, add_gamma)

    def adjoint_body(index, carry):
        values, totals = carry
        values, added = adjoint_step(
            L - 1 - index, values, lambda group, step: unpack(load(state, rows_of(group, step - 1)))
        )
        return values, tuple(total + add for total, add in zip(totals, added))

    values, totals = lax.fori_loop(0, L - 1, adjoint_body, (groups, (zero8, zero8, zero8)))
    inside = entering_groups()
    _, added = adjoint_step(0, values, lambda group, step: inside[group])
    totals = [
        jnp.sum(total + add, 0, keepdims=True) for total, add in zip(totals, added)
    ]
    small[2:3, :] = jnp.concatenate(totals[:2], 1)
    small[3:4, :] = jnp.concatenate([totals[2] / gamma, jnp.zeros_like(gamma)], 1)
    small[4:8, :] = jnp.zeros((4, D), F32)

    LAST_ROWS = 128

    @pl.loop(0, R // LAST_ROWS)
    def _(tile):
        rows = pl.ds(pl.multiple_of(tile * LAST_ROWS, LAST_ROWS), LAST_ROWS)
        d_p = (load(adjoint, rows) * gamma_signed).astype(BF16)
        d_proj[rows, :] = d_p
        d_m = d_mixed[rows, :].astype(F32)
        d_n = dot_nt(d_p, w_in[...]) + d_m * skip_row
        c = centred[rows, :]
        sums[0:8, :] += jnp.sum((d_n * c).reshape(LAST_ROWS // 8, 8, D), 0)
        sums[8:16, :] += jnp.sum(
            (d_m * normed[rows, :].astype(F32)).reshape(LAST_ROWS // 8, 8, D), 0
        )
        d_c = d_n * gain_row
        mean = jnp.mean(d_c, 1, keepdims=True)
        cross = jnp.mean(d_c * c, 1, keepdims=True)
        inv = inv_std[rows, 0:1]
        grad_tokens[rows, :] = cot[rows, :].astype(F32) + inv * (d_c - mean - c * cross)

    small[0:1, :] = jnp.sum(sums[0:8, :], 0, keepdims=True)
    small[1:2, :] = jnp.sum(sums[8:16, :], 0, keepdims=True)

    @pl.loop(0, D // 128)
    def _(tile):
        rows = pl.ds(pl.multiple_of(tile * 128, 128), 128)
        grad_in[rows, :] = dot(normed_t[rows, :], d_proj[...]).astype(BF16)


def decay_terms(decay_log, angle):
    rate_step = jnp.exp(decay_log)
    radius = jnp.exp(-rate_step)
    return (
        radius * jnp.cos(angle),
        radius * jnp.sin(angle),
        jnp.sqrt(-jnp.expm1(-2.0 * rate_step)),
    )


def local(
    S,
    T,
    tokens,
    ln_gain,
    in_proj,
    decay_log,
    angle,
    out_proj,
    skip,
    glu_proj,
    down_proj,
    lengths,
    cotangent,
):
    R, D = tokens.shape
    n = in_proj.shape[2]
    N = n * T
    hidden = down_proj.shape[0]
    w_in = lax.all_gather(in_proj, "tp", axis=2, tiled=True)
    w_in = jnp.concatenate([w_in[0], w_in[1]], 1)
    w_out = lax.all_gather(out_proj, "tp", axis=1, tiled=True).reshape(2 * N, D)
    glu = lax.all_gather(glu_proj, "tp")
    down = lax.all_gather(down_proj, "tp")
    lam_re, lam_im, gamma = decay_terms(
        lax.all_gather(decay_log, "tp", tiled=True), lax.all_gather(angle, "tp", tiled=True)
    )
    rates = jnp.stack([jnp.concatenate([lam_re, lam_im]), jnp.concatenate([gamma, gamma])])
    rates = jnp.concatenate([rates, jnp.zeros((6, 2 * N), F32)])
    links = 2 * (T - 1 + S - 1)
    vmem = pl.BlockSpec(memory_space=pltpu.VMEM)
    outs = pl.pallas_call(
        functools.partial(layer_kernel, S, T),
        out_shape=(
            jax.ShapeDtypeStruct((R, D), BF16),
            jax.ShapeDtypeStruct((R, D), F32),
            jax.ShapeDtypeStruct((8, D), F32),
            jax.ShapeDtypeStruct((D, 2 * N), BF16),
            jax.ShapeDtypeStruct((2 * N, D), BF16),
            jax.ShapeDtypeStruct((T, 2, D, hidden), BF16),
            jax.ShapeDtypeStruct((T, D, hidden), BF16),
        ),
        in_specs=[pl.BlockSpec(memory_space=pltpu.SMEM)] + [vmem] * 9,
        out_specs=(vmem,) * 7,
        scratch_shapes=[
            pltpu.VMEM((R, D), F32),
            pltpu.VMEM((R, 128), F32),
            pltpu.VMEM((R, D), BF16),
            pltpu.VMEM((D, R), BF16),
            pltpu.VMEM((D, R), BF16),
            pltpu.VMEM((2 * N // 128, R, 128), F32),
            pltpu.VMEM((R, 128), F32),
            pltpu.VMEM((R, 128), F32),
            pltpu.VMEM((2 * N // 128, R, 128), F32),
            pltpu.VMEM((2 * N, R), BF16),
            pltpu.VMEM((R, D), BF16),
            pltpu.VMEM((D, R), BF16),
            pltpu.VMEM((R, D), F32),
            pltpu.VMEM((R, D), F32),
            pltpu.VMEM((R, D), F32),
            pltpu.VMEM((R, D), BF16),
            pltpu.VMEM((2 * N // 128, R, 128), F32),
            pltpu.VMEM((R, 2 * N), BF16),
            pltpu.VMEM((R, hidden), BF16),
            pltpu.VMEM((R, hidden), BF16),
            pltpu.VMEM((R, hidden), BF16),
            pltpu.VMEM((8 * GROUPS, 2 * N), F32),
            pltpu.VMEM((16, D), F32),
            pltpu.VMEM((T, 8, 2 * N), F32),
            pltpu.VMEM((S, 8, 2 * N), F32),
            pltpu.VMEM((T, 8, 2 * N), F32),
            pltpu.VMEM((S, 8, 2 * N), F32),
            pltpu.SemaphoreType.DMA((links,)),
            pltpu.SemaphoreType.DMA((links,)),
        ],
        compiler_params=pltpu.CompilerParams(
            collective_id=0, has_side_effects=True, vmem_limit_bytes=58 * 2**20
        ),
    )(
        lengths,
        tokens,
        cotangent,
        ln_gain.reshape(1, D),
        skip.reshape(1, D),
        rates,
        w_in,
        w_out,
        glu,
        down,
    )
    result, grad_tokens, small, grad_in, grad_out, grad_glu, grad_down = outs
    small = lax.psum(small, ("seq", "tp"))
    t = lax.axis_index("tp")

    def reduced(part):
        part = lax.psum_scatter(part, "tp", scatter_dimension=0, tiled=True)
        return lax.psum(part, "seq").astype(F32)

    grad_in = grad_in.reshape(D, 2, T, n).transpose(2, 1, 0, 3).reshape(T * 2, D, n)
    grad_in = reduced(grad_in)
    grad_out = grad_out.reshape(2, T, n, D).transpose(1, 0, 2, 3).reshape(T * 2, n, D)
    grad_out = reduced(grad_out)
    grad_glu = reduced(grad_glu.reshape(T * 2, D, hidden))
    grad_down = reduced(grad_down)[0].T

    def mine(row):
        return lax.dynamic_slice_in_dim(row, t * n, n)

    g_re, g_im, g_gamma = (mine(small[2, :N]), mine(small[2, N:]), mine(small[3, :N]))
    _, pull = jax.vjp(decay_terms, decay_log, angle)
    grad_decay, grad_angle = pull((g_re, g_im, g_gamma))
    return (
        result,
        grad_tokens,
        small[0],
        grad_in,
        grad_decay,
        grad_angle,
        grad_out,
        small[1],
        grad_glu,
        grad_down,
    )


def solution(mesh):
    in_specs = (
        P(("seq", "tp"), None),
        P(),
        P(None, None, "tp"),
        P("tp"),
        P("tp"),
        P(None, "tp", None),
        P(),
        P(None, None, "tp"),
        P("tp", None),
        P(),
        P(("seq", "tp"), None),
    )
    out_specs = (
        P(("seq", "tp"), None),
        P(("seq", "tp"), None),
        P(),
        P(None, None, "tp"),
        P("tp"),
        P("tp"),
        P(None, "tp", None),
        P(),
        P(None, None, "tp"),
        P("tp", None),
    )
    return jax.shard_map(
        functools.partial(local, mesh.shape["seq"], mesh.shape["tp"]),
        mesh=mesh,
        in_specs=in_specs,
        out_specs=out_specs,
        check_vma=False,
    )
```

```python
import functools
import types
import jax
import jax.numpy as jnp
from jax import lax
from jax.experimental import pallas as pl
from jax.experimental.pallas import tpu as pltpu
from jax.sharding import PartitionSpec as P

epsilon = 1e-05
MESH = pl.DeviceIdType.MESH
F32 = jnp.float32
BF16 = jnp.bfloat16
GROUPS = 2
SEGMENTS = 8 * GROUPS
BLOCK = SEGMENTS * SEGMENTS


def dot(left, right):
    return jnp.dot(left, right, preferred_element_type=F32)


def dot_nt(left, right):
    return lax.dot_general(left, right, (((1,), (1,)), ((), ())), preferred_element_type=F32)


def complex_mul(left_re, left_im, right_re, right_im):
    return (left_re * right_re - left_im * right_im, left_re * right_im + left_im * right_re)


def power(base, exponent):
    result = None
    square = base
    while exponent:
        if exponent & 1:
            result = square if result is None else complex_mul(*result, *square)
        exponent >>= 1
        if exponent:
            square = complex_mul(*square, *square)
    return result


class Links:
    def __init__(self, send_sem, recv_sem):
        self.send_sem = send_sem
        self.recv_sem = recv_sem
        self.started = []

    def send(self, source, target, device):
        index = len(self.started)
        copy = pltpu.make_async_remote_copy(
            src_ref=source,
            dst_ref=target,
            send_sem=self.send_sem.at[index],
            recv_sem=self.recv_sem.at[index],
            device_id=device,
            device_id_type=MESH,
        )
        copy.start()
        self.started.append(copy)
        return copy

    def close(self):
        for copy in self.started:
            copy.wait_send()


def arrive(copies):
    for copy in copies:
        copy.wait_recv()


class Gather:
    def __init__(self, place, buffer):
        self.place = place
        self.buffer = buffer

    def over_tp(self):
        p = self.place
        self.copies = [
            p.links.send(
                self.buffer.at[0, p.chip, p.core],
                self.buffer.at[p.T - k, p.chip, p.core],
                (p.s, lax.rem(p.t + k, p.T)),
            )
            for k in range(1, p.T)
        ]

    def over_plane(self):
        p = self.place
        arrive(self.copies)
        mine = self.buffer.at[pl.ds(1, p.T - 1), p.chip, p.core]
        self.copies = [p.links.send(mine, mine, device) for _, device in p.chips]

    def over_cores(self):
        p = self.place
        arrive(self.copies)
        mine = self.buffer.at[pl.ds(1, p.T - 1), :, p.core]
        self.copies = [p.links.send(mine, mine, p.sibling)]

    def finish(self):
        arrive(self.copies)


class Reduce:
    def __init__(self, place, full, halves, eighths, summed):
        self.place = place
        self.full = full
        self.halves = halves
        self.eighths = eighths
        self.summed = summed

    def over_cores(self):
        p = self.place
        self.copies = [
            p.links.send(self.full.at[:, :, 1 - p.core], self.halves, p.sibling)
        ]

    def over_plane(self):
        p = self.place
        arrive(self.copies)
        parts, chips = self.halves.shape[:2]

        @pl.loop(0, parts * chips)
        def _(index):
            part, chip = (lax.div(index, chips), lax.rem(index, chips))
            self.halves[part, chip] = (
                self.full[part, chip, p.core].astype(F32) + self.halves[part, chip].astype(F32)
            ).astype(BF16)

        self.copies = [
            p.links.send(self.halves.at[:, chip], self.eighths.at[k], device)
            for k, (chip, device) in enumerate(p.chips)
        ]

    def sum_plane(self):
        p = self.place
        arrive(self.copies)

        @pl.loop(0, self.halves.shape[0])
        def _(part):
            total = self.halves[part, p.chip].astype(F32)
            for k in range(len(p.chips)):
                total = total + self.eighths[k, part].astype(F32)
            self.summed[part] = total.astype(BF16)


class Spread:
    def __init__(self, place, buffer):
        self.place = place
        self.buffer = buffer

    def over_plane(self):
        p = self.place
        mine = self.buffer.at[:, p.chip, p.core]
        self.copies = [p.links.send(mine, mine, device) for _, device in p.chips]

    def over_cores(self):
        p = self.place
        arrive(self.copies)
        mine = self.buffer.at[:, :, p.core]
        self.copies = [p.links.send(mine, mine, p.sibling)]

    def finish(self):
        arrive(self.copies)


class Place:
    def __init__(self, S, T, links):
        self.S, self.T, self.links = (S, T, links)
        self.s = lax.axis_index("seq")
        self.t = lax.axis_index("tp")
        C = S // 2
        self.core = lax.rem(self.s, 2)
        self.chip = lax.div(self.s, 2)
        self.sibling = (self.chip * 2 + 1 - self.core, self.t)
        self.chips = []
        for k in range(1, C):
            chip = lax.rem(self.chip + k, C)
            self.chips.append((chip, (chip * 2 + self.core, self.t)))


def layer_kernel(S, T, fused, names, *refs):
    r = types.SimpleNamespace(**dict(zip(names, refs)))
    links = Links(r.send_sem, r.recv_sem)
    place = Place(S, T, links)
    lengths = r.lengths
    tokens = r.tokens
    cot = r.cot
    gain = r.gain
    skip = r.skip
    result, grad_tokens, small = (r.result, r.grad_tokens, r.small)
    turn = r.turn
    tokens_in = r.tokens_in
    cot_in = r.cot_in
    centred = r.centred
    inv_std = r.inv_std
    normed = r.normed
    normed_t = r.normed_t
    cot_t = r.cot_t
    proj = r.proj
    keep = r.keep
    keep_next = r.keep_next
    state = r.state
    state_t = r.state_t
    act = r.act
    act_t = r.act_t
    d_gelu = r.d_gelu
    d_act = r.d_act
    summed = r.summed
    d_mixed = r.d_mixed
    adjoint = r.adjoint
    d_proj = r.d_proj
    hidden = r.hidden
    d_value = r.d_value
    d_gate = r.d_gate
    seg_carry, sums = (r.seg_carry, r.sums)
    w_in, w_out = (r.w_in, r.w_out)
    R, D = tokens.shape
    N = w_in.shape[1] // 2
    n = N // T
    L = R // SEGMENTS
    s = place.s
    t = place.t
    first = (s * T + t) * R

    peers_tp = [lax.rem(t + k, T) for k in range(1, T)]
    peers_seq = [lax.rem(s + k, S) for k in range(1, S)]
    barrier = pltpu.get_barrier_semaphore()
    for peer in peers_tp:
        pl.semaphore_signal(barrier, inc=1, device_id=(s, peer), device_id_type=MESH)
    for peer in peers_seq:
        pl.semaphore_signal(barrier, inc=1, device_id=(peer, t), device_id_type=MESH)

    lane = lax.broadcasted_iota(jnp.int32, (D, 128), 1)
    if fused:
        in_slices, out_slices = (r.in_slices, r.out_slices)
        glu_slices, down_slices = (r.glu_slices, r.down_slices)
        local_copies = [
            pltpu.make_async_copy(r.out_proj, out_slices.at[0], r.local_sem.at[0]),
            pltpu.make_async_copy(r.glu_proj.at[0], glu_slices.at[0, 0], r.local_sem.at[1]),
            pltpu.make_async_copy(r.glu_proj.at[1], glu_slices.at[1, 0], r.local_sem.at[2]),
            pltpu.make_async_copy(r.down_proj, down_slices.at[0], r.local_sem.at[3]),
        ]
        for copy in local_copies:
            copy.start()
        row = lax.broadcasted_iota(jnp.int32, (n, 128), 0)
        column = lax.broadcasted_iota(jnp.int32, (n, 128), 1)
        merged = dot(r.in_proj[0], jnp.where(row == column, 1.0, 0.0).astype(BF16)) + dot(
            r.in_proj[1], jnp.where(row + n == column, 1.0, 0.0).astype(BF16)
        )
        in_slices[0] = merged.astype(BF16).reshape(in_slices.shape[1:])
        r.rates_all[t] = r.rates[...]
        for copy in local_copies:
            copy.wait()
        gather_in = Gather(place, in_slices)
        gather_out = Gather(place, out_slices)
        gather_value = Gather(place, glu_slices.at[0])
        gather_gate = Gather(place, glu_slices.at[1])
        gather_down = Gather(place, down_slices)
        pl.semaphore_wait(barrier, T - 1 + S - 1)
        rate_copies = [
            links.send(r.rates_all.at[t], r.rates_all.at[t], (s, peer)) for peer in peers_tp
        ]
        for gather in (gather_in, gather_out, gather_value, gather_gate, gather_down):
            gather.over_tp()

    starts = []
    total = jnp.int32(0)
    for index in range(lengths.shape[0]):
        starts.append(total)
        total = total + lengths[index]

    def keeps(position):
        hit = position == starts[0]
        for start in starts[1:]:
            hit = hit | (position == start)
        return jnp.where(hit, 0.0, 1.0)

    def clear(low, high):
        hit = (starts[0] >= low) & (starts[0] < high)
        for start in starts[1:]:
            hit = hit | ((start >= low) & (start < high))
        return jnp.where(hit, 0.0, 1.0)

    gain_row = gain[...]
    skip_row = skip[...].astype(F32)

    down_index = lax.broadcasted_iota(jnp.int32, (BLOCK, BLOCK), 0)
    across_index = lax.broadcasted_iota(jnp.int32, (BLOCK, BLOCK), 1)
    turned = lax.rem(down_index, SEGMENTS) * SEGMENTS + lax.div(down_index, SEGMENTS)
    turn[...] = jnp.where(turned == across_index, 1.0, 0.0).astype(BF16)

    def pieces(block):
        return [
            pl.ds(pl.multiple_of(run * L + block * SEGMENTS, SEGMENTS), SEGMENTS)
            for run in range(SEGMENTS)
        ]

    def taken(ref, block):
        return dot(turn[...], jnp.concatenate([ref[piece, :] for piece in pieces(block)], 0))

    def block_rows(tile):
        return pl.ds(pl.multiple_of(tile * BLOCK, BLOCK), BLOCK)

    def norm_tile(tile):
        rows = block_rows(tile)
        x = taken(tokens, tile)
        tokens_in[rows, :] = x.astype(BF16)
        mean = jnp.mean(x, 1, keepdims=True)
        inv = lax.rsqrt(jnp.mean(x * x, 1, keepdims=True) - mean * mean + epsilon)
        c = (x - mean) * inv
        centred[rows, :] = c
        inv_std[rows, :] = jnp.broadcast_to(inv, (BLOCK, 128))
        n_rows = (c * gain_row).astype(BF16)
        normed[rows, :] = n_rows
        normed_t[:, rows] = n_rows.T

    def cot_tile(tile):
        rows = block_rows(tile)
        cot_rows = taken(cot, tile).astype(BF16)
        cot_in[rows, :] = cot_rows
        cot_t[:, rows] = cot_rows.T
        index = tile * BLOCK + lax.broadcasted_iota(jnp.int32, (BLOCK, 128), 0)
        position = first + lax.rem(index, SEGMENTS) * L + lax.div(index, SEGMENTS)
        keep[rows, :] = keeps(position)
        keep_next[rows, :] = keeps(position + 1)

    pl.loop(0, R // BLOCK)(norm_tile)
    if fused:
        gather_in.over_plane()
        gather_out.over_plane()
    pl.loop(0, R // BLOCK)(cot_tile)
    if fused:
        gather_in.over_cores()
        gather_out.over_cores()
        arrive(rate_copies)
        gather_value.over_plane()
        gather_in.finish()
        half = lane < 64
        for k in range(T // 2):
            even, odd = (
                in_slices[lax.rem(2 * k + part + T - t, T)].reshape(D, 128).astype(F32)
                for part in range(2)
            )
            at = k * 128
            w_in[:, at : at + 128] = jnp.where(half, even, pltpu.roll(odd, 64, 1)).astype(BF16)
            w_in[:, N + at : N + at + 128] = jnp.where(half, pltpu.roll(even, 64, 1), odd).astype(
                BF16
            )
        rate_rows = [r.rates_all[z] for z in range(T)]
        half8 = lane[:8] < 64

        def joined(rows, part):
            out = []
            for k in range(T // 2):
                even, odd = (rows[2 * k], rows[2 * k + 1])
                if part == 0:
                    out.append(jnp.where(half8, even, pltpu.roll(odd, 64, 1)))
                else:
                    out.append(jnp.where(half8, pltpu.roll(even, 64, 1), odd))
            return jnp.concatenate(out, 1)

        lam_gamma = joined(rate_rows, 0)
        lam_re = lam_gamma[0:1]
        lam_im = joined(rate_rows, 1)[0:1]
        gamma = lam_gamma[1:2]
    else:
        pl.semaphore_wait(barrier, T - 1 + S - 1)
        lam_re = r.rates[0:1, :N]
        lam_im = r.rates[0:1, N:]
        gamma = r.rates[1:2, :N]
    gamma_signed = jnp.concatenate([gamma, -gamma], 1)

    @pl.loop(0, R // BLOCK)
    def _(tile):
        rows = block_rows(tile)
        proj[rows, :] = dot(normed[rows, :], w_in[...]) * gamma_signed

    low8_re = jnp.broadcast_to(lam_re, (8, N))
    low8_im = jnp.broadcast_to(lam_im, (8, N))

    def rows_of(group, step):
        return pl.ds(pl.multiple_of(step * SEGMENTS + group * 8, 8), 8)

    def spread(row):
        return jnp.concatenate([row] * (N // 128), 1)

    def scan_step(values, mask, add, sign):
        new_re, new_im = complex_mul(low8_re, sign * low8_im, *(value * mask for value in values))
        return (new_re + add[:, :N], new_im + add[:, N:])

    zero8 = jnp.zeros((8, N), F32)
    none = tuple((zero8, zero8) for _ in range(GROUPS))

    def forward_step(step, carry):
        return tuple(
            scan_step(
                carry[group],
                spread(keep[rows_of(group, step), :]),
                proj[rows_of(group, step), :],
                -1.0,
            )
            for group in range(GROUPS)
        )

    def segment_rows(finals):
        return [
            (finals[group][0][sub : sub + 1], finals[group][1][sub : sub + 1])
            for group in range(GROUPS)
            for sub in range(8)
        ]

    def fold(start, factor, items, masks, taken):
        before = []
        carry = start
        for (item_re, item_im), mask, take in zip(items, masks, taken):
            before.append(carry)
            moved = complex_mul(*factor, *carry)
            longer = (moved[0] * mask + item_re, moved[1] * mask + item_im)
            if take is None:
                carry = longer
            else:
                carry = tuple(jnp.where(take, new, old) for new, old in zip(longer, carry))
        return carry, before

    zero1 = (jnp.zeros((1, N), F32), jnp.zeros((1, N), F32))
    lam = (lam_re, lam_im)
    conj = (lam_re, -lam_im)

    def unpack(row):
        return (row[:, :N], row[:, N:])

    def packed(row, height):
        parts = [row[:, at : at + 128] for at in range(0, row.shape[1], 128)]
        return jnp.concatenate(parts + [parts[0]] * (height - len(parts)), 0)

    def unpacked(tile, height):
        return jnp.concatenate([tile[k : k + 1, :] for k in range(height)], 1)

    class Exchange:
        def __init__(self, own, factor, tp_buf, seq_buf, forward):
            self.forward = forward
            self.shift = 0 if forward else 1
            self.factor_tp = power(factor, R)
            self.factor_seq = power(self.factor_tp, T)
            self.tp_buf, self.seq_buf = (tp_buf, seq_buf)
            tp_buf[t] = packed(jnp.concatenate(own, 1), 8)
            self.copies = [
                links.send(tp_buf.at[t], tp_buf.at[t], (s, peer)) for peer in peers_tp
            ]

        def order(self, count):
            return list(range(count)) if self.forward else list(range(count))[::-1]

        def before(self, other, mine):
            return other < mine if self.forward else other > mine

        def value(self, tile):
            return unpack(unpacked(tile, 2 * N // 128))

        def over_seq(self):
            arrive(self.copies)
            row = s * T * R + self.shift
            self.items = [self.value(self.tp_buf[z]) for z in self.order(T)]
            self.masks = [clear(row + z * R, row + (z + 1) * R) for z in self.order(T)]
            block, _ = fold(zero1, self.factor_tp, self.items, self.masks, [None] * T)
            self.seq_buf[s] = packed(jnp.concatenate(block, 1), 8)
            self.copies = [
                links.send(self.seq_buf.at[s], self.seq_buf.at[s], (peer, t)) for peer in peers_seq
            ]

        def carry(self):
            arrive(self.copies)
            blocks = self.order(S)
            span = T * R
            carry, _ = fold(
                zero1,
                self.factor_seq,
                [self.value(self.seq_buf[block]) for block in blocks],
                [clear(block * span + self.shift, (block + 1) * span + self.shift) for block in blocks],
                [self.before(block, s) for block in blocks],
            )
            carry, _ = fold(
                carry,
                self.factor_tp,
                self.items,
                self.masks,
                [self.before(z, t) for z in self.order(T)],
            )
            return carry

    finals = segment_rows(lax.fori_loop(0, L, forward_step, none))
    seg_masks = [clear(first + index * L, first + (index + 1) * L) for index in range(SEGMENTS)]
    factor_seg = power(conj, L)
    own, _ = fold(zero1, factor_seg, finals, seg_masks, [None] * SEGMENTS)
    exchange = Exchange(own, conj, r.state_tp, r.state_seq, True)
    if fused:
        gather_gate.over_plane()
    exchange.over_seq()
    if fused:
        gather_down.over_plane()
        gather_out.finish()
        for i in range(T):
            at = lax.rem(t + i, T) * n
            for part in range(2):
                w_out[pl.ds(pl.multiple_of(part * N + at, n), n), :] = out_slices[
                    i, part * (S // 4) : (part + 1) * (S // 4)
                ].reshape(n, D)
    carry = exchange.carry()
    _, entering = fold(carry, factor_seg, finals, seg_masks, [None] * SEGMENTS)
    for index, (row_re, row_im) in enumerate(entering):
        seg_carry[index : index + 1, :] = jnp.concatenate([row_re, row_im], 1)

    def write_state(step, carry):
        new = forward_step(step, carry)
        for group in range(GROUPS):
            state[rows_of(group, step), :] = jnp.concatenate(new[group], 1)
        return new

    def entering_groups():
        return tuple(
            unpack(seg_carry[group * 8 : group * 8 + 8, :]) for group in range(GROUPS)
        )

    lax.fori_loop(0, L, write_state, entering_groups())

    if fused:
        gather_value.over_cores()

    @pl.loop(0, R // BLOCK)
    def _(tile):
        rows = block_rows(tile)
        low = state[rows, :].astype(BF16)
        state_t[:, rows] = low.T
        x = dot(low, w_out[...]) + skip_row * normed[rows, :].astype(F32)
        scale = 0.7978845608028654
        th = jnp.tanh(scale * (x + 0.044715 * x * x * x))
        half = 0.5 * (1.0 + th)
        a = (x * half).astype(BF16)
        act[rows, :] = a
        act_t[:, rows] = a.T
        d_gelu[rows, :] = half + 0.5 * x * (1.0 - th * th) * scale * (1.0 + 0.134145 * x * x)

    if fused:
        gather_gate.over_cores()
        gather_down.over_cores()
        units = [
            Reduce(
                place,
                r.unit_full.at[i],
                r.unit_halves.at[i],
                r.unit_eighths.at[i],
                r.unit_summed.at[i],
            )
            for i in range(T)
        ]

    for i in range(T):
        c = lax.rem(t + i, T)
        if fused:
            if i == 1:
                for gather in (gather_value, gather_gate, gather_down):
                    gather.finish()

            def weight(part):
                return glu_slices[part, i].reshape(D, -1)

            def weight_down():
                return down_slices[i].reshape(-1, D)

        else:

            def weight(part):
                return r.glu[c, part]

            def weight_down():
                return r.down[c]

        @pl.loop(0, R // BLOCK)
        def _(tile):
            rows = block_rows(tile)
            a = act[rows, :]
            value = dot(a, weight(0))
            gate = dot(a, weight(1))
            sigma = 0.5 * jnp.tanh(0.5 * gate) + 0.5
            gated = value * sigma
            h = gated.astype(BF16)
            hidden[rows, :] = h
            d_h = dot_nt(cot_in[rows, :], weight_down())
            d_v = (d_h * sigma).astype(BF16)
            d_g = (d_h * gated * (1.0 - sigma)).astype(BF16)
            d_value[rows, :] = d_v
            d_gate[rows, :] = d_g
            added = dot(h, weight_down())
            d_a = dot_nt(d_v, weight(0)) + dot_nt(d_g, weight(1))
            if i > 0:
                added = added + summed[rows, :]
                d_a = d_a + d_act[rows, :]
            if i < T - 1:
                summed[rows, :] = added
                d_act[rows, :] = d_a
            else:
                out = (tokens_in[rows, :].astype(F32) + added).astype(BF16)
                out = dot(turn[...], out).astype(BF16)
                for run, piece in enumerate(pieces(tile)):
                    result[piece, :] = out[run * SEGMENTS : run * SEGMENTS + SEGMENTS]
                d_m = (d_gelu[rows, :] * d_a).astype(BF16)
                d_mixed[rows, :] = d_m
                adjoint[rows, :] = dot_nt(d_m, w_out[...])

        if fused and i > 0:
            units[i - 1].over_plane()

        GRAD_ROWS = 128
        for k, (left, right) in enumerate(((cot_t, hidden), (act_t, d_value), (act_t, d_gate))):

            @pl.loop(0, D // GRAD_ROWS)
            def _(tile):
                rows = pl.ds(pl.multiple_of(tile * GRAD_ROWS, GRAD_ROWS), GRAD_ROWS)
                g = dot(left[rows, :], right[...]).astype(BF16)
                if fused:
                    full = r.unit_full
                    r.unit_full[i, k, tile] = g.reshape(full.shape[3:])
                elif k == 0:
                    r.grad_down[c, rows, :] = g
                else:
                    r.grad_glu[c, k - 1, rows, :] = g

        if fused:
            units[i].over_cores()
            if i > 0:
                units[i - 1].sum_plane()
                unit_copies = [] if i == 1 else unit_copies
                if i > 1:
                    unit_copies.append(
                        links.send(
                            r.unit_summed.at[i - 1],
                            r.unit_sums.at[i - 2],
                            (s, lax.rem(t + i - 1, T)),
                        )
                    )

    def backward_step(index, carry):
        step = L - 1 - index
        return tuple(
            scan_step(
                carry[group],
                spread(keep_next[rows_of(group, step), :]),
                adjoint[rows_of(group, step), :],
                1.0,
            )
            for group in range(GROUPS)
        )

    finals = segment_rows(lax.fori_loop(0, L, backward_step, none))[::-1]
    seg_masks = [
        clear(first + index * L + 1, first + (index + 1) * L + 1) for index in range(SEGMENTS)
    ][::-1]
    factor_seg = power(lam, L)
    own, _ = fold(zero1, factor_seg, finals, seg_masks, [None] * SEGMENTS)
    exchange = Exchange(own, lam, r.adj_tp, r.adj_seq, False)
    if fused:
        units[T - 1].over_plane()
    exchange.over_seq()

    grad_out = r.grad_out_full if fused else r.grad_out

    @pl.loop(0, 2 * N // 128)
    def _(tile):
        rows = pl.ds(pl.multiple_of(tile * 128, 128), 128)
        grad_out[rows, :] = dot(state_t[rows, :], d_mixed[...]).astype(BF16)

    if fused:
        out_full = r.out_full
        for i in range(T):
            at = lax.rem(t + i, T) * n
            for part in range(2):
                rows = pl.ds(pl.multiple_of(part * N + at, n), n)
                out_full[i, part * (S // 4) : (part + 1) * (S // 4)] = grad_out[rows, :].reshape(
                    S // 4, 2, -1, D
                )
        out_reduce = Reduce(place, out_full, r.out_halves, r.out_eighths, r.out_summed)
        out_reduce.over_cores()

    carry = exchange.carry()
    _, entering = fold(carry, factor_seg, finals, seg_masks, [None] * SEGMENTS)
    entering = entering[::-1]
    groups = tuple(
        tuple(
            jnp.concatenate([entering[group * 8 + sub][part] for sub in range(8)], 0)
            for part in range(2)
        )
        for group in range(GROUPS)
    )
    sums[...] = jnp.zeros_like(sums)

    def adjoint_step(step, carry, previous):
        new = []
        add_re = zero8
        add_im = zero8
        add_gamma = zero8
        for group in range(GROUPS):
            rows = rows_of(group, step)
            b = scan_step(carry[group], spread(keep_next[rows, :]), adjoint[rows, :], 1.0)
            new.append(b)
            adjoint[rows, :] = jnp.concatenate(b, 1)
            u = unpack(proj[rows, :])
            v = previous(group, step)
            mask = spread(keep[rows, :])
            add_re = add_re + mask * (b[0] * v[0] + b[1] * v[1])
            add_im = add_im + mask * (b[0] * v[1] - b[1] * v[0])
            add_gamma = add_gamma + b[0] * u[0] + b[1] * u[1]
        return tuple(new), (add_re, add_im, add_gamma)

    def adjoint_body(index, carry):
        values, totals = carry
        values, added = adjoint_step(
            L - 1 - index, values, lambda group, step: unpack(state[rows_of(group, step - 1), :])
        )
        return values, tuple(total + add for total, add in zip(totals, added))

    values, totals = lax.fori_loop(0, L - 1, adjoint_body, (groups, (zero8, zero8, zero8)))
    inside = entering_groups()
    _, added = adjoint_step(0, values, lambda group, step: inside[group])
    totals = [jnp.sum(total + add, 0, keepdims=True) for total, add in zip(totals, added)]

    if fused:
        out_reduce.over_plane()
        units[T - 1].sum_plane()
        unit_copies.append(
            links.send(
                r.unit_summed.at[T - 1], r.unit_sums.at[T - 2], (s, lax.rem(t + T - 1, T))
            )
        )

    @pl.loop(0, R // BLOCK)
    def _(tile):
        rows = block_rows(tile)
        d_proj[rows, :] = (adjoint[rows, :] * gamma_signed).astype(BF16)

    grad_in = r.grad_in_full if fused else r.grad_in

    @pl.loop(0, D // 128)
    def _(tile):
        rows = pl.ds(pl.multiple_of(tile * 128, 128), 128)
        grad_in[rows, :] = dot(normed_t[rows, :], d_proj[...]).astype(grad_in.dtype)

    if fused:
        in_full = r.in_full
        for k in range(T // 2):
            re = grad_in[:, k * 128 : k * 128 + 128]
            im = grad_in[:, N + k * 128 : N + k * 128 + 128]
            even = jnp.where(half, re, pltpu.roll(im, 64, 1))
            odd = jnp.where(half, pltpu.roll(re, 64, 1), im)
            for part, value in enumerate((even, odd)):
                in_full[lax.rem(2 * k + part + T - t, T)] = value.astype(BF16).reshape(
                    in_full.shape[1:]
                )
        in_reduce = Reduce(place, in_full, r.in_halves, r.in_eighths, r.in_summed)
        in_reduce.over_cores()
        out_reduce.sum_plane()
        out_copies = [
            links.send(r.out_summed.at[i], r.out_sums.at[i - 1], (s, lax.rem(t + i, T)))
            for i in range(1, T)
        ]
        in_reduce.over_plane()

    @pl.loop(0, R // BLOCK)
    def _(tile):
        rows = block_rows(tile)
        d_m = d_mixed[rows, :].astype(F32)
        d_n = dot_nt(d_proj[rows, :], w_in[...]) + d_m * skip_row
        c = centred[rows, :]
        sums[0:8, :] += jnp.sum((d_n * c).reshape(BLOCK // 8, 8, D), 0)
        sums[8:16, :] += jnp.sum((d_m * normed[rows, :].astype(F32)).reshape(BLOCK // 8, 8, D), 0)
        d_c = d_n * gain_row
        mean = jnp.mean(d_c, 1, keepdims=True)
        cross = jnp.mean(d_c * c, 1, keepdims=True)
        inv = inv_std[rows, 0:1]
        out = cot_in[rows, :].astype(F32) + inv * (d_c - mean - c * cross)
        high = out.astype(BF16)
        out = dot(turn[...], high) + dot(turn[...], (out - high.astype(F32)).astype(BF16))
        for run, piece in enumerate(pieces(tile)):
            grad_tokens[piece, :] = out[run * SEGMENTS : run * SEGMENTS + SEGMENTS]

    small_rows = [
        jnp.sum(sums[0:8, :], 0, keepdims=True),
        jnp.sum(sums[8:16, :], 0, keepdims=True),
        jnp.concatenate(totals[:2], 1),
        jnp.concatenate([totals[2] / gamma, jnp.zeros_like(gamma)], 1),
    ]
    if not fused:
        for k, row in enumerate(small_rows):
            small[k : k + 1, :] = row
        small[4:8, :] = jnp.zeros((4, D), F32)
        links.close()
        return

    small_tp, small_seq = (r.small_tp, r.small_seq)
    small_tp[t] = jnp.concatenate([packed(row, D // 128) for row in small_rows], 0)
    small_copies = [links.send(small_tp.at[t], small_tp.at[t], (s, peer)) for peer in peers_tp]

    def total_of(own, buffer):
        total = own.astype(F32)
        for k in range(buffer.shape[0]):
            total = total + buffer[k].astype(F32)
        return total.astype(BF16)

    unit_sum = r.unit_sum
    arrive(unit_copies)
    unit_sum[:, place.chip, place.core] = total_of(r.unit_summed[0], r.unit_sums)
    unit_spread = Spread(place, unit_sum)
    unit_spread.over_plane()

    in_reduce.sum_plane()
    in_copies = [
        links.send(r.in_summed.at[i], r.in_sums.at[i - 1], (s, lax.rem(t + i, T)))
        for i in range(1, T)
    ]
    out_sum, in_sum = (r.out_sum, r.in_sum)
    arrive(out_copies)
    out_sum[0, place.chip, place.core] = total_of(r.out_summed[0], r.out_sums)
    out_spread = Spread(place, out_sum)
    out_spread.over_plane()

    arrive(small_copies)
    part = small_tp[0]
    for z in range(1, T):
        part = part + small_tp[z]
    small_seq[s] = part
    small_copies = [links.send(small_seq.at[s], small_seq.at[s], (peer, t)) for peer in peers_seq]

    unit_spread.over_cores()
    arrive(in_copies)
    in_sum[0, place.chip, place.core] = total_of(r.in_summed[0], r.in_sums)
    in_spread = Spread(place, in_sum)
    in_spread.over_plane()
    out_spread.over_cores()

    unit_spread.finish()
    for k in range(2):
        r.grad_glu[k] = unit_sum[k + 1].reshape(D, -1).astype(F32)
    width = r.grad_down.shape[0]
    row = lax.broadcasted_iota(jnp.int32, (width, width), 0)
    column = lax.broadcasted_iota(jnp.int32, (width, width), 1)
    unit = jnp.where(row == column, 1.0, 0.0).astype(BF16)
    r.grad_down[...] = dot_nt(unit, unit_sum[0].reshape(D, -1))

    arrive(small_copies)
    part = small_seq[0]
    for block in range(1, S):
        part = part + small_seq[block]
    for k in range(4):
        height = D // 128
        small[k : k + 1, :] = unpacked(part[k * height : (k + 1) * height], height)
    small[4:8, :] = jnp.zeros((4, D), F32)

    out_spread.finish()
    r.grad_out[...] = out_sum[0].reshape(2, n, D).astype(F32)
    in_spread.over_cores()
    in_spread.finish()
    value = in_sum[0].reshape(D, 128).astype(F32)
    r.grad_in[0] = value[:, :n]
    r.grad_in[1] = pltpu.roll(value, 64, 1)[:, :n]
    links.close()


def decay_terms(decay_log, angle):
    rate_step = jnp.exp(decay_log)
    radius = jnp.exp(-rate_step)
    return (
        radius * jnp.cos(angle),
        radius * jnp.sin(angle),
        jnp.sqrt(-jnp.expm1(-2.0 * rate_step)),
    )


def local(
    S,
    T,
    tokens,
    ln_gain,
    in_proj,
    decay_log,
    angle,
    out_proj,
    skip,
    glu_proj,
    down_proj,
    lengths,
    cotangent,
):
    R, D = tokens.shape
    n = in_proj.shape[2]
    N = n * T
    units = down_proj.shape[0]
    C = S // 2
    fused = (
        S % 4 == 0
        and T % 2 == 0
        and 2 * n == 128
        and units % 128 == 0
        and all(size % (16 * S) == 0 for size in (D, 2 * n, units))
        and (2 * C) * 64 == D
    )
    vmem = pl.BlockSpec(memory_space=pltpu.VMEM)
    anywhere = pl.BlockSpec(memory_space=pl.ANY)
    lam_re, lam_im, gamma = decay_terms(decay_log, angle)
    ins = dict(
        lengths=(lengths, pl.BlockSpec(memory_space=pltpu.SMEM)),
        tokens=(tokens, vmem),
        cot=(cotangent, vmem),
        gain=(ln_gain.reshape(1, D), vmem),
        skip=(skip.reshape(1, D), vmem),
    )
    outs = dict(
        result=((R, D), BF16),
        grad_tokens=((R, D), F32),
        small=((8, D), F32),
    )
    scratch = dict(
        turn=((BLOCK, BLOCK), BF16),
        tokens_in=((R, D), BF16),
        cot_in=((R, D), BF16),
        centred=((R, D), F32),
        inv_std=((R, 128), F32),
        normed=((R, D), BF16),
        normed_t=((D, R), BF16),
        cot_t=((D, R), BF16),
        proj=((R, 2 * N), F32),
        keep=((R, 128), F32),
        keep_next=((R, 128), F32),
        state=((R, 2 * N), F32),
        state_t=((2 * N, R), BF16),
        act=((R, D), BF16),
        act_t=((D, R), BF16),
        d_gelu=((R, D), F32),
        d_act=((R, D), F32),
        summed=((R, D), F32),
        d_mixed=((R, D), BF16),
        adjoint=((R, 2 * N), F32),
        d_proj=((R, 2 * N), BF16),
        hidden=((R, units), BF16),
        d_value=((R, units), BF16),
        d_gate=((R, units), BF16),
        seg_carry=((SEGMENTS, 2 * N), F32),
        sums=((16, D), F32),
        state_tp=((T, 8, 128), F32),
        state_seq=((S, 8, 128), F32),
        adj_tp=((T, 8, 128), F32),
        adj_seq=((S, 8, 128), F32),
    )
    if fused:
        rates = jnp.stack(
            [jnp.concatenate([lam_re, lam_im]), jnp.concatenate([gamma, gamma])]
            + [jnp.zeros((2 * n,), F32)] * 6
        )
        ins.update(
            rates=(rates, vmem),
            in_proj=(in_proj, vmem),
            out_proj=(out_proj.reshape(C, 2, 2 * n // S, D), anywhere),
            glu_proj=(glu_proj.reshape(2, C, 2, D // S, units), anywhere),
            down_proj=(down_proj.reshape(C, 2, units // S, D), anywhere),
        )
        outs.update(
            grad_in=((2, D, n), F32),
            grad_out=((2, n, D), F32),
            grad_glu=((2, D, units), F32),
            grad_down=((units, D), F32),
        )

        def whole(parts, rows, lanes, lead=()):
            return (lead + (parts, C, 2, rows, lanes), BF16)

        def halves(parts, rows, lanes, lead=()):
            return (lead + (parts, C, rows, lanes), BF16)

        def eighths(parts, rows, lanes, lead=()):
            return (lead + (C - 1, parts, rows, lanes), BF16)

        def own(parts, rows, lanes, lead=()):
            return (lead + (parts, rows, lanes), BF16)

        unit_sizes = (3, D // S, units, (T,))
        out_sizes = (T, 2 * n // S, D)
        in_sizes = (T, D // S, 2 * n)
        scratch.update(
            w_in=((D, 2 * N), BF16),
            w_out=((2 * N, D), BF16),
            rates_all=((T, 8, 128), F32),
            in_slices=((T, C, 2, D // S, 2 * n), BF16),
            out_slices=((T, C, 2, 2 * n // S, D), BF16),
            glu_slices=((2, T, C, 2, D // S, units), BF16),
            down_slices=((T, C, 2, units // S, D), BF16),
            grad_out_full=((2 * N, D), BF16),
            grad_in_full=((D, 2 * N), F32),
            small_tp=((T, 16, 128), F32),
            small_seq=((S, 16, 128), F32),
            unit_sums=((T - 1, 3, D // S, units), BF16),
            out_sums=((T - 1, 2 * n // S, D), BF16),
            in_sums=((T - 1, D // S, 2 * n), BF16),
            unit_sum=((3, C, 2, D // S, units), BF16),
            out_sum=((1, C, 2, 2 * n // S, D), BF16),
            in_sum=((1, C, 2, D // S, 2 * n), BF16),
        )
        scratch.update(
            unit_full=whole(*unit_sizes),
            unit_halves=halves(*unit_sizes),
            unit_eighths=eighths(*unit_sizes),
            unit_summed=own(*unit_sizes),
            out_full=whole(*out_sizes),
            out_halves=halves(*out_sizes),
            out_eighths=eighths(*out_sizes),
            out_summed=own(*out_sizes),
            in_full=whole(*in_sizes),
            in_halves=halves(*in_sizes),
            in_eighths=eighths(*in_sizes),
            in_summed=own(*in_sizes),
        )
        links = 160
    else:
        w_in = lax.all_gather(in_proj, "tp", axis=2, tiled=True)
        w_out = lax.all_gather(out_proj, "tp", axis=1, tiled=True).reshape(2 * N, D)
        lam_re, lam_im, gamma = (
            lax.all_gather(part, "tp", tiled=True) for part in (lam_re, lam_im, gamma)
        )
        rates = jnp.stack(
            [jnp.concatenate([lam_re, lam_im]), jnp.concatenate([gamma, gamma])]
            + [jnp.zeros((2 * N,), F32)] * 6
        )
        ins.update(
            rates=(rates, vmem),
            w_in=(jnp.concatenate([w_in[0], w_in[1]], 1), vmem),
            w_out=(w_out, vmem),
            glu=(lax.all_gather(glu_proj, "tp"), vmem),
            down=(lax.all_gather(down_proj, "tp"), vmem),
        )
        outs.update(
            grad_in=((D, 2 * N), BF16),
            grad_out=((2 * N, D), BF16),
            grad_glu=((T, 2, D, units), BF16),
            grad_down=((T, D, units), BF16),
        )
        links = 2 * (T - 1 + S - 1)
    names = [*ins, *outs, *scratch, *dict(local_sem=0, send_sem=0, recv_sem=0)]
    result, grad_tokens, small, grad_in, grad_out, grad_glu, grad_down = pl.pallas_call(
        functools.partial(layer_kernel, S, T, fused, names),
        out_shape=tuple(jax.ShapeDtypeStruct(shape, dtype) for shape, dtype in outs.values()),
        in_specs=[spec for _, spec in ins.values()],
        out_specs=(vmem,) * len(outs),
        scratch_shapes=[pltpu.VMEM(shape, dtype) for shape, dtype in scratch.values()]
        + [
            pltpu.SemaphoreType.DMA((4,)),
            pltpu.SemaphoreType.DMA((links,)),
            pltpu.SemaphoreType.DMA((links,)),
        ],
        compiler_params=pltpu.CompilerParams(
            collective_id=0, has_side_effects=True, vmem_limit_bytes=60 * 2**20
        ),
    )(*[value for value, _ in ins.values()])
    t = lax.axis_index("tp")
    if not fused:
        small = lax.psum(small, ("seq", "tp"))

        def reduced(part):
            part = lax.psum_scatter(part, "tp", scatter_dimension=0, tiled=True)
            return lax.psum(part, "seq").astype(F32)

        grad_in = grad_in.reshape(D, 2, T, n).transpose(2, 1, 0, 3).reshape(T * 2, D, n)
        grad_in = reduced(grad_in)
        grad_out = grad_out.reshape(2, T, n, D).transpose(1, 0, 2, 3).reshape(T * 2, n, D)
        grad_out = reduced(grad_out)
        grad_glu = reduced(grad_glu.reshape(T * 2, D, units))
        grad_down = reduced(grad_down)[0].T

    def mine(row):
        return lax.dynamic_slice_in_dim(row, t * n, n)

    g_re, g_im, g_gamma = (mine(small[2, :N]), mine(small[2, N:]), mine(small[3, :N]))
    _, pull = jax.vjp(decay_terms, decay_log, angle)
    grad_decay, grad_angle = pull((g_re, g_im, g_gamma))
    return (
        result,
        grad_tokens,
        small[0],
        grad_in,
        grad_decay,
        grad_angle,
        grad_out,
        small[1],
        grad_glu,
        grad_down,
    )


def solution(mesh):
    in_specs = (
        P(("seq", "tp"), None),
        P(),
        P(None, None, "tp"),
        P("tp"),
        P("tp"),
        P(None, "tp", None),
        P(),
        P(None, None, "tp"),
        P("tp", None),
        P(),
        P(("seq", "tp"), None),
    )
    out_specs = (
        P(("seq", "tp"), None),
        P(("seq", "tp"), None),
        P(),
        P(None, None, "tp"),
        P("tp"),
        P("tp"),
        P(None, "tp", None),
        P(),
        P(None, None, "tp"),
        P("tp", None),
    )
    return jax.shard_map(
        functools.partial(local, mesh.shape["seq"], mesh.shape["tp"]),
        mesh=mesh,
        in_specs=in_specs,
        out_specs=out_specs,
        check_vma=False,
    )
```

```python
import functools
import types
import jax
import jax.numpy as jnp
from jax import lax
from jax.experimental import pallas as pl
from jax.experimental.pallas import tpu as pltpu
from jax.sharding import PartitionSpec as P

epsilon = 1e-05
MESH = pl.DeviceIdType.MESH
F32 = jnp.float32
BF16 = jnp.bfloat16
GROUPS = 2
SEGMENTS = 8 * GROUPS
BLOCK = SEGMENTS * SEGMENTS


def dot(left, right):
    return jnp.dot(left, right, preferred_element_type=F32)


def dot_nt(left, right):
    return lax.dot_general(left, right, (((1,), (1,)), ((), ())), preferred_element_type=F32)


def complex_mul(left_re, left_im, right_re, right_im):
    return (left_re * right_re - left_im * right_im, left_re * right_im + left_im * right_re)


def dot_tn(left, right):
    return lax.dot_general(left, right, (((0,), (0,)), ((), ())), preferred_element_type=F32)


def power(base, exponent):
    result = None
    square = base
    while exponent:
        if exponent & 1:
            result = square if result is None else complex_mul(*result, *square)
        exponent >>= 1
        if exponent:
            square = complex_mul(*square, *square)
    return result


class Links:
    def __init__(self, send_sem, recv_sem):
        self.send_sem = send_sem
        self.recv_sem = recv_sem
        self.started = []

    def send(self, source, target, device):
        index = len(self.started)
        copy = pltpu.make_async_remote_copy(
            src_ref=source,
            dst_ref=target,
            send_sem=self.send_sem.at[index],
            recv_sem=self.recv_sem.at[index],
            device_id=device,
            device_id_type=MESH,
        )
        copy.start()
        self.started.append(copy)
        return copy

    def close(self):
        for copy in self.started:
            copy.wait_send()


def arrive(copies):
    for copy in copies:
        copy.wait_recv()


class Gather:
    def __init__(self, place, buffer, first, last):
        self.place = place
        self.buffer = buffer
        self.slots = range(first, last)
        self.part = buffer.at[pl.ds(first, last - first)]

    def over_tp(self):
        p = self.place
        self.copies = [
            p.links.send(
                self.buffer.at[0, p.chip, p.core],
                self.buffer.at[slot, p.chip, p.core],
                (p.s, lax.rem(p.t + p.T - slot, p.T)),
            )
            for slot in self.slots
        ]

    def over_plane(self):
        p = self.place
        arrive(self.copies)
        mine = self.part.at[:, p.chip, p.core]
        self.copies = [p.links.send(mine, mine, device) for _, device in p.chips]

    def over_cores(self):
        p = self.place
        arrive(self.copies)
        mine = self.part.at[:, :, p.core]
        self.copies = [p.links.send(mine, mine, p.sibling)]

    def finish(self):
        arrive(self.copies)


class Reduce:
    def __init__(self, place, full, halves, eighths, summed):
        self.place = place
        self.full = full
        self.halves = halves
        self.eighths = eighths
        self.summed = summed

    def over_cores(self):
        p = self.place
        self.copies = [
            p.links.send(self.full.at[:, :, 1 - p.core], self.halves, p.sibling)
        ]

    def over_plane(self):
        p = self.place
        arrive(self.copies)
        parts, chips = self.halves.shape[:2]

        @pl.loop(0, parts * chips)
        def _(index):
            part, chip = (lax.div(index, chips), lax.rem(index, chips))
            self.halves[part, chip] = (
                self.full[part, chip, p.core].astype(F32) + self.halves[part, chip].astype(F32)
            ).astype(BF16)

        self.copies = [
            p.links.send(self.halves.at[:, chip], self.eighths.at[k], device)
            for k, (chip, device) in enumerate(p.chips)
        ]

    def sum_plane(self):
        p = self.place
        arrive(self.copies)

        @pl.loop(0, self.halves.shape[0])
        def _(part):
            total = self.halves[part, p.chip].astype(F32)
            for k in range(len(p.chips)):
                total = total + self.eighths[k, part].astype(F32)
            self.summed[part] = total.astype(BF16)


class Reduce2(Reduce):
    def __init__(self, place, full, halves, eighths, summed):
        super().__init__(place, full, halves, eighths, summed)
        self.rows = halves.shape[2] // 2
        self.ours = halves.at[:, :, pl.ds(0, self.rows)]
        self.theirs = halves.at[:, :, pl.ds(self.rows, self.rows)]

    def sum_cores(self, chip):
        self.halves[0, chip] = (
            self.full[0, chip, self.place.core].astype(F32) + self.halves[0, chip].astype(F32)
        ).astype(BF16)

    def over_plane(self):
        p = self.place
        arrive(self.copies)
        self.sum_cores(p.by_x)
        self.sum_cores(p.by_y)
        self.sum_cores(p.by_xy)
        self.copies = [
            p.links.send(part.at[0, chip], self.eighths.at[index, 0, rows], device)
            for index, part, chip, rows, device in (
                (0, self.ours, p.by_x, pl.ds(0, self.rows), p.x_device),
                (1, self.ours, p.by_xy, pl.ds(0, self.rows), p.x_device),
                (0, self.theirs, p.by_y, pl.ds(self.rows, self.rows), p.y_device),
                (1, self.theirs, p.by_xy, pl.ds(self.rows, self.rows), p.y_device),
            )
        ]
        self.sum_cores(p.chip)

    def turn_plane(self):
        p = self.place
        arrive(self.copies)
        n = self.rows
        for index, chip in ((0, p.chip), (1, p.by_y)):
            self.halves[0, chip, 0:n] = (
                self.halves[0, chip, 0:n].astype(F32) + self.eighths[index, 0, 0:n].astype(F32)
            ).astype(BF16)
        for index, chip in ((0, p.chip), (1, p.by_x)):
            self.halves[0, chip, n:] = (
                self.halves[0, chip, n:].astype(F32) + self.eighths[index, 0, n:].astype(F32)
            ).astype(BF16)
        self.copies = [
            p.links.send(self.ours.at[0, p.by_y], self.eighths.at[2, 0, pl.ds(0, n)], p.y_device),
            p.links.send(self.theirs.at[0, p.by_x], self.eighths.at[2, 0, pl.ds(n, n)], p.x_device),
        ]

    def sum_plane(self):
        p = self.place
        arrive(self.copies)
        self.summed[0] = (
            self.halves[0, p.chip].astype(F32) + self.eighths[2, 0].astype(F32)
        ).astype(BF16)


class Spread:
    def __init__(self, place, buffer):
        self.place = place
        self.buffer = buffer

    def over_plane(self):
        p = self.place
        mine = self.buffer.at[:, p.chip, p.core]
        self.copies = [p.links.send(mine, mine, device) for _, device in p.chips]

    def over_cores(self):
        p = self.place
        arrive(self.copies)
        mine = self.buffer.at[:, :, p.core]
        self.copies = [p.links.send(mine, mine, p.sibling)]

    def finish(self):
        arrive(self.copies)


class Place:
    def __init__(self, S, T, links):
        self.S, self.T, self.links = (S, T, links)
        self.s = lax.axis_index("seq")
        self.t = lax.axis_index("tp")
        C = S // 2
        self.core = lax.rem(self.s, 2)
        self.chip = lax.div(self.s, 2)
        self.sibling = (self.chip * 2 + 1 - self.core, self.t)
        x = lax.rem(self.chip, 2)
        y = lax.div(self.chip, 2)
        self.by_x = y * 2 + 1 - x
        self.by_y = (1 - y) * 2 + x
        self.by_xy = (1 - y) * 2 + 1 - x
        self.x_device = (self.by_x * 2 + self.core, self.t)
        self.y_device = (self.by_y * 2 + self.core, self.t)
        self.chips = []
        for k in range(1, C):
            chip = lax.rem(self.chip + k, C)
            self.chips.append((chip, (chip * 2 + self.core, self.t)))


def layer_kernel(S, T, fused, names, *refs):
    r = types.SimpleNamespace(**dict(zip(names, refs)))
    links = Links(r.send_sem, r.recv_sem)
    place = Place(S, T, links)
    lengths = r.lengths
    tokens = r.tokens_raw
    cot = r.cot_raw
    result = r.result_rows
    grad_tokens = r.grad_rows
    turn = r.turn
    tokens_in = r.tokens_in
    cot_in = r.cot_in
    centred = r.centred
    inv_std = r.inv_std
    normed = r.normed
    proj = r.proj
    keep = r.keep
    keep_next = r.keep_next
    state = r.state
    state_low = r.state_low
    act = r.act
    d_gelu = r.d_gelu
    d_act = r.d_act
    summed = r.summed
    d_mixed = r.d_mixed
    adjoint = r.adjoint
    d_proj = r.d_proj
    hidden = r.hidden
    d_unit = r.d_unit
    seg_carry, sums = (r.seg_carry, r.sums)
    w_in, w_out = (r.w_in, r.w_out)
    R, D = tokens.shape
    N = w_in.shape[0] // 2
    n = N // T
    L = R // SEGMENTS
    s = place.s
    t = place.t
    first = (s * T + t) * R

    peers_tp = [lax.rem(t + k, T) for k in range(1, T)]
    peers_seq = [lax.rem(s + k, S) for k in range(1, S)]
    barrier = pltpu.get_barrier_semaphore()
    for peer in peers_tp:
        pl.semaphore_signal(barrier, inc=1, device_id=(s, peer), device_id_type=MESH)
    for peer in peers_seq:
        pl.semaphore_signal(barrier, inc=1, device_id=(peer, t), device_id_type=MESH)

    fetched = [
        pltpu.make_async_copy(source, target, r.local_sem.at[index])
        for index, (source, target) in enumerate(((r.tokens, tokens), (r.cot, cot)))
    ]
    if fused:
        in_slices, out_slices, unit_slices = (r.in_slices, r.out_slices, r.unit_slices)
        units = r.down_proj.shape[2] * S
        D_rows = r.glu_proj.shape[3]
        gated_rows = unit_slices.at[0, :, :, pl.ds(0, D_rows)]
        weights = [
            pltpu.make_async_copy(source, target, r.local_sem.at[2 + index])
            for index, (source, target) in enumerate(
                (
                    (r.in_proj, in_slices.at[0]),
                    (r.out_proj, out_slices.at[0]),
                    (r.glu_proj.at[0], gated_rows.at[:, :, :, pl.ds(0, units)]),
                    (r.glu_proj.at[1], gated_rows.at[:, :, :, pl.ds(units, units)]),
                    (r.down_proj, unit_slices.at[0, :, :, pl.ds(D_rows, units // S)]),
                )
            )
        ]
        for copy in weights:
            copy.start()
    for copy in fetched:
        copy.start()
    if fused:
        rates_all = r.rates_all
        rates_all[t] = jnp.zeros(rates_all.shape[1:], F32)
        for index, row in enumerate(decay_terms(r.decay_log[...], r.angle[...])):
            rates_all[t, index : index + 1, 0:n] = row
        gather_in = Gather(place, in_slices, 1, T)
        gather_out = Gather(place, out_slices, 1, T)
        gather_units = [Gather(place, unit_slices, slot, slot + 1) for slot in range(1, T)]
        for copy in weights:
            copy.wait()
        pl.semaphore_wait(barrier, T - 1 + S - 1)
        gather_in.over_tp()
        rate_copies = [
            links.send(rates_all.at[t], rates_all.at[t], (s, peer)) for peer in peers_tp
        ]
        gather_out.over_tp()
        for gather in gather_units:
            gather.over_tp()

    starts = []
    total = jnp.int32(0)
    for index in range(lengths.shape[0]):
        starts.append(total)
        total = total + lengths[index]

    def keeps(position):
        hit = position == starts[0]
        for start in starts[1:]:
            hit = hit | (position == start)
        return jnp.where(hit, 0.0, 1.0)

    def clear(low, high):
        hit = (starts[0] >= low) & (starts[0] < high)
        for start in starts[1:]:
            hit = hit | ((start >= low) & (start < high))
        return jnp.where(hit, 0.0, 1.0)

    gain_row = r.gain[...]
    skip_row = r.skip[...].astype(F32)

    down_index = lax.broadcasted_iota(jnp.int32, (BLOCK, BLOCK), 0)
    across_index = lax.broadcasted_iota(jnp.int32, (BLOCK, BLOCK), 1)
    turned = lax.rem(down_index, SEGMENTS) * SEGMENTS + lax.div(down_index, SEGMENTS)
    turn[...] = jnp.where(turned == across_index, 1.0, 0.0).astype(BF16)

    def pieces(block):
        return [
            pl.ds(pl.multiple_of(run * L + block * SEGMENTS, SEGMENTS), SEGMENTS)
            for run in range(SEGMENTS)
        ]

    def taken(ref, block):
        return dot(turn[...], jnp.concatenate([ref[piece, :] for piece in pieces(block)], 0))

    def block_rows(tile):
        return pl.ds(pl.multiple_of(tile * BLOCK, BLOCK), BLOCK)

    def norm_tile(tile):
        rows = block_rows(tile)
        x = taken(tokens, tile)
        tokens_in[rows, :] = x.astype(BF16)
        mean = jnp.mean(x, 1, keepdims=True)
        inv = lax.rsqrt(jnp.mean(x * x, 1, keepdims=True) - mean * mean + epsilon)
        c = (x - mean) * inv
        centred[rows, :] = c
        inv_std[rows, :] = jnp.broadcast_to(inv, (BLOCK, 128))
        n_rows = (c * gain_row).astype(BF16)
        normed[rows, :] = n_rows

    def cot_tile(tile):
        rows = block_rows(tile)
        cot_rows = taken(cot, tile).astype(BF16)
        cot_in[rows, :] = cot_rows
        index = tile * BLOCK + lax.broadcasted_iota(jnp.int32, (BLOCK, 128), 0)
        position = first + lax.rem(index, SEGMENTS) * L + lax.div(index, SEGMENTS)
        keep[rows, :] = keeps(position)
        keep_next[rows, :] = keeps(position + 1)

    fetched[0].wait()
    pl.loop(0, R // BLOCK)(norm_tile)
    if fused:
        gather_in.over_plane()
        gather_out.over_plane()
    fetched[1].wait()
    pl.loop(0, R // BLOCK)(cot_tile)

    def assemble(slices, weight):
        for i in range(T):
            at = lax.rem(t + i, T) * n
            for part in range(2):
                weight[pl.ds(pl.multiple_of(part * N + at, n), n), :] = slices[
                    i, part * (S // 4) : (part + 1) * (S // 4)
                ].reshape(n, D)

    if fused:
        gather_in.over_cores()
        arrive(rate_copies)
        half = lax.broadcasted_iota(jnp.int32, (8, 128), 1) < n
        rate_rows = [rates_all[z] for z in range(T)]
        joined = jnp.concatenate(
            [
                jnp.where(half, rate_rows[z], pltpu.roll(rate_rows[z + 1], n, 1))
                for z in range(0, T, 2)
            ],
            1,
        )
        lam_re, lam_im, gamma = (joined[k : k + 1] for k in range(3))
        gather_in.finish()
        assemble(in_slices, w_in)
    else:
        pl.semaphore_wait(barrier, T - 1 + S - 1)
        lam_re, lam_im, gamma = (r.rates[k : k + 1, :] for k in range(3))
    gamma_signed = jnp.concatenate([gamma, -gamma], 1)

    @pl.loop(0, R // BLOCK)
    def _(tile):
        rows = block_rows(tile)
        proj[rows, :] = dot_nt(normed[rows, :], w_in[...]) * gamma_signed

    low8_re = jnp.broadcast_to(lam_re, (8, N))
    low8_im = jnp.broadcast_to(lam_im, (8, N))

    def rows_of(group, step):
        return pl.ds(pl.multiple_of(step * SEGMENTS + group * 8, 8), 8)

    def spread(row):
        return jnp.concatenate([row] * (N // 128), 1)

    def scan_step(values, mask, add, sign):
        new_re, new_im = complex_mul(low8_re, sign * low8_im, *(value * mask for value in values))
        return (new_re + add[:, :N], new_im + add[:, N:])

    zero8 = jnp.zeros((8, N), F32)
    none = tuple((zero8, zero8) for _ in range(GROUPS))

    def forward_step(step, carry):
        return tuple(
            scan_step(
                carry[group],
                spread(keep[rows_of(group, step), :]),
                proj[rows_of(group, step), :],
                -1.0,
            )
            for group in range(GROUPS)
        )

    def segment_rows(finals):
        return [
            (finals[group][0][sub : sub + 1], finals[group][1][sub : sub + 1])
            for group in range(GROUPS)
            for sub in range(8)
        ]

    def fold(start, factor, items, masks, taken):
        before = []
        carry = start
        for (item_re, item_im), mask, take in zip(items, masks, taken):
            before.append(carry)
            moved = complex_mul(*factor, *carry)
            longer = (moved[0] * mask + item_re, moved[1] * mask + item_im)
            if take is None:
                carry = longer
            else:
                carry = tuple(jnp.where(take, new, old) for new, old in zip(longer, carry))
        return carry, before

    zero1 = (jnp.zeros((1, N), F32), jnp.zeros((1, N), F32))
    lam = (lam_re, lam_im)
    conj = (lam_re, -lam_im)

    def unpack(row):
        return (row[:, :N], row[:, N:])

    def packed(row, height):
        parts = [row[:, at : at + 128] for at in range(0, row.shape[1], 128)]
        return jnp.concatenate(parts + [parts[0]] * (height - len(parts)), 0)

    def unpacked(tile, height):
        return jnp.concatenate([tile[k : k + 1, :] for k in range(height)], 1)

    class Exchange:
        def __init__(self, own, factor, tp_buf, seq_buf, forward):
            self.forward = forward
            self.shift = 0 if forward else 1
            self.factor_tp = power(factor, R)
            self.factor_seq = power(self.factor_tp, T)
            self.tp_buf, self.seq_buf = (tp_buf, seq_buf)
            tp_buf[t] = packed(jnp.concatenate(own, 1), 8)
            self.copies = [
                links.send(tp_buf.at[t], tp_buf.at[t], (s, peer)) for peer in peers_tp
            ]

        def order(self, count):
            return list(range(count)) if self.forward else list(range(count))[::-1]

        def before(self, other, mine):
            return other < mine if self.forward else other > mine

        def value(self, tile):
            return unpack(unpacked(tile, 2 * N // 128))

        def over_seq(self):
            arrive(self.copies)
            row = s * T * R + self.shift
            self.items = [self.value(self.tp_buf[z]) for z in self.order(T)]
            self.masks = [clear(row + z * R, row + (z + 1) * R) for z in self.order(T)]
            block, _ = fold(zero1, self.factor_tp, self.items, self.masks, [None] * T)
            self.seq_buf[s] = packed(jnp.concatenate(block, 1), 8)
            self.copies = [
                links.send(self.seq_buf.at[s], self.seq_buf.at[s], (peer, t)) for peer in peers_seq
            ]

        def carry(self):
            arrive(self.copies)
            blocks = self.order(S)
            span = T * R
            carry, _ = fold(
                zero1,
                self.factor_seq,
                [self.value(self.seq_buf[block]) for block in blocks],
                [clear(block * span + self.shift, (block + 1) * span + self.shift) for block in blocks],
                [self.before(block, s) for block in blocks],
            )
            carry, _ = fold(
                carry,
                self.factor_tp,
                self.items,
                self.masks,
                [self.before(z, t) for z in self.order(T)],
            )
            return carry

    finals = segment_rows(lax.fori_loop(0, L, forward_step, none))
    seg_masks = [clear(first + index * L, first + (index + 1) * L) for index in range(SEGMENTS)]
    factor_seg = power(conj, L)
    own, _ = fold(zero1, factor_seg, finals, seg_masks, [None] * SEGMENTS)
    exchange = Exchange(own, conj, r.state_tp, r.state_seq, True)
    if fused:
        gather_out.over_cores()
        gather_units[0].over_plane()
    exchange.over_seq()
    if fused:
        for gather in gather_units[1:]:
            gather.over_plane()
        gather_out.finish()
        assemble(out_slices, w_out)
    carry = exchange.carry()
    _, entering = fold(carry, factor_seg, finals, seg_masks, [None] * SEGMENTS)
    for index, (row_re, row_im) in enumerate(entering):
        seg_carry[index : index + 1, :] = jnp.concatenate([row_re, row_im], 1)

    def write_state(step, carry):
        new = forward_step(step, carry)
        for group in range(GROUPS):
            state[rows_of(group, step), :] = jnp.concatenate(new[group], 1)
        return new

    def entering_groups():
        return tuple(
            unpack(seg_carry[group * 8 : group * 8 + 8, :]) for group in range(GROUPS)
        )

    lax.fori_loop(0, L, write_state, entering_groups())

    @pl.loop(0, R // BLOCK)
    def _(tile):
        rows = block_rows(tile)
        low = state[rows, :].astype(BF16)
        state_low[rows, :] = low
        x = dot(low, w_out[...]) + skip_row * normed[rows, :].astype(F32)
        scale = 0.7978845608028654
        th = jnp.tanh(scale * (x + 0.044715 * x * x * x))
        half = 0.5 * (1.0 + th)
        a = (x * half).astype(BF16)
        act[rows, :] = a
        d_gelu[rows, :] = half + 0.5 * x * (1.0 - th * th) * scale * (1.0 + 0.134145 * x * x)

    if fused:
        reduces = [
            Reduce2(
                place,
                r.unit_full.at[i],
                r.unit_halves.at[i],
                r.unit_eighths.at[i],
                r.unit_summed.at[i],
            )
            for i in range(T)
        ]

    UNIT_ROWS = min(512, R)
    units = hidden.shape[1]
    unit_copies = []

    def unit_grads(i):
        c = lax.rem(t + i, T)
        gated_grad = dot_tn(act[...], d_unit[...]).astype(BF16)
        down_grad = dot_tn(hidden[...], cot_in[...]).astype(BF16)
        if fused:
            full = r.unit_full
            full[i, 0, :, :, 0:D_rows] = gated_grad.reshape(S // 2, 2, D_rows, 2 * units)
            full[i, 0, :, :, D_rows:] = down_grad.reshape(S // 2, 2, units // S, D)
            reduces[i].over_cores()
        else:
            r.grad_glu[c] = gated_grad
            r.grad_down[c] = down_grad

    def unit_sums(i):
        reduces[i].sum_plane()
        if i > 0:
            unit_copies.append(
                links.send(r.unit_summed.at[i], r.unit_sums.at[i - 1], (s, lax.rem(t + i, T)))
            )

    for i in range(T):
        c = lax.rem(t + i, T)
        if fused:
            if i > 0:
                gather_units[i - 1].finish()
            if i < T - 1:
                gather_units[i].over_cores()
            w_gated = unit_slices[i, :, :, 0:D_rows].reshape(D, 2 * units)
            w_down = unit_slices[i, :, :, D_rows:].reshape(units, D)
        else:
            w_gated = r.glu[c]
            w_down = r.down[c]

        for tile in range(R // UNIT_ROWS):
            rows = slice(tile * UNIT_ROWS, (tile + 1) * UNIT_ROWS)
            both = dot(act[rows, :], w_gated)
            value, gate = (both[:, :units], both[:, units:])
            sigma = 0.5 * jnp.tanh(0.5 * gate) + 0.5
            gated = value * sigma
            h = gated.astype(BF16)
            hidden[rows, :] = h
            d_h = dot_nt(cot_in[rows, :], w_down)
            d_both = jnp.concatenate(
                [(d_h * sigma).astype(BF16), (d_h * gated * (1.0 - sigma)).astype(BF16)], 1
            )
            d_unit[rows, :] = d_both
            added = dot(h, w_down)
            d_a = dot_nt(d_both, w_gated)
            if i > 0:
                added = added + summed[rows, :]
                d_a = d_a + d_act[rows, :]
            if i < T - 1:
                summed[rows, :] = added
                d_act[rows, :] = d_a
            else:
                d_m = (d_gelu[rows, :] * d_a).astype(BF16)
                d_mixed[rows, :] = d_m
                adjoint[rows, :] = dot_nt(d_m, w_out[...])
                out = (tokens_in[rows, :].astype(F32) + added).astype(BF16)
                for block in range(UNIT_ROWS // BLOCK):
                    turned = dot(turn[...], out[block * BLOCK : block * BLOCK + BLOCK])
                    turned = turned.astype(BF16)
                    for run, piece in enumerate(pieces(tile * (UNIT_ROWS // BLOCK) + block)):
                        result[piece, :] = turned[run * SEGMENTS : run * SEGMENTS + SEGMENTS]

        if fused and i > 0:
            reduces[i - 1].over_plane()
        if i < T - 1:
            unit_grads(i)
        if fused and i > 1:
            reduces[i - 2].turn_plane()
        if fused and i > 2:
            unit_sums(i - 3)

    result_copy = pltpu.make_async_copy(result, r.result, r.local_sem.at[0])
    result_copy.start()

    def backward_step(index, carry):
        step = L - 1 - index
        return tuple(
            scan_step(
                carry[group],
                spread(keep_next[rows_of(group, step), :]),
                adjoint[rows_of(group, step), :],
                1.0,
            )
            for group in range(GROUPS)
        )

    finals = segment_rows(lax.fori_loop(0, L, backward_step, none))[::-1]
    seg_masks = [
        clear(first + index * L + 1, first + (index + 1) * L + 1) for index in range(SEGMENTS)
    ][::-1]
    factor_seg = power(lam, L)
    own, _ = fold(zero1, factor_seg, finals, seg_masks, [None] * SEGMENTS)
    exchange = Exchange(own, lam, r.adj_tp, r.adj_seq, False)
    unit_grads(T - 1)
    if fused:
        reduces[T - 2].turn_plane()
    exchange.over_seq()
    grad_out = dot_tn(state_low[...], d_mixed[...]).astype(BF16)

    def divide(grad, full):
        for i in range(T):
            at = lax.rem(t + i, T) * n
            for part in range(2):
                rows = pl.ds(pl.multiple_of(part * N + at, n), n)
                full[i, part * (S // 4) : (part + 1) * (S // 4)] = grad[rows, :].reshape(
                    S // 4, 2, -1, D
                )

    if fused:
        r.grad_rates[...] = grad_out
        divide(r.grad_rates, r.out_full)
        out_reduce = Reduce(place, r.out_full, r.out_halves, r.out_eighths, r.out_summed)
        reduces[T - 1].over_plane()
        out_reduce.over_cores()
        unit_sums(T - 3)
    else:
        r.grad_out[...] = grad_out
    carry = exchange.carry()
    _, entering = fold(carry, factor_seg, finals, seg_masks, [None] * SEGMENTS)
    entering = entering[::-1]
    groups = tuple(
        tuple(
            jnp.concatenate([entering[group * 8 + sub][part] for sub in range(8)], 0)
            for part in range(2)
        )
        for group in range(GROUPS)
    )
    sums[...] = jnp.zeros_like(sums)

    def adjoint_step(step, carry, previous):
        new = []
        add_re = zero8
        add_im = zero8
        add_gamma = zero8
        for group in range(GROUPS):
            rows = rows_of(group, step)
            b = scan_step(carry[group], spread(keep_next[rows, :]), adjoint[rows, :], 1.0)
            new.append(b)
            adjoint[rows, :] = jnp.concatenate(b, 1)
            u = unpack(proj[rows, :])
            v = previous(group, step)
            mask = spread(keep[rows, :])
            add_re = add_re + mask * (b[0] * v[0] + b[1] * v[1])
            add_im = add_im + mask * (b[0] * v[1] - b[1] * v[0])
            add_gamma = add_gamma + b[0] * u[0] + b[1] * u[1]
        return tuple(new), (add_re, add_im, add_gamma)

    def adjoint_body(index, carry):
        values, totals = carry
        values, added = adjoint_step(
            L - 1 - index, values, lambda group, step: unpack(state[rows_of(group, step - 1), :])
        )
        return values, tuple(total + add for total, add in zip(totals, added))

    values, totals = lax.fori_loop(0, L - 1, adjoint_body, (groups, (zero8, zero8, zero8)))
    inside = entering_groups()
    _, added = adjoint_step(0, values, lambda group, step: inside[group])
    totals = [jnp.sum(total + add, 0, keepdims=True) for total, add in zip(totals, added)]

    if fused:
        out_reduce.over_plane()
    d_proj[...] = (adjoint[...] * gamma_signed).astype(BF16)
    grad_in = dot_tn(d_proj[...], normed[...]).astype(BF16)
    if fused:
        r.grad_rates[...] = grad_in
        divide(r.grad_rates, r.in_full)
        in_reduce = Reduce(place, r.in_full, r.in_halves, r.in_eighths, r.in_summed)
        in_reduce.over_cores()
        reduces[T - 1].turn_plane()
        unit_sums(T - 2)
        out_reduce.sum_plane()
        out_copies = [
            links.send(r.out_summed.at[i], r.out_sums.at[i - 1], (s, lax.rem(t + i, T)))
            for i in range(1, T)
        ]
        in_reduce.over_plane()
        unit_sums(T - 1)
    else:
        r.grad_in[...] = grad_in

    @pl.loop(0, R // BLOCK)
    def _(tile):
        rows = block_rows(tile)
        d_m = d_mixed[rows, :].astype(F32)
        d_n = dot(d_proj[rows, :], w_in[...]) + d_m * skip_row
        c = centred[rows, :]
        sums[0:8, :] += jnp.sum((d_n * c).reshape(BLOCK // 8, 8, D), 0)
        sums[8:16, :] += jnp.sum((d_m * normed[rows, :].astype(F32)).reshape(BLOCK // 8, 8, D), 0)
        d_c = d_n * gain_row
        mean = jnp.mean(d_c, 1, keepdims=True)
        cross = jnp.mean(d_c * c, 1, keepdims=True)
        inv = inv_std[rows, 0:1]
        out = cot_in[rows, :].astype(F32) + inv * (d_c - mean - c * cross)
        high = out.astype(BF16)
        out = dot(turn[...], high) + dot(turn[...], (out - high.astype(F32)).astype(BF16))
        for run, piece in enumerate(pieces(tile)):
            grad_tokens[piece, :] = out[run * SEGMENTS : run * SEGMENTS + SEGMENTS]

    grad_copy = pltpu.make_async_copy(grad_tokens, r.grad_tokens, r.local_sem.at[1])
    grad_copy.start()
    small = r.small
    small_rows = [
        jnp.sum(sums[0:8, :], 0, keepdims=True),
        jnp.sum(sums[8:16, :], 0, keepdims=True),
        jnp.concatenate(totals[:2], 1),
        jnp.concatenate([totals[2] / gamma, jnp.zeros_like(gamma)], 1),
    ]
    if not fused:
        for k, row in enumerate(small_rows):
            small[k : k + 1, :] = row
        small[4:8, :] = jnp.zeros((4, D), F32)
        links.close()
        result_copy.wait()
        grad_copy.wait()
        return

    small_tp, small_seq = (r.small_tp, r.small_seq)
    small_tp[t] = jnp.concatenate([packed(row, D // 128) for row in small_rows], 0)
    small_copies = [links.send(small_tp.at[t], small_tp.at[t], (s, peer)) for peer in peers_tp]

    def total_of(own, buffer):
        total = own.astype(F32)
        for k in range(buffer.shape[0]):
            total = total + buffer[k].astype(F32)
        return total.astype(BF16)

    unit_sum, out_sum, in_sum = (r.unit_sum, r.out_sum, r.in_sum)
    arrive(unit_copies)
    unit_sum[0, place.chip, place.core] = total_of(r.unit_summed[0, 0], r.unit_sums.at[:, 0])
    unit_spread = Spread(place, unit_sum)
    unit_spread.over_plane()

    in_reduce.sum_plane()
    in_copies = [
        links.send(r.in_summed.at[i], r.in_sums.at[i - 1], (s, lax.rem(t + i, T)))
        for i in range(1, T)
    ]
    arrive(out_copies)
    out_sum[0, place.chip, place.core] = total_of(r.out_summed[0], r.out_sums)
    out_spread = Spread(place, out_sum)
    out_spread.over_plane()

    arrive(small_copies)
    part = small_tp[0]
    for z in range(1, T):
        part = part + small_tp[z]
    small_seq[s] = part
    small_copies = [links.send(small_seq.at[s], small_seq.at[s], (peer, t)) for peer in peers_seq]

    unit_spread.over_cores()
    arrive(in_copies)
    in_sum[0, place.chip, place.core] = total_of(r.in_summed[0], r.in_sums)
    in_spread = Spread(place, in_sum)
    in_spread.over_plane()
    out_spread.over_cores()

    unit_spread.finish()
    unit_copy = pltpu.make_async_copy(unit_sum.at[0], r.grad_units, r.local_sem.at[2])
    unit_copy.start()

    arrive(small_copies)
    part = small_seq[0]
    for block in range(1, S):
        part = part + small_seq[block]
    for k in range(4):
        height = D // 128
        small[k : k + 1, :] = unpacked(part[k * height : (k + 1) * height], height)
    small[4:8, :] = jnp.zeros((4, D), F32)

    out_spread.finish()
    out_copy = pltpu.make_async_copy(out_sum.at[0], r.grad_out, r.local_sem.at[3])
    out_copy.start()
    in_spread.over_cores()
    in_spread.finish()
    in_copy = pltpu.make_async_copy(in_sum.at[0], r.grad_in, r.local_sem.at[4])
    in_copy.start()
    for copy in (result_copy, grad_copy, unit_copy, out_copy, in_copy):
        copy.wait()
    links.close()


def finish_kernel(T, names, *refs):
    r = types.SimpleNamespace(**dict(zip(names, refs)))
    half = r.grad_rows.shape[0] // 2
    arrays = [(r.result_in, r.result_rows, r.result)] + [
        tuple(ref.at[pl.ds(at, half)] for ref in (r.grad_tokens_in, r.grad_rows, r.grad_tokens))
        for at in (0, half)
    ]
    fetched = [
        pltpu.make_async_copy(source, kept, r.local_sem.at[index])
        for index, (source, kept, _) in enumerate(arrays)
    ]
    copies = [
        pltpu.make_async_copy(kept, target, r.local_sem.at[index])
        for index, (_, kept, target) in enumerate(arrays)
    ]
    for copy in fetched:
        copy.start()
    for fetch, copy in zip(fetched, copies):
        fetch.wait()
        copy.start()
    D_rows, lanes = (r.glu.shape[3], r.glu.shape[4])
    r.glu[0] = r.units_in[:, :, 0:D_rows, :lanes].astype(F32)
    r.glu[1] = r.units_in[:, :, 0:D_rows, lanes:].astype(F32)
    r.down[...] = r.units_in[:, :, D_rows:, :].astype(F32)
    r.out[...] = r.out_in[...].astype(F32)
    r.in_[...] = r.in_in[...].astype(F32)
    r.gain[...] = r.small[0:1, :]
    r.skip[...] = r.small[1:2, :]
    n = r.decay_log.shape[1]
    N = T * n
    t = lax.axis_index("tp")

    def mine(row, first):
        own = row[:, first : first + n]
        for z in range(1, T):
            own = jnp.where(t == z, row[:, first + z * n : first + z * n + n], own)
        return own

    lam_re, lam_im, gamma = decay_terms(r.decay_log[...], r.angle[...])
    g_re = mine(r.small[2:3, :], 0)
    g_im = mine(r.small[2:3, :], N)
    g_gamma = mine(r.small[3:4, :], 0)
    rate_step = jnp.exp(r.decay_log[...])
    r.decay[...] = rate_step * (
        g_gamma * (1.0 - fall(2.0 * rate_step)) / gamma - g_re * lam_re - g_im * lam_im
    )
    r.turn[...] = g_im * lam_re - g_re * lam_im
    for copy in copies:
        copy.wait()


def fall(value):
    series = jnp.ones_like(value)
    for order in range(12, 1, -1):
        series = 1.0 - value / order * series
    return jnp.where(value < 0.5, value * series, 1.0 - jnp.exp(-value))


def decay_terms(decay_log, angle):
    rate_step = jnp.exp(decay_log)
    radius = 1.0 - fall(rate_step)
    return (radius * jnp.cos(angle), radius * jnp.sin(angle), jnp.sqrt(fall(2.0 * rate_step)))


def local(
    S,
    T,
    tokens,
    ln_gain,
    in_proj,
    decay_log,
    angle,
    out_proj,
    skip,
    glu_proj,
    down_proj,
    lengths,
    cotangent,
):
    R, D = tokens.shape
    n = in_proj.shape[2]
    N = n * T
    units = down_proj.shape[0]
    C = S // 2
    fused = (
        S == 8
        and T % 2 == 0
        and T > 2
        and 2 * n == 128
        and 2 * units == D
        and all(size % (16 * S) == 0 for size in (D, 2 * n, units))
    )
    vmem = pl.BlockSpec(memory_space=pltpu.VMEM)
    anywhere = pl.BlockSpec(memory_space=pl.ANY)
    ins = dict(
        lengths=(lengths, pl.BlockSpec(memory_space=pltpu.SMEM)),
        tokens=(tokens, anywhere),
        cot=(cotangent, anywhere),
        gain=(ln_gain.reshape(1, D), vmem),
        skip=(skip.reshape(1, D), vmem),
    )
    outs = dict(
        result=((R, D), BF16, anywhere),
        grad_tokens=((R, D), F32, anywhere),
        small=((8, D), F32, vmem),
    )
    scratch = dict(
        tokens_raw=((R, D), BF16),
        cot_raw=((R, D), BF16),
        result_rows=((R, D), BF16),
        grad_rows=((R, D), F32),
        turn=((BLOCK, BLOCK), BF16),
        tokens_in=((R, D), BF16),
        cot_in=((R, D), BF16),
        centred=((R, D), F32),
        inv_std=((R, 128), F32),
        normed=((R, D), BF16),
        proj=((R, 2 * N), F32),
        keep=((R, 128), F32),
        keep_next=((R, 128), F32),
        state=((R, 2 * N), F32),
        state_low=((R, 2 * N), BF16),
        act=((R, D), BF16),
        d_gelu=((R, D), F32),
        d_act=((R, D), F32),
        summed=((R, D), F32),
        d_mixed=((R, D), BF16),
        adjoint=((R, 2 * N), F32),
        d_proj=((R, 2 * N), BF16),
        hidden=((R, units), BF16),
        d_unit=((R, 2 * units), BF16),
        seg_carry=((SEGMENTS, 2 * N), F32),
        sums=((16, D), F32),
        state_tp=((T, 8, 128), F32),
        state_seq=((S, 8, 128), F32),
        adj_tp=((T, 8, 128), F32),
        adj_seq=((S, 8, 128), F32),
    )
    in_rows = in_proj.transpose(0, 2, 1)
    if fused:
        unit_rows = D // S + units // S
        ins.update(
            decay_log=(decay_log.reshape(1, n), vmem),
            angle=(angle.reshape(1, n), vmem),
            in_proj=(in_rows.reshape(C, 2, 2 * n // S, D), anywhere),
            out_proj=(out_proj.reshape(C, 2, 2 * n // S, D), anywhere),
            glu_proj=(glu_proj.reshape(2, C, 2, D // S, units), anywhere),
            down_proj=(down_proj.reshape(C, 2, units // S, D), anywhere),
        )
        outs.update(
            grad_in=((C, 2, 2 * n // S, D), BF16, anywhere),
            grad_out=((C, 2, 2 * n // S, D), BF16, anywhere),
            grad_units=((C, 2, unit_rows, D), BF16, anywhere),
        )

        def whole(parts, rows, lead=()):
            return (lead + (parts, C, 2, rows, D), BF16)

        def halves(parts, rows, lead=()):
            return (lead + (parts, C, rows, D), BF16)

        def eighths(parts, rows, lead=()):
            return (lead + (C - 1, parts, rows, D), BF16)

        def own(parts, rows, lead=()):
            return (lead + (parts, rows, D), BF16)

        unit_sizes = (1, unit_rows, (T,))
        rate_sizes = (T, 2 * n // S)
        scratch.update(
            w_in=((2 * N, D), BF16),
            w_out=((2 * N, D), BF16),
            rates_all=((T, 8, 128), F32),
            in_slices=((T, C, 2, 2 * n // S, D), BF16),
            out_slices=((T, C, 2, 2 * n // S, D), BF16),
            unit_slices=((T, C, 2, unit_rows, D), BF16),
            grad_rates=((2 * N, D), BF16),
            small_tp=((T, 16, 128), F32),
            small_seq=((S, 16, 128), F32),
            unit_sums=((T - 1, 1, unit_rows, D), BF16),
            out_sums=((T - 1, 2 * n // S, D), BF16),
            in_sums=((T - 1, 2 * n // S, D), BF16),
            unit_sum=((1, C, 2, unit_rows, D), BF16),
            out_sum=((1, C, 2, 2 * n // S, D), BF16),
            in_sum=((1, C, 2, 2 * n // S, D), BF16),
            unit_full=whole(*unit_sizes),
            unit_halves=halves(*unit_sizes),
            unit_eighths=eighths(*unit_sizes),
            unit_summed=own(*unit_sizes),
            out_full=whole(*rate_sizes),
            out_halves=halves(*rate_sizes),
            out_eighths=eighths(*rate_sizes),
            out_summed=own(*rate_sizes),
            in_full=whole(*rate_sizes),
            in_halves=halves(*rate_sizes),
            in_eighths=eighths(*rate_sizes),
            in_summed=own(*rate_sizes),
        )
        links = 160
    else:
        w_in = lax.all_gather(in_rows, "tp", axis=1, tiled=True).reshape(2 * N, D)
        w_out = lax.all_gather(out_proj, "tp", axis=1, tiled=True).reshape(2 * N, D)
        glu = lax.all_gather(glu_proj, "tp")
        rates = jnp.stack(
            [lax.all_gather(part, "tp", tiled=True) for part in decay_terms(decay_log, angle)]
            + [jnp.zeros((N,), F32)] * 5
        )
        ins.update(
            rates=(rates, vmem),
            w_in=(w_in, vmem),
            w_out=(w_out, vmem),
            glu=(jnp.concatenate([glu[:, 0], glu[:, 1]], 2), vmem),
            down=(lax.all_gather(down_proj, "tp"), vmem),
        )
        outs.update(
            grad_in=((2 * N, D), BF16, vmem),
            grad_out=((2 * N, D), BF16, vmem),
            grad_glu=((T, D, 2 * units), BF16, vmem),
            grad_down=((T, units, D), BF16, vmem),
        )
        links = 2 * (T - 1 + S - 1)
    names = [*ins, *outs, *scratch, *dict(local_sem=0, send_sem=0, recv_sem=0)]
    results = pl.pallas_call(
        functools.partial(layer_kernel, S, T, fused, names),
        out_shape=tuple(jax.ShapeDtypeStruct(shape, dtype) for shape, dtype, _ in outs.values()),
        in_specs=[spec for _, spec in ins.values()],
        out_specs=tuple(spec for _, _, spec in outs.values()),
        scratch_shapes=[pltpu.VMEM(shape, dtype) for shape, dtype in scratch.values()]
        + [
            pltpu.SemaphoreType.DMA((7,)),
            pltpu.SemaphoreType.DMA((links,)),
            pltpu.SemaphoreType.DMA((links,)),
        ],
        compiler_params=pltpu.CompilerParams(
            collective_id=0, has_side_effects=True, vmem_limit_bytes=60 * 2**20
        ),
    )(*[value for value, _ in ins.values()])
    if fused:
        result, grad_tokens, small, grad_in, grad_out, grad_units = results
        ins = dict(
            result_in=(result, anywhere),
            grad_tokens_in=(grad_tokens, anywhere),
            small=(small, vmem),
            in_in=(grad_in, vmem),
            out_in=(grad_out, vmem),
            units_in=(grad_units, vmem),
            decay_log=(decay_log.reshape(1, n), vmem),
            angle=(angle.reshape(1, n), vmem),
        )
        outs = dict(
            result=((R, D), BF16, anywhere),
            grad_tokens=((R, D), F32, anywhere),
            gain=((1, D), F32, vmem),
            in_=((C, 2, 2 * n // S, D), F32, vmem),
            decay=((1, n), F32, vmem),
            turn=((1, n), F32, vmem),
            out=((C, 2, 2 * n // S, D), F32, vmem),
            skip=((1, D), F32, vmem),
            glu=((2, C, 2, D // S, units), F32, vmem),
            down=((C, 2, units // S, D), F32, vmem),
        )
        scratch = dict(result_rows=((R, D), BF16), grad_rows=((R, D), F32))
        names = [*ins, *outs, *scratch, *dict(local_sem=0)]
        result, grad_tokens, gain, in_, decay, turn, out, skip_sum, glu, down = pl.pallas_call(
            functools.partial(finish_kernel, T, names),
            out_shape=tuple(
                jax.ShapeDtypeStruct(shape, dtype) for shape, dtype, _ in outs.values()
            ),
            in_specs=[spec for _, spec in ins.values()],
            out_specs=tuple(spec for _, _, spec in outs.values()),
            scratch_shapes=[pltpu.VMEM(shape, dtype) for shape, dtype in scratch.values()]
            + [pltpu.SemaphoreType.DMA((3,))],
            compiler_params=pltpu.CompilerParams(vmem_limit_bytes=60 * 2**20),
        )(*[value for value, _ in ins.values()])
        return (
            result,
            grad_tokens,
            gain.reshape(D),
            in_.reshape(2, n, D).transpose(0, 2, 1),
            decay.reshape(n),
            turn.reshape(n),
            out.reshape(2, n, D),
            skip_sum.reshape(D),
            glu.reshape(2, D, units),
            down.reshape(units, D),
        )
    result, grad_tokens, small, grad_in, grad_out, grad_glu, grad_down = results
    small = lax.psum(small, ("seq", "tp"))

    def reduced(part):
        part = lax.psum_scatter(part, "tp", scatter_dimension=0, tiled=True)
        return lax.psum(part, "seq").astype(F32)

    def by_tp(grad):
        return reduced(grad.reshape(2, T, n, D).transpose(1, 0, 2, 3).reshape(T * 2, n, D))

    grad_glu = reduced(grad_glu)[0].reshape(D, 2, units).transpose(1, 0, 2)
    grad_down = reduced(grad_down)[0]

    def mine(row):
        return lax.dynamic_slice_in_dim(row, lax.axis_index("tp") * n, n)

    g_re, g_im, g_gamma = (mine(small[2, :N]), mine(small[2, N:]), mine(small[3, :N]))
    _, pull = jax.vjp(decay_terms, decay_log, angle)
    grad_decay, grad_angle = pull((g_re, g_im, g_gamma))
    return (
        result,
        grad_tokens,
        small[0],
        by_tp(grad_in).transpose(0, 2, 1),
        grad_decay,
        grad_angle,
        by_tp(grad_out),
        small[1],
        grad_glu,
        grad_down,
    )


def solution(mesh):
    in_specs = (
        P(("seq", "tp"), None),
        P(),
        P(None, None, "tp"),
        P("tp"),
        P("tp"),
        P(None, "tp", None),
        P(),
        P(None, None, "tp"),
        P("tp", None),
        P(),
        P(("seq", "tp"), None),
    )
    out_specs = (
        P(("seq", "tp"), None),
        P(("seq", "tp"), None),
        P(),
        P(None, None, "tp"),
        P("tp"),
        P("tp"),
        P(None, "tp", None),
        P(),
        P(None, None, "tp"),
        P("tp", None),
    )
    return jax.shard_map(
        functools.partial(local, mesh.shape["seq"], mesh.shape["tp"]),
        mesh=mesh,
        in_specs=in_specs,
        out_specs=out_specs,
        check_vma=False,
    )
```

```python
import functools
import types
import jax
import jax.numpy as jnp
from jax import lax
from jax.experimental import pallas as pl
from jax.experimental.pallas import tpu as pltpu
from jax.sharding import PartitionSpec as P

epsilon = 1e-05
MESH = pl.DeviceIdType.MESH
F32 = jnp.float32
BF16 = jnp.bfloat16
GROUPS = 2
SEGMENTS = 8 * GROUPS
BLOCK = SEGMENTS * SEGMENTS


def dot(left, right):
    return jnp.dot(left, right, preferred_element_type=F32)


def dot_nt(left, right):
    return lax.dot_general(left, right, (((1,), (1,)), ((), ())), preferred_element_type=F32)


def complex_mul(left_re, left_im, right_re, right_im):
    return (left_re * right_re - left_im * right_im, left_re * right_im + left_im * right_re)


def dot_tn(left, right):
    return lax.dot_general(left, right, (((0,), (0,)), ((), ())), preferred_element_type=F32)


def power(base, exponent):
    result = None
    square = base
    while exponent:
        if exponent & 1:
            result = square if result is None else complex_mul(*result, *square)
        exponent >>= 1
        if exponent:
            square = complex_mul(*square, *square)
    return result


class Links:
    def __init__(self, send_sem, recv_sem):
        self.send_sem = send_sem
        self.recv_sem = recv_sem
        self.started = []

    def send(self, source, target, device):
        index = len(self.started)
        copy = pltpu.make_async_remote_copy(
            src_ref=source,
            dst_ref=target,
            send_sem=self.send_sem.at[index],
            recv_sem=self.recv_sem.at[index],
            device_id=device,
            device_id_type=MESH,
        )
        copy.start()
        self.started.append(copy)
        return copy

    def close(self):
        for copy in self.started:
            copy.wait_send()


def arrive(copies):
    for copy in copies:
        copy.wait_recv()


class Gather:
    def __init__(self, place, buffer, first, last):
        self.place = place
        self.buffer = buffer
        self.slots = range(first, last)
        self.part = buffer.at[pl.ds(first, last - first)]

    def over_tp(self):
        p = self.place
        self.copies = [
            p.links.send(
                self.buffer.at[0, p.chip, p.core],
                self.buffer.at[slot, p.chip, p.core],
                (p.s, lax.rem(p.t + p.T - slot, p.T)),
            )
            for slot in self.slots
        ]

    def over_plane(self):
        p = self.place
        arrive(self.copies)
        mine = self.part.at[:, p.chip, p.core]
        self.copies = [p.links.send(mine, mine, device) for _, device in p.chips]

    def over_cores(self):
        p = self.place
        arrive(self.copies)
        mine = self.part.at[:, :, p.core]
        self.copies = [p.links.send(mine, mine, p.sibling)]

    def finish(self):
        arrive(self.copies)


class Reduce:
    def __init__(self, place, full, halves, eighths, summed):
        self.place = place
        self.full = full
        self.halves = halves
        self.eighths = eighths
        self.summed = summed

    def over_cores(self):
        p = self.place
        self.copies = [
            p.links.send(self.full.at[:, :, 1 - p.core], self.halves, p.sibling)
        ]

    def over_plane(self):
        p = self.place
        arrive(self.copies)
        parts, chips = self.halves.shape[:2]

        @pl.loop(0, parts * chips)
        def _(index):
            part, chip = (lax.div(index, chips), lax.rem(index, chips))
            self.halves[part, chip] = (
                self.full[part, chip, p.core].astype(F32) + self.halves[part, chip].astype(F32)
            ).astype(BF16)

        self.copies = [
            p.links.send(self.halves.at[:, chip], self.eighths.at[k], device)
            for k, (chip, device) in enumerate(p.chips)
        ]

    def sum_plane(self):
        p = self.place
        arrive(self.copies)

        @pl.loop(0, self.halves.shape[0])
        def _(part):
            total = self.halves[part, p.chip].astype(F32)
            for k in range(len(p.chips)):
                total = total + self.eighths[k, part].astype(F32)
            self.summed[part] = total.astype(BF16)


class Reduce2(Reduce):
    def __init__(self, place, full, halves, eighths, summed):
        super().__init__(place, full, halves, eighths, summed)
        self.rows = halves.shape[2] // 2
        self.ours = halves.at[:, :, pl.ds(0, self.rows)]
        self.theirs = halves.at[:, :, pl.ds(self.rows, self.rows)]

    def sum_cores(self, chip):
        self.halves[0, chip] = (
            self.full[0, chip, self.place.core].astype(F32) + self.halves[0, chip].astype(F32)
        ).astype(BF16)

    def over_plane(self):
        p = self.place
        arrive(self.copies)
        self.sum_cores(p.by_x)
        self.sum_cores(p.by_y)
        self.sum_cores(p.by_xy)
        self.copies = [
            p.links.send(part.at[0, chip], self.eighths.at[index, 0, rows], device)
            for index, part, chip, rows, device in (
                (0, self.ours, p.by_x, pl.ds(0, self.rows), p.x_device),
                (1, self.ours, p.by_xy, pl.ds(0, self.rows), p.x_device),
                (0, self.theirs, p.by_y, pl.ds(self.rows, self.rows), p.y_device),
                (1, self.theirs, p.by_xy, pl.ds(self.rows, self.rows), p.y_device),
            )
        ]
        self.sum_cores(p.chip)

    def turn_plane(self):
        p = self.place
        arrive(self.copies)
        n = self.rows
        for index, chip in ((0, p.chip), (1, p.by_y)):
            self.halves[0, chip, 0:n] = (
                self.halves[0, chip, 0:n].astype(F32) + self.eighths[index, 0, 0:n].astype(F32)
            ).astype(BF16)
        for index, chip in ((0, p.chip), (1, p.by_x)):
            self.halves[0, chip, n:] = (
                self.halves[0, chip, n:].astype(F32) + self.eighths[index, 0, n:].astype(F32)
            ).astype(BF16)
        self.copies = [
            p.links.send(self.ours.at[0, p.by_y], self.eighths.at[2, 0, pl.ds(0, n)], p.y_device),
            p.links.send(self.theirs.at[0, p.by_x], self.eighths.at[2, 0, pl.ds(n, n)], p.x_device),
        ]

    def sum_plane(self):
        p = self.place
        arrive(self.copies)
        self.summed[0] = (
            self.halves[0, p.chip].astype(F32) + self.eighths[2, 0].astype(F32)
        ).astype(BF16)


class Spread:
    def __init__(self, place, buffer):
        self.place = place
        self.buffer = buffer

    def over_plane(self):
        p = self.place
        mine = self.buffer.at[:, p.chip, p.core]
        self.copies = [p.links.send(mine, mine, device) for _, device in p.chips]

    def over_cores(self):
        p = self.place
        arrive(self.copies)
        mine = self.buffer.at[:, :, p.core]
        self.copies = [p.links.send(mine, mine, p.sibling)]

    def finish(self):
        arrive(self.copies)


class Place:
    def __init__(self, S, T, links):
        self.S, self.T, self.links = (S, T, links)
        self.s = lax.axis_index("seq")
        self.t = lax.axis_index("tp")
        C = S // 2
        self.core = lax.rem(self.s, 2)
        self.chip = lax.div(self.s, 2)
        self.sibling = (self.chip * 2 + 1 - self.core, self.t)
        x = lax.rem(self.chip, 2)
        y = lax.div(self.chip, 2)
        self.by_x = y * 2 + 1 - x
        self.by_y = (1 - y) * 2 + x
        self.by_xy = (1 - y) * 2 + 1 - x
        self.x_device = (self.by_x * 2 + self.core, self.t)
        self.y_device = (self.by_y * 2 + self.core, self.t)
        self.chips = []
        for k in range(1, C):
            chip = lax.rem(self.chip + k, C)
            self.chips.append((chip, (chip * 2 + self.core, self.t)))


def layer_kernel(S, T, fused, names, *refs):
    r = types.SimpleNamespace(**dict(zip(names, refs)))
    links = Links(r.send_sem, r.recv_sem)
    place = Place(S, T, links)
    lengths = r.counts
    tokens = r.tokens_raw
    cot = r.cot_raw
    result = r.tokens_raw
    grad_tokens = r.d_gelu
    turn = r.turn
    tokens_in = r.tokens_in
    cot_in = r.cot_in
    centred = r.centred
    inv_std = r.inv_std
    normed = r.normed
    proj = r.proj
    keep = r.keep
    keep_next = r.keep_next
    state = r.state
    state_low = r.state_low
    act = r.act
    d_gelu = r.d_gelu
    d_act = r.d_act
    summed = r.summed
    d_mixed = r.d_mixed
    adjoint = r.summed
    d_proj = r.d_proj
    hidden = r.hidden
    d_unit = r.d_unit
    seg_carry, sums = (r.seg_carry, r.sums)
    w_in, w_out = (r.w_in, r.w_out)
    R, D = tokens.shape
    N = w_in.shape[0] // 2
    n = N // T
    L = R // SEGMENTS
    s = place.s
    t = place.t
    first = (s * T + t) * R

    peers_tp = [lax.rem(t + k, T) for k in range(1, T)]
    peers_seq = [lax.rem(s + k, S) for k in range(1, S)]
    barrier = pltpu.get_barrier_semaphore()
    for peer in peers_tp:
        pl.semaphore_signal(barrier, inc=1, device_id=(s, peer), device_id_type=MESH)
    for peer in peers_seq:
        pl.semaphore_signal(barrier, inc=1, device_id=(peer, t), device_id_type=MESH)

    fetched = [
        pltpu.make_async_copy(source, target, r.local_sem.at[index])
        for index, (source, target) in enumerate(
            ((r.tokens, tokens), (r.cot, cot), (r.gain, r.gain_row), (r.skip, r.skip_row), (r.lengths, r.counts))
        )
    ]
    if fused:
        in_slices, out_slices, unit_slices = (r.in_slices, r.out_slices, r.unit_slices)
        units = r.down_proj.shape[2] * S
        D_rows = r.glu_proj.shape[3]
        gated_rows = unit_slices.at[0, :, :, pl.ds(0, D_rows)]
        weights = [
            pltpu.make_async_copy(source, target, r.local_sem.at[5 + index])
            for index, (source, target) in enumerate(
                (
                    (r.decay_log, r.decay_row),
                    (r.angle, r.angle_row),
                    (r.in_proj, in_slices.at[0]),
                    (r.out_proj, out_slices.at[0]),
                    (r.glu_proj.at[0], gated_rows.at[:, :, :, pl.ds(0, units)]),
                    (r.glu_proj.at[1], gated_rows.at[:, :, :, pl.ds(units, units)]),
                    (r.down_proj, unit_slices.at[0, :, :, pl.ds(D_rows, units // S)]),
                )
            )
        ]
        for copy in weights:
            copy.start()
    for copy in fetched:
        copy.start()
    if fused:
        rates_all = r.rates_all
        rates_all[t] = jnp.zeros(rates_all.shape[1:], F32)
        gather_in = Gather(place, in_slices, 1, T)
        gather_out = Gather(place, out_slices, 1, T)
        gather_units = [Gather(place, unit_slices, slot, slot + 1) for slot in range(1, T)]
        for copy in weights:
            copy.wait()
        for index, row in enumerate(decay_terms(r.decay_row[...], r.angle_row[...])):
            rates_all[t, index : index + 1, 0:n] = row
        pl.semaphore_wait(barrier, T - 1 + S - 1)
        gather_in.over_tp()
        rate_copies = [
            links.send(rates_all.at[t], rates_all.at[t], (s, peer)) for peer in peers_tp
        ]

    for copy in fetched[2:]:
        copy.wait()
    starts = []
    total = jnp.int32(0)
    for index in range(lengths.shape[0]):
        starts.append(total)
        total = total + lengths[index]

    def keeps(position):
        hit = position == starts[0]
        for start in starts[1:]:
            hit = hit | (position == start)
        return jnp.where(hit, 0.0, 1.0)

    def clear(low, high):
        hit = (starts[0] >= low) & (starts[0] < high)
        for start in starts[1:]:
            hit = hit | ((start >= low) & (start < high))
        return jnp.where(hit, 0.0, 1.0)

    gain_row = r.gain_row[...]
    skip_row = r.skip_row[...].astype(F32).reshape(1, D)

    down_index = lax.broadcasted_iota(jnp.int32, (BLOCK, BLOCK), 0)
    across_index = lax.broadcasted_iota(jnp.int32, (BLOCK, BLOCK), 1)
    turned = lax.rem(down_index, SEGMENTS) * SEGMENTS + lax.div(down_index, SEGMENTS)
    turn[...] = jnp.where(turned == across_index, 1.0, 0.0).astype(BF16)

    def pieces(block):
        return [
            pl.ds(pl.multiple_of(run * L + block * SEGMENTS, SEGMENTS), SEGMENTS)
            for run in range(SEGMENTS)
        ]

    def taken(ref, block):
        return dot(turn[...], jnp.concatenate([ref[piece, :] for piece in pieces(block)], 0))

    def block_rows(tile):
        return pl.ds(pl.multiple_of(tile * BLOCK, BLOCK), BLOCK)

    def norm_tile(tile):
        rows = block_rows(tile)
        x = taken(tokens, tile)
        tokens_in[rows, :] = x.astype(BF16)
        mean = jnp.mean(x, 1, keepdims=True)
        inv = lax.rsqrt(jnp.mean(x * x, 1, keepdims=True) - mean * mean + epsilon)
        c = (x - mean) * inv
        centred[rows, :] = c
        inv_std[rows, :] = jnp.broadcast_to(inv, (BLOCK, 128))
        n_rows = (c * gain_row).astype(BF16)
        normed[rows, :] = n_rows

    def cot_tile(tile):
        rows = block_rows(tile)
        cot_rows = taken(cot, tile).astype(BF16)
        cot_in[rows, :] = cot_rows
        index = tile * BLOCK + lax.broadcasted_iota(jnp.int32, (BLOCK, 128), 0)
        position = first + lax.rem(index, SEGMENTS) * L + lax.div(index, SEGMENTS)
        keep[rows, :] = keeps(position)
        keep_next[rows, :] = keeps(position + 1)

    fetched[0].wait()
    pl.loop(0, R // BLOCK)(norm_tile)
    if fused:
        gather_in.over_plane()
        gather_out.over_tp()
        gather_units[0].over_tp()
    fetched[1].wait()
    pl.loop(0, R // BLOCK)(cot_tile)

    def assemble(slices, weight):
        for i in range(T):
            at = lax.rem(t + i, T) * n
            for part in range(2):
                weight[pl.ds(pl.multiple_of(part * N + at, n), n), :] = slices[
                    i, part * (S // 4) : (part + 1) * (S // 4)
                ].reshape(n, D)

    if fused:
        gather_in.over_cores()
        gather_units[1].over_tp()
        arrive(rate_copies)
        half = lax.broadcasted_iota(jnp.int32, (8, 128), 1) < n
        rate_rows = [rates_all[z] for z in range(T)]
        joined = jnp.concatenate(
            [
                jnp.where(half, rate_rows[z], pltpu.roll(rate_rows[z + 1], n, 1))
                for z in range(0, T, 2)
            ],
            1,
        )
        lam_re, lam_im, gamma = (joined[k : k + 1] for k in range(3))
        gather_in.finish()
        for gather in gather_units[2:]:
            gather.over_tp()
        gather_out.over_plane()
        assemble(in_slices, w_in)
    else:
        pl.semaphore_wait(barrier, T - 1 + S - 1)
        lam_re, lam_im, gamma = (r.rates[k : k + 1, :] for k in range(3))
    gamma_signed = jnp.concatenate([gamma, -gamma], 1)

    @pl.loop(0, R // BLOCK)
    def _(tile):
        rows = block_rows(tile)
        proj[rows, :] = dot_nt(normed[rows, :], w_in[...]) * gamma_signed

    low8_re = jnp.broadcast_to(lam_re, (8, N))
    low8_im = jnp.broadcast_to(lam_im, (8, N))

    def rows_of(group, step):
        return pl.ds(pl.multiple_of(step * SEGMENTS + group * 8, 8), 8)

    def spread(row):
        return jnp.concatenate([row] * (N // 128), 1)

    def scan_step(values, mask, add, sign):
        new_re, new_im = complex_mul(low8_re, sign * low8_im, *(value * mask for value in values))
        return (new_re + add[:, :N], new_im + add[:, N:])

    zero8 = jnp.zeros((8, N), F32)
    none = tuple((zero8, zero8) for _ in range(GROUPS))

    def forward_step(step, carry):
        return tuple(
            scan_step(
                carry[group],
                spread(keep[rows_of(group, step), :]),
                proj[rows_of(group, step), :],
                -1.0,
            )
            for group in range(GROUPS)
        )

    def segment_rows(finals):
        return [
            (finals[group][0][sub : sub + 1], finals[group][1][sub : sub + 1])
            for group in range(GROUPS)
            for sub in range(8)
        ]

    def fold(start, factor, items, masks, taken):
        before = []
        carry = start
        for (item_re, item_im), mask, take in zip(items, masks, taken):
            before.append(carry)
            moved = complex_mul(*factor, *carry)
            longer = (moved[0] * mask + item_re, moved[1] * mask + item_im)
            if take is None:
                carry = longer
            else:
                carry = tuple(jnp.where(take, new, old) for new, old in zip(longer, carry))
        return carry, before

    zero1 = (jnp.zeros((1, N), F32), jnp.zeros((1, N), F32))
    lam = (lam_re, lam_im)
    conj = (lam_re, -lam_im)

    def unpack(row):
        return (row[:, :N], row[:, N:])

    def packed(row, height):
        parts = [row[:, at : at + 128] for at in range(0, row.shape[1], 128)]
        return jnp.concatenate(parts + [parts[0]] * (height - len(parts)), 0)

    def unpacked(tile, height):
        return jnp.concatenate([tile[k : k + 1, :] for k in range(height)], 1)

    class Exchange:
        def __init__(self, own, factor, tp_buf, seq_buf, forward):
            self.forward = forward
            self.shift = 0 if forward else 1
            self.factor_tp = power(factor, R)
            self.factor_seq = power(self.factor_tp, T)
            self.tp_buf, self.seq_buf = (tp_buf, seq_buf)
            tp_buf[t] = packed(jnp.concatenate(own, 1), 8)
            self.copies = [
                links.send(tp_buf.at[t], tp_buf.at[t], (s, peer)) for peer in peers_tp
            ]

        def order(self, count):
            return list(range(count)) if self.forward else list(range(count))[::-1]

        def before(self, other, mine):
            return other < mine if self.forward else other > mine

        def value(self, tile):
            return unpack(unpacked(tile, 2 * N // 128))

        def over_seq(self):
            arrive(self.copies)
            row = s * T * R + self.shift
            self.items = [self.value(self.tp_buf[z]) for z in self.order(T)]
            self.masks = [clear(row + z * R, row + (z + 1) * R) for z in self.order(T)]
            block, _ = fold(zero1, self.factor_tp, self.items, self.masks, [None] * T)
            self.seq_buf[s] = packed(jnp.concatenate(block, 1), 8)
            self.copies = [
                links.send(self.seq_buf.at[s], self.seq_buf.at[s], (peer, t)) for peer in peers_seq
            ]

        def carry(self):
            arrive(self.copies)
            blocks = self.order(S)
            span = T * R
            carry, _ = fold(
                zero1,
                self.factor_seq,
                [self.value(self.seq_buf[block]) for block in blocks],
                [clear(block * span + self.shift, (block + 1) * span + self.shift) for block in blocks],
                [self.before(block, s) for block in blocks],
            )
            carry, _ = fold(
                carry,
                self.factor_tp,
                self.items,
                self.masks,
                [self.before(z, t) for z in self.order(T)],
            )
            return carry

    finals = segment_rows(lax.fori_loop(0, L, forward_step, none))
    seg_masks = [clear(first + index * L, first + (index + 1) * L) for index in range(SEGMENTS)]
    factor_seg = power(conj, L)
    own, _ = fold(zero1, factor_seg, finals, seg_masks, [None] * SEGMENTS)
    exchange = Exchange(own, conj, r.state_tp, r.state_seq, True)
    if fused:
        gather_units[0].over_plane()
        gather_out.over_cores()
    exchange.over_seq()
    if fused:
        gather_units[1].over_plane()
        gather_out.finish()
        assemble(out_slices, w_out)
    carry = exchange.carry()
    _, entering = fold(carry, factor_seg, finals, seg_masks, [None] * SEGMENTS)
    for index, (row_re, row_im) in enumerate(entering):
        seg_carry[index : index + 1, :] = jnp.concatenate([row_re, row_im], 1)

    def write_state(step, carry):
        new = forward_step(step, carry)
        for group in range(GROUPS):
            state[rows_of(group, step), :] = jnp.concatenate(new[group], 1)
        return new

    def entering_groups():
        return tuple(
            unpack(seg_carry[group * 8 : group * 8 + 8, :]) for group in range(GROUPS)
        )

    lax.fori_loop(0, L, write_state, entering_groups())
    if fused:
        for gather in gather_units[2:]:
            gather.over_plane()

    @pl.loop(0, R // BLOCK)
    def _(tile):
        rows = block_rows(tile)
        low = state[rows, :].astype(BF16)
        state_low[rows, :] = low
        x = dot(low, w_out[...]) + skip_row * normed[rows, :].astype(F32)
        scale = 0.7978845608028654
        th = jnp.tanh(scale * (x + 0.044715 * x * x * x))
        half = 0.5 * (1.0 + th)
        a = (x * half).astype(BF16)
        act[rows, :] = a
        d_gelu[rows, :] = half + 0.5 * x * (1.0 - th * th) * scale * (1.0 + 0.134145 * x * x)

    if fused:
        reduces = [
            Reduce2(
                place,
                r.unit_full.at[i],
                r.unit_halves.at[i],
                r.unit_eighths.at[i],
                r.unit_summed.at[i],
            )
            for i in range(T)
        ]

    UNIT_ROWS = min(512, R)
    units = hidden.shape[1]
    unit_copies = []

    def unit_grads(i):
        c = lax.rem(t + i, T)
        gated_grad = dot_tn(act[...], d_unit[...]).astype(BF16)
        down_grad = dot_tn(hidden[...], cot_in[...]).astype(BF16)
        if fused:
            full = r.unit_full
            full[i, 0, :, :, 0:D_rows] = gated_grad.reshape(S // 2, 2, D_rows, 2 * units)
            full[i, 0, :, :, D_rows:] = down_grad.reshape(S // 2, 2, units // S, D)
            reduces[i].over_cores()
        else:
            r.grad_glu[c] = gated_grad
            r.grad_down[c] = down_grad

    def unit_sums(i):
        reduces[i].sum_plane()
        if i > 0:
            unit_copies.append(
                links.send(r.unit_summed.at[i], r.unit_sums.at[i - 1], (s, lax.rem(t + i, T)))
            )

    for i in range(T):
        c = lax.rem(t + i, T)
        if fused:
            if i > 0:
                gather_units[i - 1].finish()
            if i < T - 1:
                gather_units[i].over_cores()
            w_gated = unit_slices[i, :, :, 0:D_rows].reshape(D, 2 * units)
            w_down = unit_slices[i, :, :, D_rows:].reshape(units, D)
        else:
            w_gated = r.glu[c]
            w_down = r.down[c]

        for tile in range(R // UNIT_ROWS):
            rows = slice(tile * UNIT_ROWS, (tile + 1) * UNIT_ROWS)
            both = dot(act[rows, :], w_gated)
            value, gate = (both[:, :units], both[:, units:])
            sigma = 0.5 * jnp.tanh(0.5 * gate) + 0.5
            gated = value * sigma
            h = gated.astype(BF16)
            hidden[rows, :] = h
            d_h = dot_nt(cot_in[rows, :], w_down)
            d_both = jnp.concatenate(
                [(d_h * sigma).astype(BF16), (d_h * gated * (1.0 - sigma)).astype(BF16)], 1
            )
            d_unit[rows, :] = d_both
            added = dot(h, w_down)
            d_a = dot_nt(d_both, w_gated)
            if i > 0:
                added = added + summed[rows, :]
                d_a = d_a + d_act[rows, :]
            if i < T - 1:
                summed[rows, :] = added
                d_act[rows, :] = d_a
            else:
                d_m = (d_gelu[rows, :] * d_a).astype(BF16)
                d_mixed[rows, :] = d_m
                adjoint[rows, :] = dot_nt(d_m, w_out[...])
                out = (tokens_in[rows, :].astype(F32) + added).astype(BF16)
                for block in range(UNIT_ROWS // BLOCK):
                    turned = dot(turn[...], out[block * BLOCK : block * BLOCK + BLOCK])
                    turned = turned.astype(BF16)
                    for run, piece in enumerate(pieces(tile * (UNIT_ROWS // BLOCK) + block)):
                        result[piece, :] = turned[run * SEGMENTS : run * SEGMENTS + SEGMENTS]

        if fused and i > 0:
            reduces[i - 1].over_plane()
        if i < T - 1:
            unit_grads(i)
        if fused and i > 1:
            reduces[i - 2].turn_plane()
        if fused and i > 2:
            unit_sums(i - 3)

    result_copy = pltpu.make_async_copy(result, r.result, r.local_sem.at[0])
    result_copy.start()

    def backward_step(index, carry):
        step = L - 1 - index
        return tuple(
            scan_step(
                carry[group],
                spread(keep_next[rows_of(group, step), :]),
                adjoint[rows_of(group, step), :],
                1.0,
            )
            for group in range(GROUPS)
        )

    finals = segment_rows(lax.fori_loop(0, L, backward_step, none))[::-1]
    seg_masks = [
        clear(first + index * L + 1, first + (index + 1) * L + 1) for index in range(SEGMENTS)
    ][::-1]
    factor_seg = power(lam, L)
    own, _ = fold(zero1, factor_seg, finals, seg_masks, [None] * SEGMENTS)
    exchange = Exchange(own, lam, r.adj_tp, r.adj_seq, False)
    unit_grads(T - 1)
    if fused:
        reduces[T - 2].turn_plane()
    exchange.over_seq()
    grad_out = dot_tn(state_low[...], d_mixed[...]).astype(BF16)

    def divide(grad, full):
        for i in range(T):
            at = lax.rem(t + i, T) * n
            for part in range(2):
                rows = pl.ds(pl.multiple_of(part * N + at, n), n)
                full[i, part * (S // 4) : (part + 1) * (S // 4)] = grad[rows, :].reshape(
                    S // 4, 2, -1, D
                )

    if fused:
        r.grad_rates[...] = grad_out
        divide(r.grad_rates, r.out_full)
        out_reduce = Reduce(place, r.out_full, r.out_halves, r.out_eighths, r.out_summed)
        reduces[T - 1].over_plane()
        out_reduce.over_cores()
        unit_sums(T - 3)
    else:
        r.grad_out[...] = grad_out
    carry = exchange.carry()
    _, entering = fold(carry, factor_seg, finals, seg_masks, [None] * SEGMENTS)
    entering = entering[::-1]
    groups = tuple(
        tuple(
            jnp.concatenate([entering[group * 8 + sub][part] for sub in range(8)], 0)
            for part in range(2)
        )
        for group in range(GROUPS)
    )
    sums[...] = jnp.zeros_like(sums)

    def adjoint_step(step, carry, previous):
        new = []
        add_re = zero8
        add_im = zero8
        add_gamma = zero8
        for group in range(GROUPS):
            rows = rows_of(group, step)
            b = scan_step(carry[group], spread(keep_next[rows, :]), adjoint[rows, :], 1.0)
            new.append(b)
            adjoint[rows, :] = jnp.concatenate(b, 1)
            u = unpack(proj[rows, :])
            v = previous(group, step)
            mask = spread(keep[rows, :])
            add_re = add_re + mask * (b[0] * v[0] + b[1] * v[1])
            add_im = add_im + mask * (b[0] * v[1] - b[1] * v[0])
            add_gamma = add_gamma + b[0] * u[0] + b[1] * u[1]
        return tuple(new), (add_re, add_im, add_gamma)

    def adjoint_body(index, carry):
        values, totals = carry
        values, added = adjoint_step(
            L - 1 - index, values, lambda group, step: unpack(state[rows_of(group, step - 1), :])
        )
        return values, tuple(total + add for total, add in zip(totals, added))

    values, totals = lax.fori_loop(0, L - 1, adjoint_body, (groups, (zero8, zero8, zero8)))
    inside = entering_groups()
    _, added = adjoint_step(0, values, lambda group, step: inside[group])
    totals = [jnp.sum(total + add, 0, keepdims=True) for total, add in zip(totals, added)]

    if fused:
        out_reduce.over_plane()
    d_proj[...] = (adjoint[...] * gamma_signed).astype(BF16)
    grad_in = dot_tn(d_proj[...], normed[...]).astype(BF16)
    if fused:
        r.grad_rates[...] = grad_in
        divide(r.grad_rates, r.in_full)
        in_reduce = Reduce(place, r.in_full, r.in_halves, r.in_eighths, r.in_summed)
        in_reduce.over_cores()
        reduces[T - 1].turn_plane()
        unit_sums(T - 2)
        out_reduce.sum_plane()
        out_copies = [
            links.send(r.out_summed.at[i], r.out_sums.at[i - 1], (s, lax.rem(t + i, T)))
            for i in range(1, T)
        ]
        in_reduce.over_plane()
        unit_sums(T - 1)
    else:
        r.grad_in[...] = grad_in

    @pl.loop(0, R // BLOCK)
    def _(tile):
        rows = block_rows(tile)
        d_m = d_mixed[rows, :].astype(F32)
        d_n = dot(d_proj[rows, :], w_in[...]) + d_m * skip_row
        c = centred[rows, :]
        sums[0:8, :] += jnp.sum((d_n * c).reshape(BLOCK // 8, 8, D), 0)
        sums[8:16, :] += jnp.sum((d_m * normed[rows, :].astype(F32)).reshape(BLOCK // 8, 8, D), 0)
        d_c = d_n * gain_row
        mean = jnp.mean(d_c, 1, keepdims=True)
        cross = jnp.mean(d_c * c, 1, keepdims=True)
        inv = inv_std[rows, 0:1]
        out = cot_in[rows, :].astype(F32) + inv * (d_c - mean - c * cross)
        high = out.astype(BF16)
        out = dot(turn[...], high) + dot(turn[...], (out - high.astype(F32)).astype(BF16))
        for run, piece in enumerate(pieces(tile)):
            grad_tokens[piece, :] = out[run * SEGMENTS : run * SEGMENTS + SEGMENTS]

    grad_copy = pltpu.make_async_copy(grad_tokens, r.grad_tokens, r.local_sem.at[1])
    grad_copy.start()
    small = r.small
    small_rows = [
        jnp.sum(sums[0:8, :], 0, keepdims=True),
        jnp.sum(sums[8:16, :], 0, keepdims=True),
        jnp.concatenate(totals[:2], 1),
        jnp.concatenate([totals[2] / gamma, jnp.zeros_like(gamma)], 1),
    ]
    if not fused:
        for k, row in enumerate(small_rows):
            small[k : k + 1, :] = row
        small[4:8, :] = jnp.zeros((4, D), F32)
        links.close()
        result_copy.wait()
        grad_copy.wait()
        return

    small_tp, small_seq = (r.small_tp, r.small_seq)
    small_tp[t] = jnp.concatenate([packed(row, D // 128) for row in small_rows], 0)
    small_copies = [links.send(small_tp.at[t], small_tp.at[t], (s, peer)) for peer in peers_tp]

    def total_of(own, buffer):
        total = own.astype(F32)
        for k in range(buffer.shape[0]):
            total = total + buffer[k].astype(F32)
        return total.astype(BF16)

    unit_sum, out_sum, in_sum = (r.unit_sum, r.out_sum, r.in_sum)
    arrive(unit_copies)
    unit_sum[0, place.chip, place.core] = total_of(r.unit_summed[0, 0], r.unit_sums.at[:, 0])
    unit_spread = Spread(place, unit_sum)
    unit_spread.over_plane()

    in_reduce.sum_plane()
    in_copies = [
        links.send(r.in_summed.at[i], r.in_sums.at[i - 1], (s, lax.rem(t + i, T)))
        for i in range(1, T)
    ]
    arrive(out_copies)
    out_sum[0, place.chip, place.core] = total_of(r.out_summed[0], r.out_sums)
    out_spread = Spread(place, out_sum)
    out_spread.over_plane()

    arrive(small_copies)
    part = small_tp[0]
    for z in range(1, T):
        part = part + small_tp[z]
    small_seq[s] = part
    small_copies = [links.send(small_seq.at[s], small_seq.at[s], (peer, t)) for peer in peers_seq]

    unit_spread.over_cores()
    arrive(in_copies)
    in_sum[0, place.chip, place.core] = total_of(r.in_summed[0], r.in_sums)
    in_spread = Spread(place, in_sum)
    in_spread.over_plane()
    out_spread.over_cores()

    unit_spread.finish()
    unit_copy = pltpu.make_async_copy(unit_sum.at[0], r.grad_units, r.local_sem.at[2])
    unit_copy.start()

    arrive(small_copies)
    part = small_seq[0]
    for block in range(1, S):
        part = part + small_seq[block]
    for k in range(4):
        height = D // 128
        small[k : k + 1, :] = unpacked(part[k * height : (k + 1) * height], height)
    small[4:8, :] = jnp.zeros((4, D), F32)

    out_spread.finish()
    out_copy = pltpu.make_async_copy(out_sum.at[0], r.grad_out, r.local_sem.at[3])
    out_copy.start()
    in_spread.over_cores()
    in_spread.finish()
    in_copy = pltpu.make_async_copy(in_sum.at[0], r.grad_in, r.local_sem.at[4])
    in_copy.start()
    for copy in (result_copy, grad_copy, unit_copy, out_copy, in_copy):
        copy.wait()
    links.close()


def finish_kernel(T, names, *refs):
    r = types.SimpleNamespace(**dict(zip(names, refs)))
    half = r.grad_rows.shape[0] // 2
    arrays = [(r.result_in, r.result_rows, r.result)] + [
        tuple(ref.at[pl.ds(at, half)] for ref in (r.grad_tokens_in, r.grad_rows, r.grad_tokens))
        for at in (0, half)
    ]
    fetched = [
        pltpu.make_async_copy(source, kept, r.local_sem.at[index])
        for index, (source, kept, _) in enumerate(arrays)
    ]
    copies = [
        pltpu.make_async_copy(kept, target, r.local_sem.at[index])
        for index, (_, kept, target) in enumerate(arrays)
    ]
    for copy in fetched:
        copy.start()
    for fetch, copy in zip(fetched, copies):
        fetch.wait()
        copy.start()
    D_rows, lanes = (r.glu.shape[3], r.glu.shape[4])
    r.glu[0] = r.units_in[:, :, 0:D_rows, :lanes].astype(F32)
    r.glu[1] = r.units_in[:, :, 0:D_rows, lanes:].astype(F32)
    r.down[...] = r.units_in[:, :, D_rows:, :].astype(F32)
    r.out[...] = r.out_in[...].astype(F32)
    r.in_[...] = r.in_in[...].astype(F32)
    r.gain[...] = r.small[0:1, :]
    r.skip[...] = r.small[1:2, :]
    n = r.decay_log.shape[1]
    N = T * n
    t = lax.axis_index("tp")

    def mine(row, first):
        own = row[:, first : first + n]
        for z in range(1, T):
            own = jnp.where(t == z, row[:, first + z * n : first + z * n + n], own)
        return own

    lam_re, lam_im, gamma = decay_terms(r.decay_log[...], r.angle[...])
    g_re = mine(r.small[2:3, :], 0)
    g_im = mine(r.small[2:3, :], N)
    g_gamma = mine(r.small[3:4, :], 0)
    rate_step = jnp.exp(r.decay_log[...])
    r.decay[...] = rate_step * (
        g_gamma * (1.0 - fall(2.0 * rate_step)) / gamma - g_re * lam_re - g_im * lam_im
    )
    r.turn[...] = g_im * lam_re - g_re * lam_im
    for copy in copies:
        copy.wait()


def fall(value):
    series = jnp.ones_like(value)
    for order in range(12, 1, -1):
        series = 1.0 - value / order * series
    return jnp.where(value < 0.5, value * series, 1.0 - jnp.exp(-value))


def decay_terms(decay_log, angle):
    rate_step = jnp.exp(decay_log)
    radius = 1.0 - fall(rate_step)
    return (radius * jnp.cos(angle), radius * jnp.sin(angle), jnp.sqrt(fall(2.0 * rate_step)))


def local(
    S,
    T,
    tokens,
    ln_gain,
    in_proj,
    decay_log,
    angle,
    out_proj,
    skip,
    glu_proj,
    down_proj,
    lengths,
    cotangent,
):
    R, D = tokens.shape
    n = in_proj.shape[2]
    N = n * T
    units = down_proj.shape[0]
    C = S // 2
    fused = (
        S == 8
        and T % 2 == 0
        and T > 2
        and 2 * n == 128
        and 2 * units == D
        and all(size % (16 * S) == 0 for size in (D, 2 * n, units))
    )
    vmem = pl.BlockSpec(memory_space=pltpu.VMEM)
    anywhere = pl.BlockSpec(memory_space=pl.ANY)
    hbm = pl.BlockSpec(memory_space=pltpu.HBM)
    ins = dict(
        lengths=(lengths, hbm),
        tokens=(tokens, hbm),
        cot=(cotangent, hbm),
        gain=(ln_gain.reshape(1, D), hbm),
        skip=(skip, hbm),
    )
    outs = dict(
        result=((R, D), BF16, anywhere),
        grad_tokens=((R, D), F32, anywhere),
        small=((8, D), F32, vmem),
    )
    scratch = dict(
        gain_row=((1, D), F32),
        skip_row=((D,), BF16),
        tokens_raw=((R, D), BF16),
        cot_raw=((R, D), BF16),
        turn=((BLOCK, BLOCK), BF16),
        tokens_in=((R, D), BF16),
        cot_in=((R, D), BF16),
        centred=((R, D), F32),
        inv_std=((R, 128), F32),
        normed=((R, D), BF16),
        proj=((R, 2 * N), F32),
        keep=((R, 128), F32),
        keep_next=((R, 128), F32),
        state=((R, 2 * N), F32),
        state_low=((R, 2 * N), BF16),
        act=((R, D), BF16),
        d_gelu=((R, D), F32),
        d_act=((R, D), F32),
        summed=((R, D), F32),
        d_mixed=((R, D), BF16),
        d_proj=((R, 2 * N), BF16),
        hidden=((R, units), BF16),
        d_unit=((R, 2 * units), BF16),
        seg_carry=((SEGMENTS, 2 * N), F32),
        sums=((16, D), F32),
        state_tp=((T, 8, 128), F32),
        state_seq=((S, 8, 128), F32),
        adj_tp=((T, 8, 128), F32),
        adj_seq=((S, 8, 128), F32),
    )
    in_rows = in_proj.transpose(0, 2, 1)
    if fused:
        unit_rows = D // S + units // S
        ins.update(
            decay_log=(decay_log.reshape(1, n), hbm),
            angle=(angle.reshape(1, n), hbm),
            in_proj=(in_rows.reshape(C, 2, 2 * n // S, D), hbm),
            out_proj=(out_proj.reshape(C, 2, 2 * n // S, D), hbm),
            glu_proj=(glu_proj.reshape(2, C, 2, D // S, units), hbm),
            down_proj=(down_proj.reshape(C, 2, units // S, D), hbm),
        )
        outs.update(
            grad_in=((C, 2, 2 * n // S, D), BF16, anywhere),
            grad_out=((C, 2, 2 * n // S, D), BF16, anywhere),
            grad_units=((C, 2, unit_rows, D), BF16, anywhere),
        )

        def whole(parts, rows, lead=()):
            return (lead + (parts, C, 2, rows, D), BF16)

        def halves(parts, rows, lead=()):
            return (lead + (parts, C, rows, D), BF16)

        def eighths(parts, rows, lead=()):
            return (lead + (C - 1, parts, rows, D), BF16)

        def own(parts, rows, lead=()):
            return (lead + (parts, rows, D), BF16)

        unit_sizes = (1, unit_rows, (T,))
        rate_sizes = (T, 2 * n // S)
        scratch.update(
            w_in=((2 * N, D), BF16),
            w_out=((2 * N, D), BF16),
            rates_all=((T, 8, 128), F32),
            decay_row=((1, n), F32),
            angle_row=((1, n), F32),
            in_slices=((T, C, 2, 2 * n // S, D), BF16),
            out_slices=((T, C, 2, 2 * n // S, D), BF16),
            unit_slices=((T, C, 2, unit_rows, D), BF16),
            grad_rates=((2 * N, D), BF16),
            small_tp=((T, 16, 128), F32),
            small_seq=((S, 16, 128), F32),
            unit_sums=((T - 1, 1, unit_rows, D), BF16),
            out_sums=((T - 1, 2 * n // S, D), BF16),
            in_sums=((T - 1, 2 * n // S, D), BF16),
            unit_sum=((1, C, 2, unit_rows, D), BF16),
            out_sum=((1, C, 2, 2 * n // S, D), BF16),
            in_sum=((1, C, 2, 2 * n // S, D), BF16),
            unit_full=whole(*unit_sizes),
            unit_halves=halves(*unit_sizes),
            unit_eighths=eighths(*unit_sizes),
            unit_summed=own(*unit_sizes),
            out_full=whole(*rate_sizes),
            out_halves=halves(*rate_sizes),
            out_eighths=eighths(*rate_sizes),
            out_summed=own(*rate_sizes),
            in_full=whole(*rate_sizes),
            in_halves=halves(*rate_sizes),
            in_eighths=eighths(*rate_sizes),
            in_summed=own(*rate_sizes),
        )
        links = 160
    else:
        w_in = lax.all_gather(in_rows, "tp", axis=1, tiled=True).reshape(2 * N, D)
        w_out = lax.all_gather(out_proj, "tp", axis=1, tiled=True).reshape(2 * N, D)
        glu = lax.all_gather(glu_proj, "tp")
        rates = jnp.stack(
            [lax.all_gather(part, "tp", tiled=True) for part in decay_terms(decay_log, angle)]
            + [jnp.zeros((N,), F32)] * 5
        )
        ins.update(
            rates=(rates, vmem),
            w_in=(w_in, vmem),
            w_out=(w_out, vmem),
            glu=(jnp.concatenate([glu[:, 0], glu[:, 1]], 2), vmem),
            down=(lax.all_gather(down_proj, "tp"), vmem),
        )
        outs.update(
            grad_in=((2 * N, D), BF16, vmem),
            grad_out=((2 * N, D), BF16, vmem),
            grad_glu=((T, D, 2 * units), BF16, vmem),
            grad_down=((T, units, D), BF16, vmem),
        )
        links = 2 * (T - 1 + S - 1)
    names = [*ins, *outs, *scratch, *dict(counts=0, local_sem=0, send_sem=0, recv_sem=0)]
    results = pl.pallas_call(
        functools.partial(layer_kernel, S, T, fused, names),
        out_shape=tuple(jax.ShapeDtypeStruct(shape, dtype) for shape, dtype, _ in outs.values()),
        in_specs=[spec for _, spec in ins.values()],
        out_specs=tuple(spec for _, _, spec in outs.values()),
        scratch_shapes=[pltpu.VMEM(shape, dtype) for shape, dtype in scratch.values()]
        + [
            pltpu.SMEM(lengths.shape, jnp.int32),
            pltpu.SemaphoreType.DMA((12,)),
            pltpu.SemaphoreType.DMA((links,)),
            pltpu.SemaphoreType.DMA((links,)),
        ],
        compiler_params=pltpu.CompilerParams(
            collective_id=0, has_side_effects=True, vmem_limit_bytes=46 * 2**20
        ),
    )(
        *[
            pltpu.with_memory_space_constraint(value, pltpu.HBM) if spec is hbm else value
            for value, spec in ins.values()
        ]
    )
    if fused:
        result, grad_tokens, small, grad_in, grad_out, grad_units = results
        ins = dict(
            result_in=(result, anywhere),
            grad_tokens_in=(grad_tokens, anywhere),
            small=(small, vmem),
            in_in=(grad_in, vmem),
            out_in=(grad_out, vmem),
            units_in=(grad_units, vmem),
            decay_log=(decay_log.reshape(1, n), vmem),
            angle=(angle.reshape(1, n), vmem),
        )
        outs = dict(
            result=((R, D), BF16, anywhere),
            grad_tokens=((R, D), F32, anywhere),
            gain=((1, D), F32, vmem),
            in_=((C, 2, 2 * n // S, D), F32, vmem),
            decay=((1, n), F32, vmem),
            turn=((1, n), F32, vmem),
            out=((C, 2, 2 * n // S, D), F32, vmem),
            skip=((1, D), F32, vmem),
            glu=((2, C, 2, D // S, units), F32, vmem),
            down=((C, 2, units // S, D), F32, vmem),
        )
        scratch = dict(result_rows=((R, D), BF16), grad_rows=((R, D), F32))
        names = [*ins, *outs, *scratch, *dict(local_sem=0)]
        result, grad_tokens, gain, in_, decay, turn, out, skip_sum, glu, down = pl.pallas_call(
            functools.partial(finish_kernel, T, names),
            out_shape=tuple(
                jax.ShapeDtypeStruct(shape, dtype) for shape, dtype, _ in outs.values()
            ),
            in_specs=[spec for _, spec in ins.values()],
            out_specs=tuple(spec for _, _, spec in outs.values()),
            scratch_shapes=[pltpu.VMEM(shape, dtype) for shape, dtype in scratch.values()]
            + [pltpu.SemaphoreType.DMA((3,))],
            compiler_params=pltpu.CompilerParams(vmem_limit_bytes=16 * 2**20),
        )(*[value for value, _ in ins.values()])
        return (
            result,
            grad_tokens,
            gain.reshape(D),
            in_.reshape(2, n, D).transpose(0, 2, 1),
            decay.reshape(n),
            turn.reshape(n),
            out.reshape(2, n, D),
            skip_sum.reshape(D),
            glu.reshape(2, D, units),
            down.reshape(units, D),
        )
    result, grad_tokens, small, grad_in, grad_out, grad_glu, grad_down = results
    small = lax.psum(small, ("seq", "tp"))

    def reduced(part):
        part = lax.psum_scatter(part, "tp", scatter_dimension=0, tiled=True)
        return lax.psum(part, "seq").astype(F32)

    def by_tp(grad):
        return reduced(grad.reshape(2, T, n, D).transpose(1, 0, 2, 3).reshape(T * 2, n, D))

    grad_glu = reduced(grad_glu)[0].reshape(D, 2, units).transpose(1, 0, 2)
    grad_down = reduced(grad_down)[0]

    def mine(row):
        return lax.dynamic_slice_in_dim(row, lax.axis_index("tp") * n, n)

    g_re, g_im, g_gamma = (mine(small[2, :N]), mine(small[2, N:]), mine(small[3, :N]))
    _, pull = jax.vjp(decay_terms, decay_log, angle)
    grad_decay, grad_angle = pull((g_re, g_im, g_gamma))
    return (
        result,
        grad_tokens,
        small[0],
        by_tp(grad_in).transpose(0, 2, 1),
        grad_decay,
        grad_angle,
        by_tp(grad_out),
        small[1],
        grad_glu,
        grad_down,
    )


def solution(mesh):
    in_specs = (
        P(("seq", "tp"), None),
        P(),
        P(None, None, "tp"),
        P("tp"),
        P("tp"),
        P(None, "tp", None),
        P(),
        P(None, None, "tp"),
        P("tp", None),
        P(),
        P(("seq", "tp"), None),
    )
    out_specs = (
        P(("seq", "tp"), None),
        P(("seq", "tp"), None),
        P(),
        P(None, None, "tp"),
        P("tp"),
        P("tp"),
        P(None, "tp", None),
        P(),
        P(None, None, "tp"),
        P("tp", None),
    )
    return jax.shard_map(
        functools.partial(local, mesh.shape["seq"], mesh.shape["tp"]),
        mesh=mesh,
        in_specs=in_specs,
        out_specs=out_specs,
        check_vma=False,
    )
```

```python
import functools
import types
import jax
import jax.numpy as jnp
from jax import lax
from jax.experimental import pallas as pl
from jax.experimental.pallas import tpu as pltpu
from jax.sharding import PartitionSpec as P

epsilon = 1e-05
MESH = pl.DeviceIdType.MESH
F32 = jnp.float32
BF16 = jnp.bfloat16
GROUPS = 2
SEGMENTS = 8 * GROUPS
BLOCK = SEGMENTS * SEGMENTS


def dot(left, right):
    return jnp.dot(left, right, preferred_element_type=F32)


def dot_nt(left, right):
    return lax.dot_general(left, right, (((1,), (1,)), ((), ())), preferred_element_type=F32)


def complex_mul(left_re, left_im, right_re, right_im):
    return (left_re * right_re - left_im * right_im, left_re * right_im + left_im * right_re)


def dot_tn(left, right):
    return lax.dot_general(left, right, (((0,), (0,)), ((), ())), preferred_element_type=F32)


def power(base, exponent):
    result = None
    square = base
    while exponent:
        if exponent & 1:
            result = square if result is None else complex_mul(*result, *square)
        exponent >>= 1
        if exponent:
            square = complex_mul(*square, *square)
    return result


class Links:
    def __init__(self, send_sem, recv_sem):
        self.send_sem = send_sem
        self.recv_sem = recv_sem
        self.started = []

    def send(self, source, target, device):
        index = len(self.started)
        copy = pltpu.make_async_remote_copy(
            src_ref=source,
            dst_ref=target,
            send_sem=self.send_sem.at[index],
            recv_sem=self.recv_sem.at[index],
            device_id=device,
            device_id_type=MESH,
        )
        copy.start()
        self.started.append(copy)
        return copy

    def close(self):
        for copy in self.started:
            copy.wait_send()


def arrive(copies):
    for copy in copies:
        copy.wait_recv()


class Gather:
    def __init__(self, place, buffer, first, last):
        self.place = place
        self.buffer = buffer
        self.slots = range(first, last)
        self.part = buffer.at[pl.ds(first, last - first)]

    def over_tp(self):
        p = self.place
        self.copies = [
            p.links.send(
                self.buffer.at[0, p.chip, p.core],
                self.buffer.at[slot, p.chip, p.core],
                (p.s, lax.rem(p.t + p.T - slot, p.T)),
            )
            for slot in self.slots
        ]

    def over_plane(self):
        p = self.place
        arrive(self.copies)
        mine = self.part.at[:, p.chip, p.core]
        self.copies = [p.links.send(mine, mine, device) for _, device in p.chips]

    def over_cores(self):
        p = self.place
        arrive(self.copies)
        mine = self.part.at[:, :, p.core]
        self.copies = [p.links.send(mine, mine, p.sibling)]

    def finish(self):
        arrive(self.copies)


class Reduce:
    def __init__(self, place, full, halves, eighths, summed):
        self.place = place
        self.full = full
        self.halves = halves
        self.eighths = eighths
        self.summed = summed

    def over_cores(self):
        p = self.place
        self.copies = [
            p.links.send(self.full.at[:, :, 1 - p.core], self.halves, p.sibling)
        ]

    def over_plane(self):
        p = self.place
        arrive(self.copies)
        parts, chips = self.halves.shape[:2]

        @pl.loop(0, parts * chips)
        def _(index):
            part, chip = (lax.div(index, chips), lax.rem(index, chips))
            self.halves[part, chip] = (
                self.full[part, chip, p.core].astype(F32) + self.halves[part, chip].astype(F32)
            ).astype(BF16)

        self.copies = [
            p.links.send(self.halves.at[:, chip], self.eighths.at[k], device)
            for k, (chip, device) in enumerate(p.chips)
        ]

    def sum_plane(self):
        p = self.place
        arrive(self.copies)

        @pl.loop(0, self.halves.shape[0])
        def _(part):
            total = self.halves[part, p.chip].astype(F32)
            for k in range(len(p.chips)):
                total = total + self.eighths[k, part].astype(F32)
            self.summed[part] = total.astype(BF16)


class Reduce2(Reduce):
    def __init__(self, place, full, halves, eighths, summed):
        super().__init__(place, full, halves, eighths, summed)
        self.rows = halves.shape[2] // 2
        self.ours = halves.at[:, :, pl.ds(0, self.rows)]
        self.theirs = halves.at[:, :, pl.ds(self.rows, self.rows)]

    def sum_cores(self, chip):
        self.halves[0, chip] = (
            self.full[0, chip, self.place.core].astype(F32) + self.halves[0, chip].astype(F32)
        ).astype(BF16)

    def over_plane(self):
        p = self.place
        arrive(self.copies)
        self.sum_cores(p.by_x)
        self.sum_cores(p.by_y)
        self.sum_cores(p.by_xy)
        self.copies = [
            p.links.send(part.at[0, chip], self.eighths.at[index, 0, rows], device)
            for index, part, chip, rows, device in (
                (0, self.ours, p.by_x, pl.ds(0, self.rows), p.x_device),
                (1, self.ours, p.by_xy, pl.ds(0, self.rows), p.x_device),
                (0, self.theirs, p.by_y, pl.ds(self.rows, self.rows), p.y_device),
                (1, self.theirs, p.by_xy, pl.ds(self.rows, self.rows), p.y_device),
            )
        ]
        self.sum_cores(p.chip)

    def turn_plane(self):
        p = self.place
        arrive(self.copies)
        n = self.rows
        for index, chip in ((0, p.chip), (1, p.by_y)):
            self.halves[0, chip, 0:n] = (
                self.halves[0, chip, 0:n].astype(F32) + self.eighths[index, 0, 0:n].astype(F32)
            ).astype(BF16)
        for index, chip in ((0, p.chip), (1, p.by_x)):
            self.halves[0, chip, n:] = (
                self.halves[0, chip, n:].astype(F32) + self.eighths[index, 0, n:].astype(F32)
            ).astype(BF16)
        self.copies = [
            p.links.send(self.ours.at[0, p.by_y], self.eighths.at[2, 0, pl.ds(0, n)], p.y_device),
            p.links.send(self.theirs.at[0, p.by_x], self.eighths.at[2, 0, pl.ds(n, n)], p.x_device),
        ]

    def sum_plane(self):
        p = self.place
        arrive(self.copies)
        self.summed[0] = (
            self.halves[0, p.chip].astype(F32) + self.eighths[2, 0].astype(F32)
        ).astype(BF16)


class Spread:
    def __init__(self, place, buffer):
        self.place = place
        self.buffer = buffer

    def over_plane(self):
        p = self.place
        mine = self.buffer.at[:, p.chip, p.core]
        self.copies = [p.links.send(mine, mine, device) for _, device in p.chips]

    def over_cores(self):
        p = self.place
        arrive(self.copies)
        mine = self.buffer.at[:, :, p.core]
        self.copies = [p.links.send(mine, mine, p.sibling)]

    def finish(self):
        arrive(self.copies)


class Place:
    def __init__(self, S, T, links):
        self.S, self.T, self.links = (S, T, links)
        self.s = lax.axis_index("seq")
        self.t = lax.axis_index("tp")
        C = S // 2
        self.core = lax.rem(self.s, 2)
        self.chip = lax.div(self.s, 2)
        self.sibling = (self.chip * 2 + 1 - self.core, self.t)
        x = lax.rem(self.chip, 2)
        y = lax.div(self.chip, 2)
        self.by_x = y * 2 + 1 - x
        self.by_y = (1 - y) * 2 + x
        self.by_xy = (1 - y) * 2 + 1 - x
        self.x_device = (self.by_x * 2 + self.core, self.t)
        self.y_device = (self.by_y * 2 + self.core, self.t)
        self.chips = []
        for k in range(1, C):
            chip = lax.rem(self.chip + k, C)
            self.chips.append((chip, (chip * 2 + self.core, self.t)))


def layer_kernel(S, T, fused, names, *refs):
    r = types.SimpleNamespace(**dict(zip(names, refs)))
    links = Links(r.send_sem, r.recv_sem)
    place = Place(S, T, links)
    lengths = r.counts
    tokens = r.tokens_raw
    cot = r.cot_raw
    result = r.tokens_raw
    grad_tokens = r.d_gelu
    turn = r.turn
    tokens_in = r.tokens_in
    cot_in = r.cot_in
    centred = r.centred
    inv_std = r.inv_std
    normed = r.normed
    proj = r.proj
    keep = r.keep
    keep_next = r.keep_next
    state = r.state
    state_low = r.state_low
    act = r.act
    d_gelu = r.d_gelu
    d_act = r.d_act
    summed = r.summed
    d_mixed = r.d_mixed
    adjoint = r.summed
    d_proj = r.d_proj
    hidden = r.hidden
    d_unit = r.d_unit
    seg_carry, sums = (r.seg_carry, r.sums)
    w_in, w_out = (r.w_in, r.w_out)
    R, D = tokens.shape
    N = w_in.shape[0] // 2
    n = N // T
    L = R // SEGMENTS
    s = place.s
    t = place.t
    first = (s * T + t) * R

    peers_tp = [lax.rem(t + k, T) for k in range(1, T)]
    peers_seq = [lax.rem(s + k, S) for k in range(1, S)]
    barrier = pltpu.get_barrier_semaphore()
    for peer in peers_tp:
        pl.semaphore_signal(barrier, inc=1, device_id=(s, peer), device_id_type=MESH)
    for peer in peers_seq:
        pl.semaphore_signal(barrier, inc=1, device_id=(peer, t), device_id_type=MESH)

    fetched = [
        pltpu.make_async_copy(source, target, r.local_sem.at[index])
        for index, (source, target) in enumerate(
            ((r.tokens, tokens), (r.cot, cot), (r.gain, r.gain_row), (r.skip, r.skip_row), (r.lengths, r.counts))
        )
    ]
    if fused:
        in_slices, out_slices, unit_slices = (r.in_slices, r.out_slices, r.unit_slices)
        units = r.down_proj.shape[2] * S
        D_rows = r.glu_proj.shape[3]
        gated_rows = unit_slices.at[0, :, :, pl.ds(0, D_rows)]
        weights = [
            pltpu.make_async_copy(source, target, r.local_sem.at[5 + index])
            for index, (source, target) in enumerate(
                (
                    (r.decay_log, r.decay_row),
                    (r.angle, r.angle_row),
                    (r.in_proj, in_slices.at[0]),
                    (r.out_proj, out_slices.at[0]),
                    (r.glu_proj.at[0], gated_rows.at[:, :, :, pl.ds(0, units)]),
                    (r.glu_proj.at[1], gated_rows.at[:, :, :, pl.ds(units, units)]),
                    (r.down_proj, unit_slices.at[0, :, :, pl.ds(D_rows, units // S)]),
                )
            )
        ]
        for copy in weights:
            copy.start()
    for copy in fetched:
        copy.start()
    if fused:
        rates_all = r.rates_all
        rates_all[t] = jnp.zeros(rates_all.shape[1:], F32)
        gather_in = Gather(place, in_slices, 1, T)
        gather_out = Gather(place, out_slices, 1, T)
        gather_units = [Gather(place, unit_slices, slot, slot + 1) for slot in range(1, T)]
        for copy in weights:
            copy.wait()
        for index, row in enumerate(decay_terms(r.decay_row[...], r.angle_row[...])):
            rates_all[t, index : index + 1, 0:n] = row
        pl.semaphore_wait(barrier, T - 1 + S - 1)
        gather_in.over_tp()
        rate_copies = [
            links.send(rates_all.at[t], rates_all.at[t], (s, peer)) for peer in peers_tp
        ]

    for copy in fetched[2:]:
        copy.wait()
    starts = []
    total = jnp.int32(0)
    for index in range(lengths.shape[0]):
        starts.append(total)
        total = total + lengths[index]

    def keeps(position):
        hit = position == starts[0]
        for start in starts[1:]:
            hit = hit | (position == start)
        return jnp.where(hit, 0.0, 1.0)

    def clear(low, high):
        hit = (starts[0] >= low) & (starts[0] < high)
        for start in starts[1:]:
            hit = hit | ((start >= low) & (start < high))
        return jnp.where(hit, 0.0, 1.0)

    gain_row = r.gain_row[...]
    skip_row = r.skip_row[...].astype(F32).reshape(1, D)

    down_index = lax.broadcasted_iota(jnp.int32, (BLOCK, BLOCK), 0)
    across_index = lax.broadcasted_iota(jnp.int32, (BLOCK, BLOCK), 1)
    turned = lax.rem(down_index, SEGMENTS) * SEGMENTS + lax.div(down_index, SEGMENTS)
    turn[...] = jnp.where(turned == across_index, 1.0, 0.0).astype(BF16)

    def pieces(block):
        return [
            pl.ds(pl.multiple_of(run * L + block * SEGMENTS, SEGMENTS), SEGMENTS)
            for run in range(SEGMENTS)
        ]

    def taken(ref, block):
        return dot(turn[...], jnp.concatenate([ref[piece, :] for piece in pieces(block)], 0))

    def block_rows(tile):
        return pl.ds(pl.multiple_of(tile * BLOCK, BLOCK), BLOCK)

    def norm_tile(tile):
        rows = block_rows(tile)
        x = taken(tokens, tile)
        tokens_in[rows, :] = x.astype(BF16)
        mean = jnp.mean(x, 1, keepdims=True)
        inv = lax.rsqrt(jnp.mean(x * x, 1, keepdims=True) - mean * mean + epsilon)
        c = (x - mean) * inv
        centred[rows, :] = c
        inv_std[rows, :] = jnp.broadcast_to(inv, (BLOCK, 128))
        n_rows = (c * gain_row).astype(BF16)
        normed[rows, :] = n_rows

    def cot_tile(tile):
        rows = block_rows(tile)
        cot_rows = taken(cot, tile).astype(BF16)
        cot_in[rows, :] = cot_rows
        index = tile * BLOCK + lax.broadcasted_iota(jnp.int32, (BLOCK, 128), 0)
        position = first + lax.rem(index, SEGMENTS) * L + lax.div(index, SEGMENTS)
        keep[rows, :] = keeps(position)
        keep_next[rows, :] = keeps(position + 1)

    fetched[0].wait()
    pl.loop(0, R // BLOCK)(norm_tile)
    if fused:
        gather_in.over_plane()
        gather_out.over_tp()
        gather_units[0].over_tp()
    fetched[1].wait()
    pl.loop(0, R // BLOCK)(cot_tile)

    def assemble(slices, weight):
        for i in range(T):
            at = lax.rem(t + i, T) * n
            for part in range(2):
                weight[pl.ds(pl.multiple_of(part * N + at, n), n), :] = slices[
                    i, part * (S // 4) : (part + 1) * (S // 4)
                ].reshape(n, D)

    if fused:
        gather_in.over_cores()
        gather_units[1].over_tp()
        arrive(rate_copies)
        half = lax.broadcasted_iota(jnp.int32, (8, 128), 1) < n
        rate_rows = [rates_all[z] for z in range(T)]
        joined = jnp.concatenate(
            [
                jnp.where(half, rate_rows[z], pltpu.roll(rate_rows[z + 1], n, 1))
                for z in range(0, T, 2)
            ],
            1,
        )
        lam_re, lam_im, gamma = (joined[k : k + 1] for k in range(3))
        gather_in.finish()
        for gather in gather_units[2:]:
            gather.over_tp()
        gather_out.over_plane()
        assemble(in_slices, w_in)
    else:
        pl.semaphore_wait(barrier, T - 1 + S - 1)
        lam_re, lam_im, gamma = (r.rates[k : k + 1, :] for k in range(3))
    gamma_signed = jnp.concatenate([gamma, -gamma], 1)

    @pl.loop(0, R // BLOCK)
    def _(tile):
        rows = block_rows(tile)
        proj[rows, :] = dot_nt(normed[rows, :], w_in[...]) * gamma_signed

    low8_re = jnp.broadcast_to(lam_re, (8, N))
    low8_im = jnp.broadcast_to(lam_im, (8, N))

    def rows_of(group, step):
        return pl.ds(pl.multiple_of(step * SEGMENTS + group * 8, 8), 8)

    def spread(row):
        return jnp.concatenate([row] * (N // 128), 1)

    def scan_step(values, mask, add, sign):
        new_re, new_im = complex_mul(low8_re, sign * low8_im, *(value * mask for value in values))
        return (new_re + add[:, :N], new_im + add[:, N:])

    zero8 = jnp.zeros((8, N), F32)
    none = tuple((zero8, zero8) for _ in range(GROUPS))

    def forward_step(step, carry):
        return tuple(
            scan_step(
                carry[group],
                spread(keep[rows_of(group, step), :]),
                proj[rows_of(group, step), :],
                -1.0,
            )
            for group in range(GROUPS)
        )

    def segment_rows(finals):
        return [
            (finals[group][0][sub : sub + 1], finals[group][1][sub : sub + 1])
            for group in range(GROUPS)
            for sub in range(8)
        ]

    def fold(start, factor, items, masks, taken):
        before = []
        carry = start
        for (item_re, item_im), mask, take in zip(items, masks, taken):
            before.append(carry)
            moved = complex_mul(*factor, *carry)
            longer = (moved[0] * mask + item_re, moved[1] * mask + item_im)
            if take is None:
                carry = longer
            else:
                carry = tuple(jnp.where(take, new, old) for new, old in zip(longer, carry))
        return carry, before

    zero1 = (jnp.zeros((1, N), F32), jnp.zeros((1, N), F32))
    lam = (lam_re, lam_im)
    conj = (lam_re, -lam_im)

    def unpack(row):
        return (row[:, :N], row[:, N:])

    def packed(row, height):
        parts = [row[:, at : at + 128] for at in range(0, row.shape[1], 128)]
        return jnp.concatenate(parts + [parts[0]] * (height - len(parts)), 0)

    def unpacked(tile, height):
        return jnp.concatenate([tile[k : k + 1, :] for k in range(height)], 1)

    class Exchange:
        def __init__(self, own, factor, buffer, forward):
            self.forward = forward
            self.shift = 0 if forward else 1
            self.factor = power(factor, R)
            self.buffer = buffer
            buffer[t, s] = packed(jnp.concatenate(own, 1), 2 * N // 128)
            mine = buffer.at[t, s]
            self.copies = [links.send(mine, mine, (s, peer)) for peer in peers_tp]
            self.copies += [links.send(mine, mine, (peer, t)) for peer in peers_seq]
            self.copies += [
                links.send(mine, mine, (peer, peer_tp))
                for peer_tp in peers_tp
                for peer in peers_seq
            ]

        def carry(self):
            arrive(self.copies)

            def order(count):
                return list(range(count)) if self.forward else list(range(count))[::-1]

            def ahead(block, z):
                mine, other = (s * T + t, block * T + z)
                return other < mine if self.forward else other > mine

            rows = [
                jnp.concatenate(
                    [unpacked(self.buffer[z, block], 2 * N // 128) for block in range(S)], 0
                )
                for z in range(T)
            ]
            block = lax.broadcasted_iota(jnp.int32, (S, N), 0)
            carry = (jnp.zeros((S, N), F32), jnp.zeros((S, N), F32))
            for z in order(T):
                low = (block * T + z) * R + self.shift
                mask = clear(low, low + R)
                item = (rows[z][:, :N], rows[z][:, N:])
                moved = complex_mul(*self.factor, *carry)
                longer = (moved[0] * mask + item[0], moved[1] * mask + item[1])
                mine = block == s
                taken = jnp.logical_or(jnp.logical_not(mine), ahead(s, z))
                carry = tuple(jnp.where(taken, new, old) for new, old in zip(longer, carry))
            result = zero1
            whole = power(self.factor, T)
            for b in order(S):
                low = b * T * R + self.shift
                mask = clear(low, low + T * R)
                moved = complex_mul(*whole, *result)
                longer = (
                    moved[0] * mask + carry[0][b : b + 1],
                    moved[1] * mask + carry[1][b : b + 1],
                )
                earlier = b < s if self.forward else b > s
                result = tuple(jnp.where(earlier, new, old) for new, old in zip(longer, result))
            inside = tuple(
                jnp.sum(jnp.where(block == s, part, 0.0), 0, keepdims=True) for part in carry
            )
            for z in order(T):
                low = (s * T + z) * R + self.shift
                mask = clear(low, low + R)
                moved = complex_mul(*self.factor, *result)
                longer = (moved[0] * mask, moved[1] * mask)
                result = tuple(
                    jnp.where(ahead(s, z), new, old) for new, old in zip(longer, result)
                )
            return (result[0] + inside[0], result[1] + inside[1])

    finals = segment_rows(lax.fori_loop(0, L, forward_step, none))
    seg_masks = [clear(first + index * L, first + (index + 1) * L) for index in range(SEGMENTS)]
    factor_seg = power(conj, L)
    own, _ = fold(zero1, factor_seg, finals, seg_masks, [None] * SEGMENTS)
    exchange = Exchange(own, conj, r.state_all, True)
    if fused:
        gather_units[0].over_plane()
        gather_out.over_cores()
    if fused:
        gather_units[1].over_plane()
        gather_out.finish()
        assemble(out_slices, w_out)
    carry = exchange.carry()
    _, entering = fold(carry, factor_seg, finals, seg_masks, [None] * SEGMENTS)
    for index, (row_re, row_im) in enumerate(entering):
        seg_carry[index : index + 1, :] = jnp.concatenate([row_re, row_im], 1)

    def write_state(step, carry):
        new = forward_step(step, carry)
        for group in range(GROUPS):
            state[rows_of(group, step), :] = jnp.concatenate(new[group], 1)
        return new

    def entering_groups():
        return tuple(
            unpack(seg_carry[group * 8 : group * 8 + 8, :]) for group in range(GROUPS)
        )

    lax.fori_loop(0, L, write_state, entering_groups())
    if fused:
        for gather in gather_units[2:]:
            gather.over_plane()

    @pl.loop(0, R // BLOCK)
    def _(tile):
        rows = block_rows(tile)
        low = state[rows, :].astype(BF16)
        state_low[rows, :] = low
        x = dot(low, w_out[...]) + skip_row * normed[rows, :].astype(F32)
        scale = 0.7978845608028654
        th = jnp.tanh(scale * (x + 0.044715 * x * x * x))
        half = 0.5 * (1.0 + th)
        a = (x * half).astype(BF16)
        act[rows, :] = a
        d_gelu[rows, :] = half + 0.5 * x * (1.0 - th * th) * scale * (1.0 + 0.134145 * x * x)

    if fused:
        reduces = [
            Reduce2(
                place,
                r.unit_full.at[i],
                r.unit_halves.at[i],
                r.unit_eighths.at[i],
                r.unit_summed.at[i],
            )
            for i in range(T)
        ]

    UNIT_ROWS = min(512, R)
    units = hidden.shape[1]
    unit_copies = []

    def unit_grads(i):
        c = lax.rem(t + i, T)
        gated_grad = dot_tn(act[...], d_unit[...]).astype(BF16)
        down_grad = dot_tn(hidden[...], cot_in[...]).astype(BF16)
        if fused:
            full = r.unit_full
            full[i, 0, :, :, 0:D_rows] = gated_grad.reshape(S // 2, 2, D_rows, 2 * units)
            full[i, 0, :, :, D_rows:] = down_grad.reshape(S // 2, 2, units // S, D)
            reduces[i].over_cores()
        else:
            r.grad_glu[c] = gated_grad
            r.grad_down[c] = down_grad

    def unit_sums(i):
        reduces[i].sum_plane()
        if i > 0:
            unit_copies.append(
                links.send(r.unit_summed.at[i], r.unit_sums.at[i - 1], (s, lax.rem(t + i, T)))
            )

    for i in range(T):
        c = lax.rem(t + i, T)
        if fused:
            if i > 0:
                gather_units[i - 1].finish()
            if i < T - 1:
                gather_units[i].over_cores()
            w_gated = unit_slices[i, :, :, 0:D_rows].reshape(D, 2 * units)
            w_down = unit_slices[i, :, :, D_rows:].reshape(units, D)
        else:
            w_gated = r.glu[c]
            w_down = r.down[c]

        for tile in range(R // UNIT_ROWS):
            rows = slice(tile * UNIT_ROWS, (tile + 1) * UNIT_ROWS)
            both = dot(act[rows, :], w_gated)
            value, gate = (both[:, :units], both[:, units:])
            sigma = 0.5 * jnp.tanh(0.5 * gate) + 0.5
            gated = value * sigma
            h = gated.astype(BF16)
            hidden[rows, :] = h
            d_h = dot_nt(cot_in[rows, :], w_down)
            d_both = jnp.concatenate(
                [(d_h * sigma).astype(BF16), (d_h * gated * (1.0 - sigma)).astype(BF16)], 1
            )
            d_unit[rows, :] = d_both
            added = dot(h, w_down)
            d_a = dot_nt(d_both, w_gated)
            if i > 0:
                added = added + summed[rows, :]
                d_a = d_a + d_act[rows, :]
            if i < T - 1:
                summed[rows, :] = added
                d_act[rows, :] = d_a
            else:
                d_m = (d_gelu[rows, :] * d_a).astype(BF16)
                d_mixed[rows, :] = d_m
                adjoint[rows, :] = dot_nt(d_m, w_out[...])
                out = (tokens_in[rows, :].astype(F32) + added).astype(BF16)
                for block in range(UNIT_ROWS // BLOCK):
                    turned = dot(turn[...], out[block * BLOCK : block * BLOCK + BLOCK])
                    turned = turned.astype(BF16)
                    for run, piece in enumerate(pieces(tile * (UNIT_ROWS // BLOCK) + block)):
                        result[piece, :] = turned[run * SEGMENTS : run * SEGMENTS + SEGMENTS]

        if fused and i > 0:
            reduces[i - 1].over_plane()
        unit_grads(i)
        if fused and i > 1:
            reduces[i - 2].turn_plane()
        if fused and i > 2:
            unit_sums(i - 3)

    result_copy = pltpu.make_async_copy(result, r.result, r.local_sem.at[0])
    result_copy.start()

    def backward_step(index, carry):
        step = L - 1 - index
        return tuple(
            scan_step(
                carry[group],
                spread(keep_next[rows_of(group, step), :]),
                adjoint[rows_of(group, step), :],
                1.0,
            )
            for group in range(GROUPS)
        )

    finals = segment_rows(lax.fori_loop(0, L, backward_step, none))[::-1]
    seg_masks = [
        clear(first + index * L + 1, first + (index + 1) * L + 1) for index in range(SEGMENTS)
    ][::-1]
    factor_seg = power(lam, L)
    own, _ = fold(zero1, factor_seg, finals, seg_masks, [None] * SEGMENTS)
    exchange = Exchange(own, lam, r.adj_all, False)
    if fused:
        reduces[T - 2].turn_plane()
        reduces[T - 1].over_plane()
    grad_out = dot_tn(state_low[...], d_mixed[...]).astype(BF16)

    def divide(grad, full):
        for i in range(T):
            at = lax.rem(t + i, T) * n
            for part in range(2):
                rows = pl.ds(pl.multiple_of(part * N + at, n), n)
                full[i, part * (S // 4) : (part + 1) * (S // 4)] = grad[rows, :].reshape(
                    S // 4, 2, -1, D
                )

    if fused:
        r.grad_rates[...] = grad_out
        divide(r.grad_rates, r.out_full)
        out_reduce = Reduce(place, r.out_full, r.out_halves, r.out_eighths, r.out_summed)
        out_reduce.over_cores()
        unit_sums(T - 3)
    else:
        r.grad_out[...] = grad_out
    carry = exchange.carry()
    _, entering = fold(carry, factor_seg, finals, seg_masks, [None] * SEGMENTS)
    entering = entering[::-1]
    groups = tuple(
        tuple(
            jnp.concatenate([entering[group * 8 + sub][part] for sub in range(8)], 0)
            for part in range(2)
        )
        for group in range(GROUPS)
    )
    sums[...] = jnp.zeros_like(sums)

    def adjoint_step(step, carry, previous):
        new = []
        add_re = zero8
        add_im = zero8
        add_gamma = zero8
        for group in range(GROUPS):
            rows = rows_of(group, step)
            b = scan_step(carry[group], spread(keep_next[rows, :]), adjoint[rows, :], 1.0)
            new.append(b)
            adjoint[rows, :] = jnp.concatenate(b, 1)
            u = unpack(proj[rows, :])
            v = previous(group, step)
            mask = spread(keep[rows, :])
            add_re = add_re + mask * (b[0] * v[0] + b[1] * v[1])
            add_im = add_im + mask * (b[0] * v[1] - b[1] * v[0])
            add_gamma = add_gamma + b[0] * u[0] + b[1] * u[1]
        return tuple(new), (add_re, add_im, add_gamma)

    def adjoint_body(index, carry):
        values, totals = carry
        values, added = adjoint_step(
            L - 1 - index, values, lambda group, step: unpack(state[rows_of(group, step - 1), :])
        )
        return values, tuple(total + add for total, add in zip(totals, added))

    values, totals = lax.fori_loop(0, L - 1, adjoint_body, (groups, (zero8, zero8, zero8)))
    inside = entering_groups()
    _, added = adjoint_step(0, values, lambda group, step: inside[group])
    totals = [jnp.sum(total + add, 0, keepdims=True) for total, add in zip(totals, added)]

    if fused:
        out_reduce.over_plane()
    d_proj[...] = (adjoint[...] * gamma_signed).astype(BF16)
    grad_in = dot_tn(d_proj[...], normed[...]).astype(BF16)
    if fused:
        r.grad_rates[...] = grad_in
        divide(r.grad_rates, r.in_full)
        in_reduce = Reduce(place, r.in_full, r.in_halves, r.in_eighths, r.in_summed)
        in_reduce.over_cores()
        reduces[T - 1].turn_plane()
        unit_sums(T - 2)
        out_reduce.sum_plane()
        out_copies = [
            links.send(r.out_summed.at[i], r.out_sums.at[i - 1], (s, lax.rem(t + i, T)))
            for i in range(1, T)
        ]
        in_reduce.over_plane()
        unit_sums(T - 1)
    else:
        r.grad_in[...] = grad_in

    @pl.loop(0, R // BLOCK)
    def _(tile):
        rows = block_rows(tile)
        d_m = d_mixed[rows, :].astype(F32)
        d_n = dot(d_proj[rows, :], w_in[...]) + d_m * skip_row
        c = centred[rows, :]
        sums[0:8, :] += jnp.sum((d_n * c).reshape(BLOCK // 8, 8, D), 0)
        sums[8:16, :] += jnp.sum((d_m * normed[rows, :].astype(F32)).reshape(BLOCK // 8, 8, D), 0)
        d_c = d_n * gain_row
        mean = jnp.mean(d_c, 1, keepdims=True)
        cross = jnp.mean(d_c * c, 1, keepdims=True)
        inv = inv_std[rows, 0:1]
        out = cot_in[rows, :].astype(F32) + inv * (d_c - mean - c * cross)
        high = out.astype(BF16)
        out = dot(turn[...], high) + dot(turn[...], (out - high.astype(F32)).astype(BF16))
        for run, piece in enumerate(pieces(tile)):
            grad_tokens[piece, :] = out[run * SEGMENTS : run * SEGMENTS + SEGMENTS]

    grad_copy = pltpu.make_async_copy(grad_tokens, r.grad_tokens, r.local_sem.at[1])
    grad_copy.start()
    small = r.small
    small_rows = [
        jnp.sum(sums[0:8, :], 0, keepdims=True),
        jnp.sum(sums[8:16, :], 0, keepdims=True),
        jnp.concatenate(totals[:2], 1),
        jnp.concatenate([totals[2] / gamma, jnp.zeros_like(gamma)], 1),
    ]
    if not fused:
        for k, row in enumerate(small_rows):
            small[k : k + 1, :] = row
        small[4:8, :] = jnp.zeros((4, D), F32)
        links.close()
        result_copy.wait()
        grad_copy.wait()
        return

    small_tp, small_seq = (r.small_tp, r.small_seq)
    small_tp[t] = jnp.concatenate([packed(row, D // 128) for row in small_rows], 0)
    small_copies = [links.send(small_tp.at[t], small_tp.at[t], (s, peer)) for peer in peers_tp]

    def total_of(own, buffer):
        total = own.astype(F32)
        for k in range(buffer.shape[0]):
            total = total + buffer[k].astype(F32)
        return total.astype(BF16)

    unit_sum, out_sum, in_sum = (r.unit_sum, r.out_sum, r.in_sum)
    arrive(unit_copies)
    unit_sum[0, place.chip, place.core] = total_of(r.unit_summed[0, 0], r.unit_sums.at[:, 0])
    unit_spread = Spread(place, unit_sum)
    unit_spread.over_plane()

    in_reduce.sum_plane()
    in_copies = [
        links.send(r.in_summed.at[i], r.in_sums.at[i - 1], (s, lax.rem(t + i, T)))
        for i in range(1, T)
    ]
    arrive(out_copies)
    out_sum[0, place.chip, place.core] = total_of(r.out_summed[0], r.out_sums)
    out_spread = Spread(place, out_sum)
    out_spread.over_plane()

    arrive(small_copies)
    part = small_tp[0]
    for z in range(1, T):
        part = part + small_tp[z]
    small_seq[s] = part
    small_copies = [links.send(small_seq.at[s], small_seq.at[s], (peer, t)) for peer in peers_seq]

    unit_spread.over_cores()
    arrive(in_copies)
    in_sum[0, place.chip, place.core] = total_of(r.in_summed[0], r.in_sums)
    in_spread = Spread(place, in_sum)
    in_spread.over_plane()
    out_spread.over_cores()

    unit_spread.finish()
    unit_copy = pltpu.make_async_copy(unit_sum.at[0], r.grad_units, r.local_sem.at[2])
    unit_copy.start()

    arrive(small_copies)
    part = small_seq[0]
    for block in range(1, S):
        part = part + small_seq[block]
    for k in range(4):
        height = D // 128
        small[k : k + 1, :] = unpacked(part[k * height : (k + 1) * height], height)
    small[4:8, :] = jnp.zeros((4, D), F32)

    out_spread.finish()
    out_copy = pltpu.make_async_copy(out_sum.at[0], r.grad_out, r.local_sem.at[3])
    out_copy.start()
    in_spread.over_cores()
    in_spread.finish()
    in_copy = pltpu.make_async_copy(in_sum.at[0], r.grad_in, r.local_sem.at[4])
    in_copy.start()
    for copy in (result_copy, grad_copy, unit_copy, out_copy, in_copy):
        copy.wait()
    links.close()


def finish_kernel(T, names, *refs):
    r = types.SimpleNamespace(**dict(zip(names, refs)))
    half = r.grad_rows.shape[0] // 2
    arrays = [(r.result_in, r.result_rows, r.result)] + [
        tuple(ref.at[pl.ds(at, half)] for ref in (r.grad_tokens_in, r.grad_rows, r.grad_tokens))
        for at in (0, half)
    ]
    fetched = [
        pltpu.make_async_copy(source, kept, r.local_sem.at[index])
        for index, (source, kept, _) in enumerate(arrays)
    ]
    copies = [
        pltpu.make_async_copy(kept, target, r.local_sem.at[index])
        for index, (_, kept, target) in enumerate(arrays)
    ]
    for copy in fetched:
        copy.start()
    for fetch, copy in zip(fetched, copies):
        fetch.wait()
        copy.start()
    D_rows, lanes = (r.glu.shape[3], r.glu.shape[4])
    r.glu[0] = r.units_in[:, :, 0:D_rows, :lanes].astype(F32)
    r.glu[1] = r.units_in[:, :, 0:D_rows, lanes:].astype(F32)
    r.down[...] = r.units_in[:, :, D_rows:, :].astype(F32)
    r.out[...] = r.out_in[...].astype(F32)
    r.in_[...] = r.in_in[...].astype(F32)
    r.gain[...] = r.small[0:1, :]
    r.skip[...] = r.small[1:2, :]
    n = r.decay_log.shape[1]
    N = T * n
    t = lax.axis_index("tp")

    def mine(row, first):
        own = row[:, first : first + n]
        for z in range(1, T):
            own = jnp.where(t == z, row[:, first + z * n : first + z * n + n], own)
        return own

    lam_re, lam_im, gamma = decay_terms(r.decay_log[...], r.angle[...])
    g_re = mine(r.small[2:3, :], 0)
    g_im = mine(r.small[2:3, :], N)
    g_gamma = mine(r.small[3:4, :], 0)
    rate_step = jnp.exp(r.decay_log[...])
    r.decay[...] = rate_step * (
        g_gamma * (1.0 - fall(2.0 * rate_step)) / gamma - g_re * lam_re - g_im * lam_im
    )
    r.turn[...] = g_im * lam_re - g_re * lam_im
    for copy in copies:
        copy.wait()


def fall(value):
    series = jnp.ones_like(value)
    for order in range(12, 1, -1):
        series = 1.0 - value / order * series
    return jnp.where(value < 0.5, value * series, 1.0 - jnp.exp(-value))


def decay_terms(decay_log, angle):
    rate_step = jnp.exp(decay_log)
    radius = 1.0 - fall(rate_step)
    return (radius * jnp.cos(angle), radius * jnp.sin(angle), jnp.sqrt(fall(2.0 * rate_step)))


def local(
    S,
    T,
    tokens,
    ln_gain,
    in_proj,
    decay_log,
    angle,
    out_proj,
    skip,
    glu_proj,
    down_proj,
    lengths,
    cotangent,
):
    R, D = tokens.shape
    n = in_proj.shape[2]
    N = n * T
    units = down_proj.shape[0]
    C = S // 2
    fused = (
        S == 8
        and T % 2 == 0
        and T > 2
        and 2 * n == 128
        and 2 * units == D
        and all(size % (16 * S) == 0 for size in (D, 2 * n, units))
    )
    vmem = pl.BlockSpec(memory_space=pltpu.VMEM)
    anywhere = pl.BlockSpec(memory_space=pl.ANY)
    hbm = pl.BlockSpec(memory_space=pltpu.HBM)
    ins = dict(
        lengths=(lengths, hbm),
        tokens=(tokens, hbm),
        cot=(cotangent, hbm),
        gain=(ln_gain.reshape(1, D), hbm),
        skip=(skip, hbm),
    )
    outs = dict(
        result=((R, D), BF16, anywhere),
        grad_tokens=((R, D), F32, anywhere),
        small=((8, D), F32, vmem),
    )
    scratch = dict(
        gain_row=((1, D), F32),
        skip_row=((D,), BF16),
        tokens_raw=((R, D), BF16),
        cot_raw=((R, D), BF16),
        turn=((BLOCK, BLOCK), BF16),
        tokens_in=((R, D), BF16),
        cot_in=((R, D), BF16),
        centred=((R, D), F32),
        inv_std=((R, 128), F32),
        normed=((R, D), BF16),
        proj=((R, 2 * N), F32),
        keep=((R, 128), F32),
        keep_next=((R, 128), F32),
        state=((R, 2 * N), F32),
        state_low=((R, 2 * N), BF16),
        act=((R, D), BF16),
        d_gelu=((R, D), F32),
        d_act=((R, D), F32),
        summed=((R, D), F32),
        d_mixed=((R, D), BF16),
        d_proj=((R, 2 * N), BF16),
        hidden=((R, units), BF16),
        d_unit=((R, 2 * units), BF16),
        seg_carry=((SEGMENTS, 2 * N), F32),
        sums=((16, D), F32),
        state_all=((T, S, 2 * N // 128, 128), F32),
        adj_all=((T, S, 2 * N // 128, 128), F32),
    )
    in_rows = in_proj.transpose(0, 2, 1)
    if fused:
        unit_rows = D // S + units // S
        ins.update(
            decay_log=(decay_log.reshape(1, n), hbm),
            angle=(angle.reshape(1, n), hbm),
            in_proj=(in_rows.reshape(C, 2, 2 * n // S, D), hbm),
            out_proj=(out_proj.reshape(C, 2, 2 * n // S, D), hbm),
            glu_proj=(glu_proj.reshape(2, C, 2, D // S, units), hbm),
            down_proj=(down_proj.reshape(C, 2, units // S, D), hbm),
        )
        outs.update(
            grad_in=((C, 2, 2 * n // S, D), BF16, anywhere),
            grad_out=((C, 2, 2 * n // S, D), BF16, anywhere),
            grad_units=((C, 2, unit_rows, D), BF16, anywhere),
        )

        def whole(parts, rows, lead=()):
            return (lead + (parts, C, 2, rows, D), BF16)

        def halves(parts, rows, lead=()):
            return (lead + (parts, C, rows, D), BF16)

        def eighths(parts, rows, lead=()):
            return (lead + (C - 1, parts, rows, D), BF16)

        def own(parts, rows, lead=()):
            return (lead + (parts, rows, D), BF16)

        unit_sizes = (1, unit_rows, (T,))
        rate_sizes = (T, 2 * n // S)
        scratch.update(
            w_in=((2 * N, D), BF16),
            w_out=((2 * N, D), BF16),
            rates_all=((T, 8, 128), F32),
            decay_row=((1, n), F32),
            angle_row=((1, n), F32),
            in_slices=((T, C, 2, 2 * n // S, D), BF16),
            out_slices=((T, C, 2, 2 * n // S, D), BF16),
            unit_slices=((T, C, 2, unit_rows, D), BF16),
            grad_rates=((2 * N, D), BF16),
            small_tp=((T, 16, 128), F32),
            small_seq=((S, 16, 128), F32),
            unit_sums=((T - 1, 1, unit_rows, D), BF16),
            out_sums=((T - 1, 2 * n // S, D), BF16),
            in_sums=((T - 1, 2 * n // S, D), BF16),
            unit_sum=((1, C, 2, unit_rows, D), BF16),
            out_sum=((1, C, 2, 2 * n // S, D), BF16),
            in_sum=((1, C, 2, 2 * n // S, D), BF16),
            unit_full=whole(*unit_sizes),
            unit_halves=halves(*unit_sizes),
            unit_eighths=eighths(*unit_sizes),
            unit_summed=own(*unit_sizes),
            out_full=whole(*rate_sizes),
            out_halves=halves(*rate_sizes),
            out_eighths=eighths(*rate_sizes),
            out_summed=own(*rate_sizes),
            in_full=whole(*rate_sizes),
            in_halves=halves(*rate_sizes),
            in_eighths=eighths(*rate_sizes),
            in_summed=own(*rate_sizes),
        )
        links = 200
    else:
        w_in = lax.all_gather(in_rows, "tp", axis=1, tiled=True).reshape(2 * N, D)
        w_out = lax.all_gather(out_proj, "tp", axis=1, tiled=True).reshape(2 * N, D)
        glu = lax.all_gather(glu_proj, "tp")
        rates = jnp.stack(
            [lax.all_gather(part, "tp", tiled=True) for part in decay_terms(decay_log, angle)]
            + [jnp.zeros((N,), F32)] * 5
        )
        ins.update(
            rates=(rates, vmem),
            w_in=(w_in, vmem),
            w_out=(w_out, vmem),
            glu=(jnp.concatenate([glu[:, 0], glu[:, 1]], 2), vmem),
            down=(lax.all_gather(down_proj, "tp"), vmem),
        )
        outs.update(
            grad_in=((2 * N, D), BF16, vmem),
            grad_out=((2 * N, D), BF16, vmem),
            grad_glu=((T, D, 2 * units), BF16, vmem),
            grad_down=((T, units, D), BF16, vmem),
        )
        links = 2 * (T * S - 1)
    names = [*ins, *outs, *scratch, *dict(counts=0, local_sem=0, send_sem=0, recv_sem=0)]
    results = pl.pallas_call(
        functools.partial(layer_kernel, S, T, fused, names),
        out_shape=tuple(jax.ShapeDtypeStruct(shape, dtype) for shape, dtype, _ in outs.values()),
        in_specs=[spec for _, spec in ins.values()],
        out_specs=tuple(spec for _, _, spec in outs.values()),
        scratch_shapes=[pltpu.VMEM(shape, dtype) for shape, dtype in scratch.values()]
        + [
            pltpu.SMEM(lengths.shape, jnp.int32),
            pltpu.SemaphoreType.DMA((12,)),
            pltpu.SemaphoreType.DMA((links,)),
            pltpu.SemaphoreType.DMA((links,)),
        ],
        compiler_params=pltpu.CompilerParams(
            collective_id=0, has_side_effects=True, vmem_limit_bytes=46 * 2**20
        ),
    )(
        *[
            pltpu.with_memory_space_constraint(value, pltpu.HBM) if spec is hbm else value
            for value, spec in ins.values()
        ]
    )
    if fused:
        result, grad_tokens, small, grad_in, grad_out, grad_units = results
        ins = dict(
            result_in=(result, anywhere),
            grad_tokens_in=(grad_tokens, anywhere),
            small=(small, vmem),
            in_in=(grad_in, vmem),
            out_in=(grad_out, vmem),
            units_in=(grad_units, vmem),
            decay_log=(decay_log.reshape(1, n), vmem),
            angle=(angle.reshape(1, n), vmem),
        )
        outs = dict(
            result=((R, D), BF16, anywhere),
            grad_tokens=((R, D), F32, anywhere),
            gain=((1, D), F32, vmem),
            in_=((C, 2, 2 * n // S, D), F32, vmem),
            decay=((1, n), F32, vmem),
            turn=((1, n), F32, vmem),
            out=((C, 2, 2 * n // S, D), F32, vmem),
            skip=((1, D), F32, vmem),
            glu=((2, C, 2, D // S, units), F32, vmem),
            down=((C, 2, units // S, D), F32, vmem),
        )
        scratch = dict(result_rows=((R, D), BF16), grad_rows=((R, D), F32))
        names = [*ins, *outs, *scratch, *dict(local_sem=0)]
        result, grad_tokens, gain, in_, decay, turn, out, skip_sum, glu, down = pl.pallas_call(
            functools.partial(finish_kernel, T, names),
            out_shape=tuple(
                jax.ShapeDtypeStruct(shape, dtype) for shape, dtype, _ in outs.values()
            ),
            in_specs=[spec for _, spec in ins.values()],
            out_specs=tuple(spec for _, _, spec in outs.values()),
            scratch_shapes=[pltpu.VMEM(shape, dtype) for shape, dtype in scratch.values()]
            + [pltpu.SemaphoreType.DMA((3,))],
            compiler_params=pltpu.CompilerParams(vmem_limit_bytes=16 * 2**20),
        )(*[value for value, _ in ins.values()])
        return (
            result,
            grad_tokens,
            gain.reshape(D),
            in_.reshape(2, n, D).transpose(0, 2, 1),
            decay.reshape(n),
            turn.reshape(n),
            out.reshape(2, n, D),
            skip_sum.reshape(D),
            glu.reshape(2, D, units),
            down.reshape(units, D),
        )
    result, grad_tokens, small, grad_in, grad_out, grad_glu, grad_down = results
    small = lax.psum(small, ("seq", "tp"))

    def reduced(part):
        part = lax.psum_scatter(part, "tp", scatter_dimension=0, tiled=True)
        return lax.psum(part, "seq").astype(F32)

    def by_tp(grad):
        return reduced(grad.reshape(2, T, n, D).transpose(1, 0, 2, 3).reshape(T * 2, n, D))

    grad_glu = reduced(grad_glu)[0].reshape(D, 2, units).transpose(1, 0, 2)
    grad_down = reduced(grad_down)[0]

    def mine(row):
        return lax.dynamic_slice_in_dim(row, lax.axis_index("tp") * n, n)

    g_re, g_im, g_gamma = (mine(small[2, :N]), mine(small[2, N:]), mine(small[3, :N]))
    _, pull = jax.vjp(decay_terms, decay_log, angle)
    grad_decay, grad_angle = pull((g_re, g_im, g_gamma))
    return (
        result,
        grad_tokens,
        small[0],
        by_tp(grad_in).transpose(0, 2, 1),
        grad_decay,
        grad_angle,
        by_tp(grad_out),
        small[1],
        grad_glu,
        grad_down,
    )


def solution(mesh):
    in_specs = (
        P(("seq", "tp"), None),
        P(),
        P(None, None, "tp"),
        P("tp"),
        P("tp"),
        P(None, "tp", None),
        P(),
        P(None, None, "tp"),
        P("tp", None),
        P(),
        P(("seq", "tp"), None),
    )
    out_specs = (
        P(("seq", "tp"), None),
        P(("seq", "tp"), None),
        P(),
        P(None, None, "tp"),
        P("tp"),
        P("tp"),
        P(None, "tp", None),
        P(),
        P(None, None, "tp"),
        P("tp", None),
    )
    return jax.shard_map(
        functools.partial(local, mesh.shape["seq"], mesh.shape["tp"]),
        mesh=mesh,
        in_specs=in_specs,
        out_specs=out_specs,
        check_vma=False,
    )
```

```python
import functools
import types
import jax
import jax.numpy as jnp
from jax import lax
from jax.experimental import pallas as pl
from jax.experimental.pallas import tpu as pltpu
from jax.sharding import PartitionSpec as P

epsilon = 1e-05
MESH = pl.DeviceIdType.MESH
F32 = jnp.float32
BF16 = jnp.bfloat16
GROUPS = 2
SEGMENTS = 8 * GROUPS
BLOCK = SEGMENTS * SEGMENTS


def dot(left, right):
    return jnp.dot(left, right, preferred_element_type=F32)


def dot_nt(left, right):
    return lax.dot_general(left, right, (((1,), (1,)), ((), ())), preferred_element_type=F32)


def complex_mul(left_re, left_im, right_re, right_im):
    return (left_re * right_re - left_im * right_im, left_re * right_im + left_im * right_re)


def dot_tn(left, right):
    return lax.dot_general(left, right, (((0,), (0,)), ((), ())), preferred_element_type=F32)


def power(base, exponent):
    result = None
    square = base
    while exponent:
        if exponent & 1:
            result = square if result is None else complex_mul(*result, *square)
        exponent >>= 1
        if exponent:
            square = complex_mul(*square, *square)
    return result


class Links:
    def __init__(self, send_sem, recv_sem):
        self.send_sem = send_sem
        self.recv_sem = recv_sem
        self.groups = []

    def group(self, whole):
        group = Group(self, len(self.groups), whole)
        self.groups.append(group)
        return group

    def send(self, whole, copies):
        group = self.group(whole)
        for source, target, device in copies:
            group.add(source, target, device)
        return group

    def close(self):
        for group in self.groups:
            group.last.wait_send()


class Group:
    def __init__(self, links, index, whole):
        self.links = links
        self.index = index
        self.whole = whole

    def copy(self, source, target, device):
        return pltpu.make_async_remote_copy(
            src_ref=source,
            dst_ref=target,
            send_sem=self.links.send_sem.at[self.index],
            recv_sem=self.links.recv_sem.at[self.index],
            device_id=device,
            device_id_type=MESH,
        )

    def add(self, source, target, device):
        self.copy(source, target, device).start()
        self.last = self.copy(self.whole, self.whole, device)

    def arrive(self):
        self.last.wait_recv()


class Gather:
    def __init__(self, place, buffer, first, last):
        self.place = place
        self.buffer = buffer
        self.slots = range(first, last)
        self.part = buffer.at[pl.ds(first, last - first)]

    def over_tp(self):
        p = self.place
        self.copies = p.links.send(
            self.part.at[:, p.chip, p.core],
            [
                (
                    self.buffer.at[0, p.chip, p.core],
                    self.buffer.at[slot, p.chip, p.core],
                    (p.s, lax.rem(p.t + p.T - slot, p.T)),
                )
                for slot in self.slots
            ],
        )

    def over_plane(self):
        p = self.place
        self.copies.arrive()
        mine = self.part.at[:, p.chip, p.core]
        self.copies = p.links.send(
            self.part.at[:, pl.ds(0, len(p.chips)), p.core],
            [(mine, mine, device) for _, device in p.chips],
        )

    def over_cores(self):
        p = self.place
        self.copies.arrive()
        mine = self.part.at[:, :, p.core]
        self.copies = p.links.send(mine, [(mine, mine, p.sibling)])

    def finish(self):
        self.copies.arrive()


class Reduce:
    def __init__(self, place, full, halves, eighths, summed):
        self.place = place
        self.full = full
        self.halves = halves
        self.eighths = eighths
        self.summed = summed

    def over_cores(self):
        p = self.place
        self.copies = p.links.send(
            self.halves, [(self.full.at[:, :, 1 - p.core], self.halves, p.sibling)]
        )

    def over_plane(self):
        p = self.place
        self.copies.arrive()
        parts, chips = self.halves.shape[:2]

        @pl.loop(0, parts * chips)
        def _(index):
            part, chip = (lax.div(index, chips), lax.rem(index, chips))
            self.halves[part, chip] = (
                self.full[part, chip, p.core].astype(F32) + self.halves[part, chip].astype(F32)
            ).astype(BF16)

        self.copies = p.links.send(
            self.eighths,
            [
                (self.halves.at[:, chip], self.eighths.at[k], device)
                for k, (chip, device) in enumerate(p.chips)
            ],
        )

    def sum_plane(self):
        p = self.place
        self.copies.arrive()

        @pl.loop(0, self.halves.shape[0])
        def _(part):
            total = self.halves[part, p.chip].astype(F32)
            for k in range(len(p.chips)):
                total = total + self.eighths[k, part].astype(F32)
            self.summed[part] = total.astype(BF16)


class Reduce2(Reduce):
    def __init__(self, place, full, halves, eighths, summed):
        super().__init__(place, full, halves, eighths, summed)
        self.rows = halves.shape[2] // 2
        self.ours = halves.at[:, :, pl.ds(0, self.rows)]
        self.theirs = halves.at[:, :, pl.ds(self.rows, self.rows)]

    def sum_cores(self, chip):
        self.halves[0, chip] = (
            self.full[0, chip, self.place.core].astype(F32) + self.halves[0, chip].astype(F32)
        ).astype(BF16)

    def over_plane(self):
        p = self.place
        self.copies.arrive()
        self.sum_cores(p.by_x)
        self.sum_cores(p.by_y)
        self.sum_cores(p.by_xy)
        self.copies = p.links.send(
            self.eighths.at[pl.ds(0, 2)],
            [
                (part.at[0, chip], self.eighths.at[index, 0, rows], device)
                for index, part, chip, rows, device in (
                    (0, self.ours, p.by_x, pl.ds(0, self.rows), p.x_device),
                    (1, self.ours, p.by_xy, pl.ds(0, self.rows), p.x_device),
                    (0, self.theirs, p.by_y, pl.ds(self.rows, self.rows), p.y_device),
                    (1, self.theirs, p.by_xy, pl.ds(self.rows, self.rows), p.y_device),
                )
            ],
        )
        self.sum_cores(p.chip)

    def turn_plane(self):
        p = self.place
        self.copies.arrive()
        n = self.rows
        for index, chip in ((0, p.chip), (1, p.by_y)):
            self.halves[0, chip, 0:n] = (
                self.halves[0, chip, 0:n].astype(F32) + self.eighths[index, 0, 0:n].astype(F32)
            ).astype(BF16)
        for index, chip in ((0, p.chip), (1, p.by_x)):
            self.halves[0, chip, n:] = (
                self.halves[0, chip, n:].astype(F32) + self.eighths[index, 0, n:].astype(F32)
            ).astype(BF16)
        self.copies = p.links.send(
            self.eighths.at[2],
            [
                (self.ours.at[0, p.by_y], self.eighths.at[2, 0, pl.ds(0, n)], p.y_device),
                (self.theirs.at[0, p.by_x], self.eighths.at[2, 0, pl.ds(n, n)], p.x_device),
            ],
        )

    def sum_plane(self):
        p = self.place
        self.copies.arrive()
        self.summed[0] = (
            self.halves[0, p.chip].astype(F32) + self.eighths[2, 0].astype(F32)
        ).astype(BF16)


class Spread:
    def __init__(self, place, buffer):
        self.place = place
        self.buffer = buffer

    def over_plane(self):
        p = self.place
        mine = self.buffer.at[:, p.chip, p.core]
        self.copies = p.links.send(
            self.buffer.at[:, pl.ds(0, len(p.chips)), p.core],
            [(mine, mine, device) for _, device in p.chips],
        )

    def over_cores(self):
        p = self.place
        self.copies.arrive()
        mine = self.buffer.at[:, :, p.core]
        self.copies = p.links.send(mine, [(mine, mine, p.sibling)])

    def finish(self):
        self.copies.arrive()


class Place:
    def __init__(self, S, T, links):
        self.S, self.T, self.links = (S, T, links)
        self.s = lax.axis_index("seq")
        self.t = lax.axis_index("tp")
        C = S // 2
        self.core = lax.rem(self.s, 2)
        self.chip = lax.div(self.s, 2)
        self.sibling = (self.chip * 2 + 1 - self.core, self.t)
        x = lax.rem(self.chip, 2)
        y = lax.div(self.chip, 2)
        self.by_x = y * 2 + 1 - x
        self.by_y = (1 - y) * 2 + x
        self.by_xy = (1 - y) * 2 + 1 - x
        self.x_device = (self.by_x * 2 + self.core, self.t)
        self.y_device = (self.by_y * 2 + self.core, self.t)
        self.chips = []
        for k in range(1, C):
            chip = lax.rem(self.chip + k, C)
            self.chips.append((chip, (chip * 2 + self.core, self.t)))


def layer_kernel(S, T, fused, names, *refs):
    r = types.SimpleNamespace(**dict(zip(names, refs)))
    links = Links(r.send_sem, r.recv_sem)
    place = Place(S, T, links)
    lengths = r.counts
    tokens = r.tokens_raw
    cot = r.cot_raw
    result = r.tokens_raw
    grad_tokens = r.d_gelu
    turn = r.turn
    tokens_in = r.tokens_in
    cot_in = r.cot_in
    centred = r.centred
    inv_std = r.inv_std
    normed = r.normed
    proj = r.proj
    keep = r.keep
    keep_next = r.keep_next
    state = r.state
    state_low = r.state_low
    act = r.act
    d_gelu = r.d_gelu
    d_act = r.d_act
    summed = r.summed
    d_mixed = r.d_mixed
    adjoint = r.summed
    d_proj = r.d_proj
    hidden = r.hidden
    d_unit = r.d_unit
    seg_carry, sums = (r.seg_carry, r.sums)
    w_in, w_out = (r.w_in, r.w_out)
    R, D = tokens.shape
    N = w_in.shape[0] // 2
    n = N // T
    L = R // SEGMENTS
    s = place.s
    t = place.t
    first = (s * T + t) * R

    peers_tp = [lax.rem(t + k, T) for k in range(1, T)]
    peers_seq = [lax.rem(s + k, S) for k in range(1, S)]
    barrier = pltpu.get_barrier_semaphore()
    for peer in peers_tp:
        pl.semaphore_signal(barrier, inc=1, device_id=(s, peer), device_id_type=MESH)
    for peer in peers_seq:
        pl.semaphore_signal(barrier, inc=1, device_id=(peer, t), device_id_type=MESH)

    fetched = [
        pltpu.make_async_copy(source, target, r.local_sem.at[index])
        for index, (source, target) in enumerate(
            ((r.tokens, tokens), (r.cot, cot), (r.gain, r.gain_row), (r.skip, r.skip_row), (r.lengths, r.counts))
        )
    ]
    if fused:
        in_slices, out_slices, unit_slices = (r.in_slices, r.out_slices, r.unit_slices)
        units = r.down_proj.shape[2] * S
        D_rows = r.glu_proj.shape[3]
        gated_rows = unit_slices.at[0, :, :, pl.ds(0, D_rows)]
        weights = [
            pltpu.make_async_copy(source, target, r.local_sem.at[5 + index])
            for index, (source, target) in enumerate(
                (
                    (r.decay_log, r.decay_row),
                    (r.angle, r.angle_row),
                    (r.in_proj, in_slices.at[0]),
                    (r.out_proj, out_slices.at[0]),
                    (r.glu_proj.at[0], gated_rows.at[:, :, :, pl.ds(0, units)]),
                    (r.glu_proj.at[1], gated_rows.at[:, :, :, pl.ds(units, units)]),
                    (r.down_proj, unit_slices.at[0, :, :, pl.ds(D_rows, units // S)]),
                )
            )
        ]
        for copy in weights:
            copy.start()
    for copy in fetched:
        copy.start()
    if fused:
        rates_all = r.rates_all
        rates_all[t] = jnp.zeros(rates_all.shape[1:], F32)
        gather_in = Gather(place, in_slices, 1, T)
        gather_out = Gather(place, out_slices, 1, T)
        gather_units = [Gather(place, unit_slices, slot, slot + 1) for slot in range(1, T)]
        for copy in weights:
            copy.wait()
        for index, row in enumerate(decay_terms(r.decay_row[...], r.angle_row[...])):
            rates_all[t, index : index + 1, 0:n] = row
        pl.semaphore_wait(barrier, T - 1 + S - 1)
        gather_in.over_tp()
        rate_copies = links.send(
            rates_all.at[pl.ds(0, T - 1)],
            [(rates_all.at[t], rates_all.at[t], (s, peer)) for peer in peers_tp],
        )

    for copy in fetched[2:]:
        copy.wait()
    starts = []
    total = jnp.int32(0)
    for index in range(lengths.shape[0]):
        starts.append(total)
        total = total + lengths[index]

    def keeps(position):
        hit = position == starts[0]
        for start in starts[1:]:
            hit = hit | (position == start)
        return jnp.where(hit, 0.0, 1.0)

    def clear(low, high):
        hit = (starts[0] >= low) & (starts[0] < high)
        for start in starts[1:]:
            hit = hit | ((start >= low) & (start < high))
        return jnp.where(hit, 0.0, 1.0)

    gain_row = r.gain_row[...]
    skip_row = r.skip_row[...].astype(F32).reshape(1, D)

    down_index = lax.broadcasted_iota(jnp.int32, (BLOCK, BLOCK), 0)
    across_index = lax.broadcasted_iota(jnp.int32, (BLOCK, BLOCK), 1)
    turned = lax.rem(down_index, SEGMENTS) * SEGMENTS + lax.div(down_index, SEGMENTS)
    turn[...] = jnp.where(turned == across_index, 1.0, 0.0).astype(BF16)

    def pieces(block):
        return [
            pl.ds(pl.multiple_of(run * L + block * SEGMENTS, SEGMENTS), SEGMENTS)
            for run in range(SEGMENTS)
        ]

    def taken(ref, block):
        return dot(turn[...], jnp.concatenate([ref[piece, :] for piece in pieces(block)], 0))

    def block_rows(tile):
        return pl.ds(pl.multiple_of(tile * BLOCK, BLOCK), BLOCK)

    def norm_tile(tile):
        rows = block_rows(tile)
        x = taken(tokens, tile)
        tokens_in[rows, :] = x.astype(BF16)
        mean = jnp.mean(x, 1, keepdims=True)
        inv = lax.rsqrt(jnp.mean(x * x, 1, keepdims=True) - mean * mean + epsilon)
        c = (x - mean) * inv
        centred[rows, :] = c
        inv_std[rows, :] = jnp.broadcast_to(inv, (BLOCK, 128))
        n_rows = (c * gain_row).astype(BF16)
        normed[rows, :] = n_rows

    def cot_tile(tile):
        rows = block_rows(tile)
        cot_rows = taken(cot, tile).astype(BF16)
        cot_in[rows, :] = cot_rows
        index = tile * BLOCK + lax.broadcasted_iota(jnp.int32, (BLOCK, 128), 0)
        position = first + lax.rem(index, SEGMENTS) * L + lax.div(index, SEGMENTS)
        keep[rows, :] = keeps(position)
        keep_next[rows, :] = keeps(position + 1)

    fetched[0].wait()
    pl.loop(0, R // BLOCK)(norm_tile)
    if fused:
        gather_in.over_plane()
        gather_out.over_tp()
        gather_units[0].over_tp()
    fetched[1].wait()
    pl.loop(0, R // BLOCK)(cot_tile)

    def assemble(slices, weight):
        for i in range(T):
            at = lax.rem(t + i, T) * n
            for part in range(2):
                weight[pl.ds(pl.multiple_of(part * N + at, n), n), :] = slices[
                    i, part * (S // 4) : (part + 1) * (S // 4)
                ].reshape(n, D)

    if fused:
        gather_in.over_cores()
        gather_units[1].over_tp()
        rate_copies.arrive()
        half = lax.broadcasted_iota(jnp.int32, (8, 128), 1) < n
        rate_rows = [rates_all[z] for z in range(T)]
        joined = jnp.concatenate(
            [
                jnp.where(half, rate_rows[z], pltpu.roll(rate_rows[z + 1], n, 1))
                for z in range(0, T, 2)
            ],
            1,
        )
        lam_re, lam_im, gamma = (joined[k : k + 1] for k in range(3))
        gather_in.finish()
        for gather in gather_units[2:]:
            gather.over_tp()
        gather_out.over_plane()
        assemble(in_slices, w_in)
    else:
        pl.semaphore_wait(barrier, T - 1 + S - 1)
        lam_re, lam_im, gamma = (r.rates[k : k + 1, :] for k in range(3))
    gamma_signed = jnp.concatenate([gamma, -gamma], 1)

    @pl.loop(0, R // BLOCK)
    def _(tile):
        rows = block_rows(tile)
        proj[rows, :] = dot_nt(normed[rows, :], w_in[...]) * gamma_signed

    low8_re = jnp.broadcast_to(lam_re, (8, N))
    low8_im = jnp.broadcast_to(lam_im, (8, N))

    def rows_of(group, step):
        return pl.ds(pl.multiple_of(step * SEGMENTS + group * 8, 8), 8)

    def spread(row):
        return jnp.concatenate([row] * (N // 128), 1)

    def scan_step(values, mask, add, sign):
        new_re, new_im = complex_mul(low8_re, sign * low8_im, *(value * mask for value in values))
        return (new_re + add[:, :N], new_im + add[:, N:])

    zero8 = jnp.zeros((8, N), F32)
    none = tuple((zero8, zero8) for _ in range(GROUPS))

    def forward_step(step, carry):
        return tuple(
            scan_step(
                carry[group],
                spread(keep[rows_of(group, step), :]),
                proj[rows_of(group, step), :],
                -1.0,
            )
            for group in range(GROUPS)
        )

    def segment_rows(finals):
        return [
            (finals[group][0][sub : sub + 1], finals[group][1][sub : sub + 1])
            for group in range(GROUPS)
            for sub in range(8)
        ]

    def fold(start, factor, items, masks, taken):
        before = []
        carry = start
        for (item_re, item_im), mask, take in zip(items, masks, taken):
            before.append(carry)
            moved = complex_mul(*factor, *carry)
            longer = (moved[0] * mask + item_re, moved[1] * mask + item_im)
            if take is None:
                carry = longer
            else:
                carry = tuple(jnp.where(take, new, old) for new, old in zip(longer, carry))
        return carry, before

    zero1 = (jnp.zeros((1, N), F32), jnp.zeros((1, N), F32))
    lam = (lam_re, lam_im)
    conj = (lam_re, -lam_im)

    def unpack(row):
        return (row[:, :N], row[:, N:])

    def packed(row, height):
        parts = [row[:, at : at + 128] for at in range(0, row.shape[1], 128)]
        return jnp.concatenate(parts + [parts[0]] * (height - len(parts)), 0)

    def unpacked(tile, height):
        return jnp.concatenate([tile[k : k + 1, :] for k in range(height)], 1)

    class Exchange:
        def __init__(self, own, factor, buffer, forward):
            self.forward = forward
            self.shift = 0 if forward else 1
            self.factor = power(factor, R)
            self.buffer = buffer
            buffer[t, s] = packed(jnp.concatenate(own, 1), 2 * N // 128)
            mine = buffer.at[t, s]
            self.copies = [
                links.send(
                    buffer.at[0], [(mine, mine, (peer, peer_tp)) for peer in [s, *peers_seq]]
                )
                for peer_tp in peers_tp
            ]
            self.copies.append(
                links.send(
                    buffer.at[0, pl.ds(0, S - 1)], [(mine, mine, (peer, t)) for peer in peers_seq]
                )
            )

        def carry(self):
            for copies in self.copies:
                copies.arrive()

            def order(count):
                return list(range(count)) if self.forward else list(range(count))[::-1]

            def ahead(block, z):
                mine, other = (s * T + t, block * T + z)
                return other < mine if self.forward else other > mine

            rows = [
                jnp.concatenate(
                    [unpacked(self.buffer[z, block], 2 * N // 128) for block in range(S)], 0
                )
                for z in range(T)
            ]
            block = lax.broadcasted_iota(jnp.int32, (S, N), 0)
            carry = (jnp.zeros((S, N), F32), jnp.zeros((S, N), F32))
            for z in order(T):
                low = (block * T + z) * R + self.shift
                mask = clear(low, low + R)
                item = (rows[z][:, :N], rows[z][:, N:])
                moved = complex_mul(*self.factor, *carry)
                longer = (moved[0] * mask + item[0], moved[1] * mask + item[1])
                mine = block == s
                taken = jnp.logical_or(jnp.logical_not(mine), ahead(s, z))
                carry = tuple(jnp.where(taken, new, old) for new, old in zip(longer, carry))
            result = zero1
            whole = power(self.factor, T)
            for b in order(S):
                low = b * T * R + self.shift
                mask = clear(low, low + T * R)
                moved = complex_mul(*whole, *result)
                longer = (
                    moved[0] * mask + carry[0][b : b + 1],
                    moved[1] * mask + carry[1][b : b + 1],
                )
                earlier = b < s if self.forward else b > s
                result = tuple(jnp.where(earlier, new, old) for new, old in zip(longer, result))
            inside = tuple(
                jnp.sum(jnp.where(block == s, part, 0.0), 0, keepdims=True) for part in carry
            )
            for z in order(T):
                low = (s * T + z) * R + self.shift
                mask = clear(low, low + R)
                moved = complex_mul(*self.factor, *result)
                longer = (moved[0] * mask, moved[1] * mask)
                result = tuple(
                    jnp.where(ahead(s, z), new, old) for new, old in zip(longer, result)
                )
            return (result[0] + inside[0], result[1] + inside[1])

    finals = segment_rows(lax.fori_loop(0, L, forward_step, none))
    seg_masks = [clear(first + index * L, first + (index + 1) * L) for index in range(SEGMENTS)]
    factor_seg = power(conj, L)
    own, _ = fold(zero1, factor_seg, finals, seg_masks, [None] * SEGMENTS)
    exchange = Exchange(own, conj, r.state_all, True)
    if fused:
        gather_units[0].over_plane()
        gather_out.over_cores()
    if fused:
        gather_units[1].over_plane()
        gather_out.finish()
        assemble(out_slices, w_out)
    carry = exchange.carry()
    _, entering = fold(carry, factor_seg, finals, seg_masks, [None] * SEGMENTS)
    for index, (row_re, row_im) in enumerate(entering):
        seg_carry[index : index + 1, :] = jnp.concatenate([row_re, row_im], 1)

    def write_state(step, carry):
        new = forward_step(step, carry)
        for group in range(GROUPS):
            state[rows_of(group, step), :] = jnp.concatenate(new[group], 1)
        return new

    def entering_groups():
        return tuple(
            unpack(seg_carry[group * 8 : group * 8 + 8, :]) for group in range(GROUPS)
        )

    lax.fori_loop(0, L, write_state, entering_groups())
    if fused:
        for gather in gather_units[2:]:
            gather.over_plane()

    @pl.loop(0, R // BLOCK)
    def _(tile):
        rows = block_rows(tile)
        low = state[rows, :].astype(BF16)
        state_low[rows, :] = low
        x = dot(low, w_out[...]) + skip_row * normed[rows, :].astype(F32)
        scale = 0.7978845608028654
        th = jnp.tanh(scale * (x + 0.044715 * x * x * x))
        half = 0.5 * (1.0 + th)
        a = (x * half).astype(BF16)
        act[rows, :] = a
        d_gelu[rows, :] = half + 0.5 * x * (1.0 - th * th) * scale * (1.0 + 0.134145 * x * x)

    if fused:
        reduces = [
            Reduce2(
                place,
                r.unit_full.at[i],
                r.unit_halves.at[i],
                r.unit_eighths.at[i],
                r.unit_summed.at[i],
            )
            for i in range(T)
        ]

    UNIT_ROWS = min(512, R)
    units = hidden.shape[1]
    unit_copies = links.group(r.unit_sums) if fused else None

    def unit_grads(i):
        c = lax.rem(t + i, T)
        gated_grad = dot_tn(act[...], d_unit[...]).astype(BF16)
        down_grad = dot_tn(hidden[...], cot_in[...]).astype(BF16)
        if fused:
            full = r.unit_full
            full[i, 0, :, :, 0:D_rows] = gated_grad.reshape(S // 2, 2, D_rows, 2 * units)
            full[i, 0, :, :, D_rows:] = down_grad.reshape(S // 2, 2, units // S, D)
            reduces[i].over_cores()
        else:
            r.grad_glu[c] = gated_grad
            r.grad_down[c] = down_grad

    def unit_sums(i):
        reduces[i].sum_plane()
        if i > 0:
            unit_copies.add(r.unit_summed.at[i], r.unit_sums.at[i - 1], (s, lax.rem(t + i, T)))

    for i in range(T):
        c = lax.rem(t + i, T)
        if fused:
            if i > 0:
                gather_units[i - 1].finish()
            if i < T - 1:
                gather_units[i].over_cores()
            w_gated = unit_slices[i, :, :, 0:D_rows].reshape(D, 2 * units)
            w_down = unit_slices[i, :, :, D_rows:].reshape(units, D)
        else:
            w_gated = r.glu[c]
            w_down = r.down[c]

        for tile in range(R // UNIT_ROWS):
            rows = slice(tile * UNIT_ROWS, (tile + 1) * UNIT_ROWS)
            both = dot(act[rows, :], w_gated)
            value, gate = (both[:, :units], both[:, units:])
            sigma = 0.5 * jnp.tanh(0.5 * gate) + 0.5
            gated = value * sigma
            h = gated.astype(BF16)
            hidden[rows, :] = h
            d_h = dot_nt(cot_in[rows, :], w_down)
            d_both = jnp.concatenate(
                [(d_h * sigma).astype(BF16), (d_h * gated * (1.0 - sigma)).astype(BF16)], 1
            )
            d_unit[rows, :] = d_both
            added = dot(h, w_down)
            d_a = dot_nt(d_both, w_gated)
            if i > 0:
                added = added + summed[rows, :]
                d_a = d_a + d_act[rows, :]
            if i < T - 1:
                summed[rows, :] = added
                d_act[rows, :] = d_a
            else:
                d_m = (d_gelu[rows, :] * d_a).astype(BF16)
                d_mixed[rows, :] = d_m
                adjoint[rows, :] = dot_nt(d_m, w_out[...])
                out = (tokens_in[rows, :].astype(F32) + added).astype(BF16)
                for block in range(UNIT_ROWS // BLOCK):
                    turned = dot(turn[...], out[block * BLOCK : block * BLOCK + BLOCK])
                    turned = turned.astype(BF16)
                    for run, piece in enumerate(pieces(tile * (UNIT_ROWS // BLOCK) + block)):
                        result[piece, :] = turned[run * SEGMENTS : run * SEGMENTS + SEGMENTS]

        if fused and i > 0:
            reduces[i - 1].over_plane()
        unit_grads(i)
        if fused and i > 1:
            reduces[i - 2].turn_plane()
        if fused and i > 2:
            unit_sums(i - 3)

    result_copy = pltpu.make_async_copy(result, r.result, r.local_sem.at[0])
    result_copy.start()

    def backward_step(index, carry):
        step = L - 1 - index
        return tuple(
            scan_step(
                carry[group],
                spread(keep_next[rows_of(group, step), :]),
                adjoint[rows_of(group, step), :],
                1.0,
            )
            for group in range(GROUPS)
        )

    finals = segment_rows(lax.fori_loop(0, L, backward_step, none))[::-1]
    seg_masks = [
        clear(first + index * L + 1, first + (index + 1) * L + 1) for index in range(SEGMENTS)
    ][::-1]
    factor_seg = power(lam, L)
    own, _ = fold(zero1, factor_seg, finals, seg_masks, [None] * SEGMENTS)
    exchange = Exchange(own, lam, r.adj_all, False)
    if fused:
        reduces[T - 2].turn_plane()
        reduces[T - 1].over_plane()
    grad_out = dot_tn(state_low[...], d_mixed[...]).astype(BF16)

    def divide(grad, full):
        for i in range(T):
            at = lax.rem(t + i, T) * n
            for part in range(2):
                rows = pl.ds(pl.multiple_of(part * N + at, n), n)
                full[i, part * (S // 4) : (part + 1) * (S // 4)] = grad[rows, :].reshape(
                    S // 4, 2, -1, D
                )

    if fused:
        r.grad_rates[...] = grad_out
        divide(r.grad_rates, r.out_full)
        out_reduce = Reduce(place, r.out_full, r.out_halves, r.out_eighths, r.out_summed)
        out_reduce.over_cores()
        unit_sums(T - 3)
    else:
        r.grad_out[...] = grad_out
    carry = exchange.carry()
    _, entering = fold(carry, factor_seg, finals, seg_masks, [None] * SEGMENTS)
    entering = entering[::-1]
    groups = tuple(
        tuple(
            jnp.concatenate([entering[group * 8 + sub][part] for sub in range(8)], 0)
            for part in range(2)
        )
        for group in range(GROUPS)
    )
    sums[...] = jnp.zeros_like(sums)

    def adjoint_step(step, carry, previous):
        new = []
        add_re = zero8
        add_im = zero8
        add_gamma = zero8
        for group in range(GROUPS):
            rows = rows_of(group, step)
            b = scan_step(carry[group], spread(keep_next[rows, :]), adjoint[rows, :], 1.0)
            new.append(b)
            adjoint[rows, :] = jnp.concatenate(b, 1)
            u = unpack(proj[rows, :])
            v = previous(group, step)
            mask = spread(keep[rows, :])
            add_re = add_re + mask * (b[0] * v[0] + b[1] * v[1])
            add_im = add_im + mask * (b[0] * v[1] - b[1] * v[0])
            add_gamma = add_gamma + b[0] * u[0] + b[1] * u[1]
        return tuple(new), (add_re, add_im, add_gamma)

    def adjoint_body(index, carry):
        values, totals = carry
        values, added = adjoint_step(
            L - 1 - index, values, lambda group, step: unpack(state[rows_of(group, step - 1), :])
        )
        return values, tuple(total + add for total, add in zip(totals, added))

    values, totals = lax.fori_loop(0, L - 1, adjoint_body, (groups, (zero8, zero8, zero8)))
    inside = entering_groups()
    _, added = adjoint_step(0, values, lambda group, step: inside[group])
    totals = [jnp.sum(total + add, 0, keepdims=True) for total, add in zip(totals, added)]

    if fused:
        out_reduce.over_plane()
    d_proj[...] = (adjoint[...] * gamma_signed).astype(BF16)
    grad_in = dot_tn(d_proj[...], normed[...]).astype(BF16)
    if fused:
        r.grad_rates[...] = grad_in
        divide(r.grad_rates, r.in_full)
        in_reduce = Reduce(place, r.in_full, r.in_halves, r.in_eighths, r.in_summed)
        in_reduce.over_cores()
        reduces[T - 1].turn_plane()
        unit_sums(T - 2)
        out_reduce.sum_plane()
        out_copies = links.send(
            r.out_sums,
            [
                (r.out_summed.at[i], r.out_sums.at[i - 1], (s, lax.rem(t + i, T)))
                for i in range(1, T)
            ],
        )
        in_reduce.over_plane()
        unit_sums(T - 1)
    else:
        r.grad_in[...] = grad_in

    @pl.loop(0, R // BLOCK)
    def _(tile):
        rows = block_rows(tile)
        d_m = d_mixed[rows, :].astype(F32)
        d_n = dot(d_proj[rows, :], w_in[...]) + d_m * skip_row
        c = centred[rows, :]
        sums[0:8, :] += jnp.sum((d_n * c).reshape(BLOCK // 8, 8, D), 0)
        sums[8:16, :] += jnp.sum((d_m * normed[rows, :].astype(F32)).reshape(BLOCK // 8, 8, D), 0)
        d_c = d_n * gain_row
        mean = jnp.mean(d_c, 1, keepdims=True)
        cross = jnp.mean(d_c * c, 1, keepdims=True)
        inv = inv_std[rows, 0:1]
        out = cot_in[rows, :].astype(F32) + inv * (d_c - mean - c * cross)
        high = out.astype(BF16)
        out = dot(turn[...], high) + dot(turn[...], (out - high.astype(F32)).astype(BF16))
        for run, piece in enumerate(pieces(tile)):
            grad_tokens[piece, :] = out[run * SEGMENTS : run * SEGMENTS + SEGMENTS]

    grad_copy = pltpu.make_async_copy(grad_tokens, r.grad_tokens, r.local_sem.at[1])
    grad_copy.start()
    small = r.small
    small_rows = [
        jnp.sum(sums[0:8, :], 0, keepdims=True),
        jnp.sum(sums[8:16, :], 0, keepdims=True),
        jnp.concatenate(totals[:2], 1),
        jnp.concatenate([totals[2] / gamma, jnp.zeros_like(gamma)], 1),
    ]
    if not fused:
        for k, row in enumerate(small_rows):
            small[k : k + 1, :] = row
        small[4:8, :] = jnp.zeros((4, D), F32)
        links.close()
        result_copy.wait()
        grad_copy.wait()
        return

    small_tp, small_seq = (r.small_tp, r.small_seq)
    small_tp[t] = jnp.concatenate([packed(row, D // 128) for row in small_rows], 0)
    small_copies = links.send(
        small_tp.at[pl.ds(0, T - 1)],
        [(small_tp.at[t], small_tp.at[t], (s, peer)) for peer in peers_tp],
    )

    def total_of(own, buffer):
        total = own.astype(F32)
        for k in range(buffer.shape[0]):
            total = total + buffer[k].astype(F32)
        return total.astype(BF16)

    unit_sum, out_sum, in_sum = (r.unit_sum, r.out_sum, r.in_sum)
    unit_copies.arrive()
    unit_sum[0, place.chip, place.core] = total_of(r.unit_summed[0, 0], r.unit_sums.at[:, 0])
    unit_spread = Spread(place, unit_sum)
    unit_spread.over_plane()

    in_reduce.sum_plane()
    in_copies = links.send(
        r.in_sums,
        [(r.in_summed.at[i], r.in_sums.at[i - 1], (s, lax.rem(t + i, T))) for i in range(1, T)],
    )
    out_copies.arrive()
    out_sum[0, place.chip, place.core] = total_of(r.out_summed[0], r.out_sums)
    out_spread = Spread(place, out_sum)
    out_spread.over_plane()

    small_copies.arrive()
    part = small_tp[0]
    for z in range(1, T):
        part = part + small_tp[z]
    small_seq[s] = part
    small_copies = links.send(
        small_seq.at[pl.ds(0, S - 1)],
        [(small_seq.at[s], small_seq.at[s], (peer, t)) for peer in peers_seq],
    )

    unit_spread.over_cores()
    in_copies.arrive()
    in_sum[0, place.chip, place.core] = total_of(r.in_summed[0], r.in_sums)
    in_spread = Spread(place, in_sum)
    in_spread.over_plane()
    out_spread.over_cores()

    unit_spread.finish()
    unit_copy = pltpu.make_async_copy(unit_sum.at[0], r.grad_units, r.local_sem.at[2])
    unit_copy.start()

    small_copies.arrive()
    part = small_seq[0]
    for block in range(1, S):
        part = part + small_seq[block]
    for k in range(4):
        height = D // 128
        small[k : k + 1, :] = unpacked(part[k * height : (k + 1) * height], height)
    small[4:8, :] = jnp.zeros((4, D), F32)

    out_spread.finish()
    out_copy = pltpu.make_async_copy(out_sum.at[0], r.grad_out, r.local_sem.at[3])
    out_copy.start()
    in_spread.over_cores()
    in_spread.finish()
    in_copy = pltpu.make_async_copy(in_sum.at[0], r.grad_in, r.local_sem.at[4])
    in_copy.start()
    for copy in (result_copy, grad_copy, unit_copy, out_copy, in_copy):
        copy.wait()
    links.close()


def finish_kernel(T, names, *refs):
    r = types.SimpleNamespace(**dict(zip(names, refs)))
    half = r.grad_rows.shape[0] // 2
    arrays = [(r.result_in, r.result_rows, r.result)] + [
        tuple(ref.at[pl.ds(at, half)] for ref in (r.grad_tokens_in, r.grad_rows, r.grad_tokens))
        for at in (0, half)
    ]
    fetched = [
        pltpu.make_async_copy(source, kept, r.local_sem.at[index])
        for index, (source, kept, _) in enumerate(arrays)
    ]
    copies = [
        pltpu.make_async_copy(kept, target, r.local_sem.at[index])
        for index, (_, kept, target) in enumerate(arrays)
    ]
    for copy in fetched:
        copy.start()
    for fetch, copy in zip(fetched, copies):
        fetch.wait()
        copy.start()
    D_rows, lanes = (r.glu.shape[3], r.glu.shape[4])
    r.glu[0] = r.units_in[:, :, 0:D_rows, :lanes].astype(F32)
    r.glu[1] = r.units_in[:, :, 0:D_rows, lanes:].astype(F32)
    r.down[...] = r.units_in[:, :, D_rows:, :].astype(F32)
    r.out[...] = r.out_in[...].astype(F32)
    r.in_[...] = r.in_in[...].astype(F32)
    r.gain[...] = r.small[0:1, :]
    r.skip[...] = r.small[1:2, :]
    n = r.decay_log.shape[1]
    N = T * n
    t = lax.axis_index("tp")

    def mine(row, first):
        own = row[:, first : first + n]
        for z in range(1, T):
            own = jnp.where(t == z, row[:, first + z * n : first + z * n + n], own)
        return own

    lam_re, lam_im, gamma = decay_terms(r.decay_log[...], r.angle[...])
    g_re = mine(r.small[2:3, :], 0)
    g_im = mine(r.small[2:3, :], N)
    g_gamma = mine(r.small[3:4, :], 0)
    rate_step = jnp.exp(r.decay_log[...])
    r.decay[...] = rate_step * (
        g_gamma * (1.0 - fall(2.0 * rate_step)) / gamma - g_re * lam_re - g_im * lam_im
    )
    r.turn[...] = g_im * lam_re - g_re * lam_im
    for copy in copies:
        copy.wait()


def fall(value):
    series = jnp.ones_like(value)
    for order in range(12, 1, -1):
        series = 1.0 - value / order * series
    return jnp.where(value < 0.5, value * series, 1.0 - jnp.exp(-value))


def decay_terms(decay_log, angle):
    rate_step = jnp.exp(decay_log)
    radius = 1.0 - fall(rate_step)
    return (radius * jnp.cos(angle), radius * jnp.sin(angle), jnp.sqrt(fall(2.0 * rate_step)))


def local(
    S,
    T,
    tokens,
    ln_gain,
    in_proj,
    decay_log,
    angle,
    out_proj,
    skip,
    glu_proj,
    down_proj,
    lengths,
    cotangent,
):
    R, D = tokens.shape
    n = in_proj.shape[2]
    N = n * T
    units = down_proj.shape[0]
    C = S // 2
    fused = (
        S == 8
        and T % 2 == 0
        and T > 2
        and 2 * n == 128
        and 2 * units == D
        and all(size % (16 * S) == 0 for size in (D, 2 * n, units))
    )
    vmem = pl.BlockSpec(memory_space=pltpu.VMEM)
    anywhere = pl.BlockSpec(memory_space=pl.ANY)
    hbm = pl.BlockSpec(memory_space=pltpu.HBM)
    ins = dict(
        lengths=(lengths, hbm),
        tokens=(tokens, hbm),
        cot=(cotangent, hbm),
        gain=(ln_gain.reshape(1, D), hbm),
        skip=(skip, hbm),
    )
    outs = dict(
        result=((R, D), BF16, anywhere),
        grad_tokens=((R, D), F32, anywhere),
        small=((8, D), F32, vmem),
    )
    scratch = dict(
        gain_row=((1, D), F32),
        skip_row=((D,), BF16),
        tokens_raw=((R, D), BF16),
        cot_raw=((R, D), BF16),
        turn=((BLOCK, BLOCK), BF16),
        tokens_in=((R, D), BF16),
        cot_in=((R, D), BF16),
        centred=((R, D), F32),
        inv_std=((R, 128), F32),
        normed=((R, D), BF16),
        proj=((R, 2 * N), F32),
        keep=((R, 128), F32),
        keep_next=((R, 128), F32),
        state=((R, 2 * N), F32),
        state_low=((R, 2 * N), BF16),
        act=((R, D), BF16),
        d_gelu=((R, D), F32),
        d_act=((R, D), F32),
        summed=((R, D), F32),
        d_mixed=((R, D), BF16),
        d_proj=((R, 2 * N), BF16),
        hidden=((R, units), BF16),
        d_unit=((R, 2 * units), BF16),
        seg_carry=((SEGMENTS, 2 * N), F32),
        sums=((16, D), F32),
        state_all=((T, S, 2 * N // 128, 128), F32),
        adj_all=((T, S, 2 * N // 128, 128), F32),
    )
    in_rows = in_proj.transpose(0, 2, 1)
    if fused:
        unit_rows = D // S + units // S
        ins.update(
            decay_log=(decay_log.reshape(1, n), hbm),
            angle=(angle.reshape(1, n), hbm),
            in_proj=(in_rows.reshape(C, 2, 2 * n // S, D), hbm),
            out_proj=(out_proj.reshape(C, 2, 2 * n // S, D), hbm),
            glu_proj=(glu_proj.reshape(2, C, 2, D // S, units), hbm),
            down_proj=(down_proj.reshape(C, 2, units // S, D), hbm),
        )
        outs.update(
            grad_in=((C, 2, 2 * n // S, D), BF16, anywhere),
            grad_out=((C, 2, 2 * n // S, D), BF16, anywhere),
            grad_units=((C, 2, unit_rows, D), BF16, anywhere),
        )

        def whole(parts, rows, lead=()):
            return (lead + (parts, C, 2, rows, D), BF16)

        def halves(parts, rows, lead=()):
            return (lead + (parts, C, rows, D), BF16)

        def eighths(parts, rows, lead=()):
            return (lead + (C - 1, parts, rows, D), BF16)

        def own(parts, rows, lead=()):
            return (lead + (parts, rows, D), BF16)

        unit_sizes = (1, unit_rows, (T,))
        rate_sizes = (T, 2 * n // S)
        scratch.update(
            w_in=((2 * N, D), BF16),
            w_out=((2 * N, D), BF16),
            rates_all=((T, 8, 128), F32),
            decay_row=((1, n), F32),
            angle_row=((1, n), F32),
            in_slices=((T, C, 2, 2 * n // S, D), BF16),
            out_slices=((T, C, 2, 2 * n // S, D), BF16),
            unit_slices=((T, C, 2, unit_rows, D), BF16),
            grad_rates=((2 * N, D), BF16),
            small_tp=((T, 16, 128), F32),
            small_seq=((S, 16, 128), F32),
            unit_sums=((T - 1, 1, unit_rows, D), BF16),
            out_sums=((T - 1, 2 * n // S, D), BF16),
            in_sums=((T - 1, 2 * n // S, D), BF16),
            unit_sum=((1, C, 2, unit_rows, D), BF16),
            out_sum=((1, C, 2, 2 * n // S, D), BF16),
            in_sum=((1, C, 2, 2 * n // S, D), BF16),
            unit_full=whole(*unit_sizes),
            unit_halves=halves(*unit_sizes),
            unit_eighths=eighths(*unit_sizes),
            unit_summed=own(*unit_sizes),
            out_full=whole(*rate_sizes),
            out_halves=halves(*rate_sizes),
            out_eighths=eighths(*rate_sizes),
            out_summed=own(*rate_sizes),
            in_full=whole(*rate_sizes),
            in_halves=halves(*rate_sizes),
            in_eighths=eighths(*rate_sizes),
            in_summed=own(*rate_sizes),
        )
        links = 19 + 8 * T
    else:
        w_in = lax.all_gather(in_rows, "tp", axis=1, tiled=True).reshape(2 * N, D)
        w_out = lax.all_gather(out_proj, "tp", axis=1, tiled=True).reshape(2 * N, D)
        glu = lax.all_gather(glu_proj, "tp")
        rates = jnp.stack(
            [lax.all_gather(part, "tp", tiled=True) for part in decay_terms(decay_log, angle)]
            + [jnp.zeros((N,), F32)] * 5
        )
        ins.update(
            rates=(rates, vmem),
            w_in=(w_in, vmem),
            w_out=(w_out, vmem),
            glu=(jnp.concatenate([glu[:, 0], glu[:, 1]], 2), vmem),
            down=(lax.all_gather(down_proj, "tp"), vmem),
        )
        outs.update(
            grad_in=((2 * N, D), BF16, vmem),
            grad_out=((2 * N, D), BF16, vmem),
            grad_glu=((T, D, 2 * units), BF16, vmem),
            grad_down=((T, units, D), BF16, vmem),
        )
        links = 2 * T
    names = [*ins, *outs, *scratch, *dict(counts=0, local_sem=0, send_sem=0, recv_sem=0)]
    results = pl.pallas_call(
        functools.partial(layer_kernel, S, T, fused, names),
        out_shape=tuple(jax.ShapeDtypeStruct(shape, dtype) for shape, dtype, _ in outs.values()),
        in_specs=[spec for _, spec in ins.values()],
        out_specs=tuple(spec for _, _, spec in outs.values()),
        scratch_shapes=[pltpu.VMEM(shape, dtype) for shape, dtype in scratch.values()]
        + [
            pltpu.SMEM(lengths.shape, jnp.int32),
            pltpu.SemaphoreType.DMA((12,)),
            pltpu.SemaphoreType.DMA((links,)),
            pltpu.SemaphoreType.DMA((links,)),
        ],
        compiler_params=pltpu.CompilerParams(
            collective_id=0, has_side_effects=True, vmem_limit_bytes=46 * 2**20
        ),
    )(
        *[
            pltpu.with_memory_space_constraint(value, pltpu.HBM) if spec is hbm else value
            for value, spec in ins.values()
        ]
    )
    if fused:
        result, grad_tokens, small, grad_in, grad_out, grad_units = results
        ins = dict(
            result_in=(result, anywhere),
            grad_tokens_in=(grad_tokens, anywhere),
            small=(small, vmem),
            in_in=(grad_in, vmem),
            out_in=(grad_out, vmem),
            units_in=(grad_units, vmem),
            decay_log=(decay_log.reshape(1, n), vmem),
            angle=(angle.reshape(1, n), vmem),
        )
        outs = dict(
            result=((R, D), BF16, anywhere),
            grad_tokens=((R, D), F32, anywhere),
            gain=((1, D), F32, vmem),
            in_=((C, 2, 2 * n // S, D), F32, vmem),
            decay=((1, n), F32, vmem),
            turn=((1, n), F32, vmem),
            out=((C, 2, 2 * n // S, D), F32, vmem),
            skip=((1, D), F32, vmem),
            glu=((2, C, 2, D // S, units), F32, vmem),
            down=((C, 2, units // S, D), F32, vmem),
        )
        scratch = dict(result_rows=((R, D), BF16), grad_rows=((R, D), F32))
        names = [*ins, *outs, *scratch, *dict(local_sem=0)]
        result, grad_tokens, gain, in_, decay, turn, out, skip_sum, glu, down = pl.pallas_call(
            functools.partial(finish_kernel, T, names),
            out_shape=tuple(
                jax.ShapeDtypeStruct(shape, dtype) for shape, dtype, _ in outs.values()
            ),
            in_specs=[spec for _, spec in ins.values()],
            out_specs=tuple(spec for _, _, spec in outs.values()),
            scratch_shapes=[pltpu.VMEM(shape, dtype) for shape, dtype in scratch.values()]
            + [pltpu.SemaphoreType.DMA((3,))],
            compiler_params=pltpu.CompilerParams(vmem_limit_bytes=16 * 2**20),
        )(*[value for value, _ in ins.values()])
        return (
            result,
            grad_tokens,
            gain.reshape(D),
            in_.reshape(2, n, D).transpose(0, 2, 1),
            decay.reshape(n),
            turn.reshape(n),
            out.reshape(2, n, D),
            skip_sum.reshape(D),
            glu.reshape(2, D, units),
            down.reshape(units, D),
        )
    result, grad_tokens, small, grad_in, grad_out, grad_glu, grad_down = results
    small = lax.psum(small, ("seq", "tp"))

    def reduced(part):
        part = lax.psum_scatter(part, "tp", scatter_dimension=0, tiled=True)
        return lax.psum(part, "seq").astype(F32)

    def by_tp(grad):
        return reduced(grad.reshape(2, T, n, D).transpose(1, 0, 2, 3).reshape(T * 2, n, D))

    grad_glu = reduced(grad_glu)[0].reshape(D, 2, units).transpose(1, 0, 2)
    grad_down = reduced(grad_down)[0]

    def mine(row):
        return lax.dynamic_slice_in_dim(row, lax.axis_index("tp") * n, n)

    g_re, g_im, g_gamma = (mine(small[2, :N]), mine(small[2, N:]), mine(small[3, :N]))
    _, pull = jax.vjp(decay_terms, decay_log, angle)
    grad_decay, grad_angle = pull((g_re, g_im, g_gamma))
    return (
        result,
        grad_tokens,
        small[0],
        by_tp(grad_in).transpose(0, 2, 1),
        grad_decay,
        grad_angle,
        by_tp(grad_out),
        small[1],
        grad_glu,
        grad_down,
    )


def solution(mesh):
    in_specs = (
        P(("seq", "tp"), None),
        P(),
        P(None, None, "tp"),
        P("tp"),
        P("tp"),
        P(None, "tp", None),
        P(),
        P(None, None, "tp"),
        P("tp", None),
        P(),
        P(("seq", "tp"), None),
    )
    out_specs = (
        P(("seq", "tp"), None),
        P(("seq", "tp"), None),
        P(),
        P(None, None, "tp"),
        P("tp"),
        P("tp"),
        P(None, "tp", None),
        P(),
        P(None, None, "tp"),
        P("tp", None),
    )
    return jax.shard_map(
        functools.partial(local, mesh.shape["seq"], mesh.shape["tp"]),
        mesh=mesh,
        in_specs=in_specs,
        out_specs=out_specs,
        check_vma=False,
    )
```

```python
import functools
import types
import jax
import jax.numpy as jnp
from jax import lax
from jax.experimental import pallas as pl
from jax.experimental.pallas import tpu as pltpu
from jax.sharding import PartitionSpec as P

epsilon = 1e-05
MESH = pl.DeviceIdType.MESH
F32 = jnp.float32
BF16 = jnp.bfloat16
GROUPS = 2
SEGMENTS = 8 * GROUPS
BLOCK = SEGMENTS * SEGMENTS


def dot(left, right):
    return jnp.dot(left, right, preferred_element_type=F32)


def dot_nt(left, right):
    return lax.dot_general(left, right, (((1,), (1,)), ((), ())), preferred_element_type=F32)


def complex_mul(left_re, left_im, right_re, right_im):
    return (left_re * right_re - left_im * right_im, left_re * right_im + left_im * right_re)


def dot_tn(left, right):
    return lax.dot_general(left, right, (((0,), (0,)), ((), ())), preferred_element_type=F32)


def power(base, exponent):
    result = None
    square = base
    while exponent:
        if exponent & 1:
            result = square if result is None else complex_mul(*result, *square)
        exponent >>= 1
        if exponent:
            square = complex_mul(*square, *square)
    return result


class Links:
    def __init__(self, send_sem, recv_sem):
        self.send_sem = send_sem
        self.recv_sem = recv_sem
        self.groups = []

    def group(self, whole):
        group = Group(self, len(self.groups), whole)
        self.groups.append(group)
        return group

    def send(self, whole, copies):
        group = self.group(whole)
        for source, target, device in copies:
            group.add(source, target, device)
        return group

    def close(self):
        for group in self.groups:
            group.last.wait_send()


class Group:
    def __init__(self, links, index, whole):
        self.links = links
        self.index = index
        self.whole = whole

    def copy(self, source, target, device):
        return pltpu.make_async_remote_copy(
            src_ref=source,
            dst_ref=target,
            send_sem=self.links.send_sem.at[self.index],
            recv_sem=self.links.recv_sem.at[self.index],
            device_id=device,
            device_id_type=MESH,
        )

    def add(self, source, target, device):
        self.copy(source, target, device).start()
        self.last = self.copy(self.whole, self.whole, device)

    def arrive(self):
        self.last.wait_recv()


class Gather:
    def __init__(self, place, buffer, first, last):
        self.place = place
        self.buffer = buffer
        self.slots = range(first, last)
        self.part = buffer.at[pl.ds(first, last - first)]

    def over_tp(self):
        p = self.place
        self.copies = p.links.send(
            self.part.at[:, p.chip, p.core],
            [
                (
                    self.buffer.at[0, p.chip, p.core],
                    self.buffer.at[slot, p.chip, p.core],
                    (p.s, lax.rem(p.t + p.T - slot, p.T)),
                )
                for slot in self.slots
            ],
        )

    def over_plane(self):
        p = self.place
        self.copies.arrive()
        mine = self.part.at[:, p.chip, p.core]
        self.copies = p.links.send(
            self.part.at[:, pl.ds(0, len(p.chips)), p.core],
            [(mine, mine, device) for _, device in p.chips],
        )

    def over_cores(self):
        p = self.place
        self.copies.arrive()
        mine = self.part.at[:, :, p.core]
        self.copies = p.links.send(mine, [(mine, mine, p.sibling)])

    def finish(self):
        self.copies.arrive()


class Reduce:
    def __init__(self, place, full, halves, eighths, summed):
        self.place = place
        self.full = full
        self.halves = halves
        self.eighths = eighths
        self.summed = summed

    def over_cores(self):
        p = self.place
        self.copies = p.links.send(
            self.halves, [(self.full.at[:, :, 1 - p.core], self.halves, p.sibling)]
        )

    def over_plane(self):
        p = self.place
        self.copies.arrive()
        parts, chips = self.halves.shape[:2]

        @pl.loop(0, parts * chips)
        def _(index):
            part, chip = (lax.div(index, chips), lax.rem(index, chips))
            self.halves[part, chip] = (
                self.full[part, chip, p.core].astype(F32) + self.halves[part, chip].astype(F32)
            ).astype(BF16)

        self.copies = p.links.send(
            self.eighths,
            [
                (self.halves.at[:, chip], self.eighths.at[k], device)
                for k, (chip, device) in enumerate(p.chips)
            ],
        )

    def sum_plane(self):
        p = self.place
        self.copies.arrive()

        @pl.loop(0, self.halves.shape[0])
        def _(part):
            total = self.halves[part, p.chip].astype(F32)
            for k in range(len(p.chips)):
                total = total + self.eighths[k, part].astype(F32)
            self.summed[part] = total.astype(BF16)


class Reduce2(Reduce):
    def __init__(self, place, full, halves, eighths, summed):
        super().__init__(place, full, halves, eighths, summed)
        self.rows = halves.shape[2] // 2
        self.ours = halves.at[:, :, pl.ds(0, self.rows)]
        self.theirs = halves.at[:, :, pl.ds(self.rows, self.rows)]

    def sum_cores(self, chip):
        self.halves[0, chip] = (
            self.full[0, chip, self.place.core].astype(F32) + self.halves[0, chip].astype(F32)
        ).astype(BF16)

    def over_plane(self):
        p = self.place
        self.copies.arrive()
        self.sum_cores(p.by_x)
        self.sum_cores(p.by_y)
        self.sum_cores(p.by_xy)
        self.copies = p.links.send(
            self.eighths.at[pl.ds(0, 2)],
            [
                (part.at[0, chip], self.eighths.at[index, 0, rows], device)
                for index, part, chip, rows, device in (
                    (0, self.ours, p.by_x, pl.ds(0, self.rows), p.x_device),
                    (1, self.ours, p.by_xy, pl.ds(0, self.rows), p.x_device),
                    (0, self.theirs, p.by_y, pl.ds(self.rows, self.rows), p.y_device),
                    (1, self.theirs, p.by_xy, pl.ds(self.rows, self.rows), p.y_device),
                )
            ],
        )
        self.sum_cores(p.chip)

    def turn_plane(self):
        p = self.place
        self.copies.arrive()
        n = self.rows
        for index, chip in ((0, p.chip), (1, p.by_y)):
            self.halves[0, chip, 0:n] = (
                self.halves[0, chip, 0:n].astype(F32) + self.eighths[index, 0, 0:n].astype(F32)
            ).astype(BF16)
        for index, chip in ((0, p.chip), (1, p.by_x)):
            self.halves[0, chip, n:] = (
                self.halves[0, chip, n:].astype(F32) + self.eighths[index, 0, n:].astype(F32)
            ).astype(BF16)
        self.copies = p.links.send(
            self.eighths.at[2],
            [
                (self.ours.at[0, p.by_y], self.eighths.at[2, 0, pl.ds(0, n)], p.y_device),
                (self.theirs.at[0, p.by_x], self.eighths.at[2, 0, pl.ds(n, n)], p.x_device),
            ],
        )

    def sum_plane(self):
        p = self.place
        self.copies.arrive()
        self.summed[0] = (
            self.halves[0, p.chip].astype(F32) + self.eighths[2, 0].astype(F32)
        ).astype(BF16)


class Spread:
    def __init__(self, place, buffer):
        self.place = place
        self.buffer = buffer

    def over_plane(self):
        p = self.place
        mine = self.buffer.at[:, p.chip, p.core]
        self.copies = p.links.send(
            self.buffer.at[:, pl.ds(0, len(p.chips)), p.core],
            [(mine, mine, device) for _, device in p.chips],
        )

    def over_cores(self):
        p = self.place
        self.copies.arrive()
        mine = self.buffer.at[:, :, p.core]
        self.copies = p.links.send(mine, [(mine, mine, p.sibling)])

    def finish(self):
        self.copies.arrive()


class Place:
    def __init__(self, S, T, links):
        self.S, self.T, self.links = (S, T, links)
        self.s = lax.axis_index("seq")
        self.t = lax.axis_index("tp")
        C = S // 2
        self.core = lax.rem(self.s, 2)
        self.chip = lax.div(self.s, 2)
        self.sibling = (self.chip * 2 + 1 - self.core, self.t)
        x = lax.rem(self.chip, 2)
        y = lax.div(self.chip, 2)
        self.by_x = y * 2 + 1 - x
        self.by_y = (1 - y) * 2 + x
        self.by_xy = (1 - y) * 2 + 1 - x
        self.x_device = (self.by_x * 2 + self.core, self.t)
        self.y_device = (self.by_y * 2 + self.core, self.t)
        self.chips = []
        for k in range(1, C):
            chip = lax.rem(self.chip + k, C)
            self.chips.append((chip, (chip * 2 + self.core, self.t)))


def layer_kernel(S, T, fused, names, *refs):
    r = types.SimpleNamespace(**dict(zip(names, refs)))
    links = Links(r.send_sem, r.recv_sem)
    place = Place(S, T, links)
    lengths = r.counts
    tokens = r.tokens_raw
    cot = r.cot_raw
    result = r.tokens_raw
    grad_tokens = r.d_gelu
    turn = r.turn
    tokens_in = r.tokens_in
    cot_in = r.cot_in
    centred = r.centred
    inv_std = r.inv_std
    normed = r.normed
    proj = r.proj
    keep = r.keep
    keep_next = r.keep_next
    state = r.state
    state_low = r.state_low
    act = r.act
    d_gelu = r.d_gelu
    d_act = r.d_act
    summed = r.summed
    d_mixed = r.d_mixed
    adjoint = r.summed
    d_proj = r.d_proj
    hidden = r.hidden
    d_unit = r.d_unit
    seg_carry, sums = (r.seg_carry, r.sums)
    w_in, w_out = (r.w_in, r.w_out)
    R, D = tokens.shape
    N = w_in.shape[0] // 2
    n = N // T
    L = R // SEGMENTS
    s = place.s
    t = place.t
    first = (s * T + t) * R

    peers_tp = [lax.rem(t + k, T) for k in range(1, T)]
    peers_seq = [lax.rem(s + k, S) for k in range(1, S)]
    barrier = pltpu.get_barrier_semaphore()
    for peer in peers_tp:
        pl.semaphore_signal(barrier, inc=1, device_id=(s, peer), device_id_type=MESH)
    for peer in peers_seq:
        pl.semaphore_signal(barrier, inc=1, device_id=(peer, t), device_id_type=MESH)

    fetched = [
        pltpu.make_async_copy(source, target, r.local_sem.at[index])
        for index, (source, target) in enumerate(
            ((r.tokens, tokens), (r.cot, cot), (r.gain, r.gain_row), (r.skip, r.skip_row), (r.lengths, r.counts))
        )
    ]
    if fused:
        in_slices, out_slices, unit_slices = (r.in_slices, r.out_slices, r.unit_slices)
        units = r.down_proj.shape[2] * S
        D_rows = r.glu_proj.shape[3]
        gated_rows = unit_slices.at[0, :, :, pl.ds(0, D_rows)]
        weights = [
            pltpu.make_async_copy(source, target, r.local_sem.at[5 + index])
            for index, (source, target) in enumerate(
                (
                    (r.decay_log, r.decay_row),
                    (r.angle, r.angle_row),
                    (r.in_proj, in_slices.at[0]),
                    (r.out_proj, out_slices.at[0]),
                    (r.glu_proj.at[0], gated_rows.at[:, :, :, pl.ds(0, units)]),
                    (r.glu_proj.at[1], gated_rows.at[:, :, :, pl.ds(units, units)]),
                    (r.down_proj, unit_slices.at[0, :, :, pl.ds(D_rows, units // S)]),
                )
            )
        ]
        for copy in weights:
            copy.start()
    for copy in fetched:
        copy.start()
    if fused:
        rates_all = r.rates_all
        rates_all[t] = jnp.zeros(rates_all.shape[1:], F32)
        gather_in = Gather(place, in_slices, 1, T)
        gather_out = Gather(place, out_slices, 1, T)
        gather_units = [Gather(place, unit_slices, slot, slot + 1) for slot in range(1, T)]
        for copy in weights:
            copy.wait()
        for index, row in enumerate(decay_terms(r.decay_row[...], r.angle_row[...])):
            rates_all[t, index : index + 1, 0:n] = row
        pl.semaphore_wait(barrier, T - 1 + S - 1)
        gather_in.over_tp()
        rate_copies = links.send(
            rates_all.at[pl.ds(0, T - 1)],
            [(rates_all.at[t], rates_all.at[t], (s, peer)) for peer in peers_tp],
        )

    for copy in fetched[2:]:
        copy.wait()
    starts = []
    total = jnp.int32(0)
    for index in range(lengths.shape[0]):
        starts.append(total)
        total = total + lengths[index]

    def keeps(position):
        hit = position == starts[0]
        for start in starts[1:]:
            hit = hit | (position == start)
        return jnp.where(hit, 0.0, 1.0)

    def clear(low, high):
        hit = (starts[0] >= low) & (starts[0] < high)
        for start in starts[1:]:
            hit = hit | ((start >= low) & (start < high))
        return jnp.where(hit, 0.0, 1.0)

    gain_row = r.gain_row[...]
    skip_row = r.skip_row[...].astype(F32).reshape(1, D)

    down_index = lax.broadcasted_iota(jnp.int32, (BLOCK, BLOCK), 0)
    across_index = lax.broadcasted_iota(jnp.int32, (BLOCK, BLOCK), 1)
    turned = lax.rem(down_index, SEGMENTS) * SEGMENTS + lax.div(down_index, SEGMENTS)
    turn[...] = jnp.where(turned == across_index, 1.0, 0.0).astype(BF16)

    def pieces(block):
        return [
            pl.ds(pl.multiple_of(run * L + block * SEGMENTS, SEGMENTS), SEGMENTS)
            for run in range(SEGMENTS)
        ]

    def taken(ref, block):
        return dot(turn[...], jnp.concatenate([ref[piece, :] for piece in pieces(block)], 0))

    def block_rows(tile):
        return pl.ds(pl.multiple_of(tile * BLOCK, BLOCK), BLOCK)

    def norm_tile(tile):
        rows = block_rows(tile)
        x = taken(tokens, tile)
        tokens_in[rows, :] = x.astype(BF16)
        mean = jnp.mean(x, 1, keepdims=True)
        inv = lax.rsqrt(jnp.mean(x * x, 1, keepdims=True) - mean * mean + epsilon)
        c = (x - mean) * inv
        centred[rows, :] = c
        inv_std[rows, :] = jnp.broadcast_to(inv, (BLOCK, 128))
        n_rows = (c * gain_row).astype(BF16)
        normed[rows, :] = n_rows

    def cot_tile(tile):
        rows = block_rows(tile)
        cot_rows = taken(cot, tile).astype(BF16)
        cot_in[rows, :] = cot_rows
        index = tile * BLOCK + lax.broadcasted_iota(jnp.int32, (BLOCK, 128), 0)
        position = first + lax.rem(index, SEGMENTS) * L + lax.div(index, SEGMENTS)
        keep[rows, :] = keeps(position)
        keep_next[rows, :] = keeps(position + 1)

    fetched[0].wait()
    pl.loop(0, R // BLOCK)(norm_tile)
    if fused:
        gather_in.over_plane()
        gather_out.over_tp()
        gather_units[0].over_tp()
    fetched[1].wait()
    pl.loop(0, R // BLOCK)(cot_tile)

    def assemble(slices, weight):
        for i in range(T):
            at = lax.rem(t + i, T) * n
            for part in range(2):
                weight[pl.ds(pl.multiple_of(part * N + at, n), n), :] = slices[
                    i, part * (S // 4) : (part + 1) * (S // 4)
                ].reshape(n, D)

    if fused:
        gather_in.over_cores()
        gather_units[1].over_tp()
        rate_copies.arrive()
        half = lax.broadcasted_iota(jnp.int32, (8, 128), 1) < n
        rate_rows = [rates_all[z] for z in range(T)]
        joined = jnp.concatenate(
            [
                jnp.where(half, rate_rows[z], pltpu.roll(rate_rows[z + 1], n, 1))
                for z in range(0, T, 2)
            ],
            1,
        )
        lam_re, lam_im, gamma = (joined[k : k + 1] for k in range(3))
        gather_in.finish()
        for gather in gather_units[2:]:
            gather.over_tp()
        gather_out.over_plane()
        assemble(in_slices, w_in)
    else:
        pl.semaphore_wait(barrier, T - 1 + S - 1)
        lam_re, lam_im, gamma = (r.rates[k : k + 1, :] for k in range(3))
    gamma_signed = jnp.concatenate([gamma, -gamma], 1)

    @pl.loop(0, R // BLOCK)
    def _(tile):
        rows = block_rows(tile)
        proj[rows, :] = dot_nt(normed[rows, :], w_in[...]) * gamma_signed

    low8_re = jnp.broadcast_to(lam_re, (8, N))
    low8_im = jnp.broadcast_to(lam_im, (8, N))

    def rows_of(group, step):
        return pl.ds(pl.multiple_of(step * SEGMENTS + group * 8, 8), 8)

    def spread(row):
        return jnp.concatenate([row] * (N // 128), 1)

    def scan_step(values, mask, add, sign):
        new_re, new_im = complex_mul(low8_re, sign * low8_im, *(value * mask for value in values))
        return (new_re + add[:, :N], new_im + add[:, N:])

    zero8 = jnp.zeros((8, N), F32)
    none = tuple((zero8, zero8) for _ in range(GROUPS))

    def forward_step(step, carry):
        return tuple(
            scan_step(
                carry[group],
                spread(keep[rows_of(group, step), :]),
                proj[rows_of(group, step), :],
                -1.0,
            )
            for group in range(GROUPS)
        )

    def segment_rows(finals):
        return [
            (finals[group][0][sub : sub + 1], finals[group][1][sub : sub + 1])
            for group in range(GROUPS)
            for sub in range(8)
        ]

    def fold(start, factor, items, masks, taken):
        before = []
        carry = start
        for (item_re, item_im), mask, take in zip(items, masks, taken):
            before.append(carry)
            moved = complex_mul(*factor, *carry)
            longer = (moved[0] * mask + item_re, moved[1] * mask + item_im)
            if take is None:
                carry = longer
            else:
                carry = tuple(jnp.where(take, new, old) for new, old in zip(longer, carry))
        return carry, before

    zero1 = (jnp.zeros((1, N), F32), jnp.zeros((1, N), F32))
    lam = (lam_re, lam_im)
    conj = (lam_re, -lam_im)

    def unpack(row):
        return (row[:, :N], row[:, N:])

    def packed(row, height):
        parts = [row[:, at : at + 128] for at in range(0, row.shape[1], 128)]
        return jnp.concatenate(parts + [parts[0]] * (height - len(parts)), 0)

    def unpacked(tile, height):
        return jnp.concatenate([tile[k : k + 1, :] for k in range(height)], 1)

    class Exchange:
        def __init__(self, own, factor, buffer, forward):
            self.forward = forward
            self.shift = 0 if forward else 1
            self.factor = power(factor, R)
            self.buffer = buffer
            buffer[t, s] = packed(jnp.concatenate(own, 1), 2 * N // 128)
            mine = buffer.at[t, s]
            self.copies = [
                links.send(
                    buffer.at[0], [(mine, mine, (peer, peer_tp)) for peer in [s, *peers_seq]]
                )
                for peer_tp in peers_tp
            ]
            self.copies.append(
                links.send(
                    buffer.at[0, pl.ds(0, S - 1)], [(mine, mine, (peer, t)) for peer in peers_seq]
                )
            )

        def carry(self):
            for copies in self.copies:
                copies.arrive()

            def order(count):
                return list(range(count)) if self.forward else list(range(count))[::-1]

            def ahead(block, z):
                mine, other = (s * T + t, block * T + z)
                return other < mine if self.forward else other > mine

            rows = [
                jnp.concatenate(
                    [unpacked(self.buffer[z, block], 2 * N // 128) for block in range(S)], 0
                )
                for z in range(T)
            ]
            block = lax.broadcasted_iota(jnp.int32, (S, N), 0)
            carry = (jnp.zeros((S, N), F32), jnp.zeros((S, N), F32))
            for z in order(T):
                low = (block * T + z) * R + self.shift
                mask = clear(low, low + R)
                item = (rows[z][:, :N], rows[z][:, N:])
                moved = complex_mul(*self.factor, *carry)
                longer = (moved[0] * mask + item[0], moved[1] * mask + item[1])
                mine = block == s
                taken = jnp.logical_or(jnp.logical_not(mine), ahead(s, z))
                carry = tuple(jnp.where(taken, new, old) for new, old in zip(longer, carry))
            result = zero1
            whole = power(self.factor, T)
            for b in order(S):
                low = b * T * R + self.shift
                mask = clear(low, low + T * R)
                moved = complex_mul(*whole, *result)
                longer = (
                    moved[0] * mask + carry[0][b : b + 1],
                    moved[1] * mask + carry[1][b : b + 1],
                )
                earlier = b < s if self.forward else b > s
                result = tuple(jnp.where(earlier, new, old) for new, old in zip(longer, result))
            inside = tuple(
                jnp.sum(jnp.where(block == s, part, 0.0), 0, keepdims=True) for part in carry
            )
            for z in order(T):
                low = (s * T + z) * R + self.shift
                mask = clear(low, low + R)
                moved = complex_mul(*self.factor, *result)
                longer = (moved[0] * mask, moved[1] * mask)
                result = tuple(
                    jnp.where(ahead(s, z), new, old) for new, old in zip(longer, result)
                )
            return (result[0] + inside[0], result[1] + inside[1])

    finals = segment_rows(lax.fori_loop(0, L, forward_step, none))
    seg_masks = [clear(first + index * L, first + (index + 1) * L) for index in range(SEGMENTS)]
    factor_seg = power(conj, L)
    own, _ = fold(zero1, factor_seg, finals, seg_masks, [None] * SEGMENTS)
    exchange = Exchange(own, conj, r.state_all, True)
    if fused:
        gather_units[0].over_plane()
        gather_out.over_cores()
    if fused:
        gather_units[1].over_plane()
        gather_out.finish()
        assemble(out_slices, w_out)
    carry = exchange.carry()
    _, entering = fold(carry, factor_seg, finals, seg_masks, [None] * SEGMENTS)
    for index, (row_re, row_im) in enumerate(entering):
        seg_carry[index : index + 1, :] = jnp.concatenate([row_re, row_im], 1)

    def write_state(step, carry):
        new = forward_step(step, carry)
        for group in range(GROUPS):
            state[rows_of(group, step), :] = jnp.concatenate(new[group], 1)
        return new

    def entering_groups():
        return tuple(
            unpack(seg_carry[group * 8 : group * 8 + 8, :]) for group in range(GROUPS)
        )

    lax.fori_loop(0, L, write_state, entering_groups())
    if fused:
        for gather in gather_units[2:]:
            gather.over_plane()

    @pl.loop(0, R // BLOCK)
    def _(tile):
        rows = block_rows(tile)
        low = state[rows, :].astype(BF16)
        state_low[rows, :] = low
        x = dot(low, w_out[...]) + skip_row * normed[rows, :].astype(F32)
        scale = 0.7978845608028654
        th = jnp.tanh(scale * (x + 0.044715 * x * x * x))
        half = 0.5 * (1.0 + th)
        a = (x * half).astype(BF16)
        act[rows, :] = a
        d_act[rows, :] = x
        summed[rows, :] = half

    if fused:
        reduces = [
            Reduce2(
                place,
                r.unit_full.at[i],
                r.unit_halves.at[i],
                r.unit_eighths.at[i],
                r.unit_summed.at[i],
            )
            for i in range(T)
        ]

    UNIT_ROWS = min(512, R)
    units = hidden.shape[1]
    unit_copies = links.group(r.unit_sums) if fused else None

    def unit_grads(i):
        c = lax.rem(t + i, T)
        gated_grad = dot_tn(act[...], d_unit[...]).astype(BF16)
        down_grad = dot_tn(hidden[...], cot_in[...]).astype(BF16)
        if fused:
            full = r.unit_full
            full[i, 0, :, :, 0:D_rows] = gated_grad.reshape(S // 2, 2, D_rows, 2 * units)
            full[i, 0, :, :, D_rows:] = down_grad.reshape(S // 2, 2, units // S, D)
            reduces[i].over_cores()
        else:
            r.grad_glu[c] = gated_grad
            r.grad_down[c] = down_grad

    def unit_sums(i):
        reduces[i].sum_plane()
        if i > 0:
            unit_copies.add(r.unit_summed.at[i], r.unit_sums.at[i - 1], (s, lax.rem(t + i, T)))

    for i in range(T):
        c = lax.rem(t + i, T)
        if fused:
            if i > 0:
                gather_units[i - 1].finish()
            if i < T - 1:
                gather_units[i].over_cores()
            w_gated = unit_slices[i, :, :, 0:D_rows].reshape(D, 2 * units)
            w_down = unit_slices[i, :, :, D_rows:].reshape(units, D)
        else:
            w_gated = r.glu[c]
            w_down = r.down[c]

        for tile in range(R // UNIT_ROWS):
            rows = slice(tile * UNIT_ROWS, (tile + 1) * UNIT_ROWS)
            both = dot(act[rows, :], w_gated)
            if i == 0:
                x = d_act[rows, :]
                half = summed[rows, :]
                slope = 1.5957691216057308 * (1.0 + 0.134145 * x * x)
                d_gelu[rows, :] = half + x * half * (1.0 - half) * slope
            value, gate = (both[:, :units], both[:, units:])
            sigma = 0.5 * jnp.tanh(0.5 * gate) + 0.5
            gated = value * sigma
            h = gated.astype(BF16)
            hidden[rows, :] = h
            d_h = dot_nt(cot_in[rows, :], w_down)
            d_both = jnp.concatenate(
                [(d_h * sigma).astype(BF16), (d_h * gated * (1.0 - sigma)).astype(BF16)], 1
            )
            d_unit[rows, :] = d_both
            added = dot(h, w_down)
            d_a = dot_nt(d_both, w_gated)
            if i > 0:
                added = added + summed[rows, :]
                d_a = d_a + d_act[rows, :]
            if i < T - 1:
                summed[rows, :] = added
                d_act[rows, :] = d_a
            else:
                d_m = (d_gelu[rows, :] * d_a).astype(BF16)
                d_mixed[rows, :] = d_m
                adjoint[rows, :] = dot_nt(d_m, w_out[...])
                out = (tokens_in[rows, :].astype(F32) + added).astype(BF16)
                for block in range(UNIT_ROWS // BLOCK):
                    turned = dot(turn[...], out[block * BLOCK : block * BLOCK + BLOCK])
                    turned = turned.astype(BF16)
                    for run, piece in enumerate(pieces(tile * (UNIT_ROWS // BLOCK) + block)):
                        result[piece, :] = turned[run * SEGMENTS : run * SEGMENTS + SEGMENTS]

        if fused and i > 0:
            reduces[i - 1].over_plane()
        unit_grads(i)
        if fused and i > 1:
            reduces[i - 2].turn_plane()
        if fused and i > 2:
            unit_sums(i - 3)

    result_copy = pltpu.make_async_copy(result, r.result, r.local_sem.at[0])
    result_copy.start()

    def backward_step(index, carry):
        step = L - 1 - index
        return tuple(
            scan_step(
                carry[group],
                spread(keep_next[rows_of(group, step), :]),
                adjoint[rows_of(group, step), :],
                1.0,
            )
            for group in range(GROUPS)
        )

    finals = segment_rows(lax.fori_loop(0, L, backward_step, none))[::-1]
    seg_masks = [
        clear(first + index * L + 1, first + (index + 1) * L + 1) for index in range(SEGMENTS)
    ][::-1]
    factor_seg = power(lam, L)
    own, _ = fold(zero1, factor_seg, finals, seg_masks, [None] * SEGMENTS)
    exchange = Exchange(own, lam, r.adj_all, False)
    if fused:
        reduces[T - 2].turn_plane()
        reduces[T - 1].over_plane()
    grad_out = dot_tn(state_low[...], d_mixed[...]).astype(BF16)

    def divide(grad, full):
        for i in range(T):
            at = lax.rem(t + i, T) * n
            for part in range(2):
                rows = pl.ds(pl.multiple_of(part * N + at, n), n)
                full[i, part * (S // 4) : (part + 1) * (S // 4)] = grad[rows, :].reshape(
                    S // 4, 2, -1, D
                )

    if fused:
        r.grad_rates[...] = grad_out
        divide(r.grad_rates, r.out_full)
        out_reduce = Reduce(place, r.out_full, r.out_halves, r.out_eighths, r.out_summed)
        out_reduce.over_cores()
        unit_sums(T - 3)
    else:
        r.grad_out[...] = grad_out
    carry = exchange.carry()
    if fused:
        reduces[T - 1].turn_plane()
        out_reduce.over_plane()
    _, entering = fold(carry, factor_seg, finals, seg_masks, [None] * SEGMENTS)
    entering = entering[::-1]
    groups = tuple(
        tuple(
            jnp.concatenate([entering[group * 8 + sub][part] for sub in range(8)], 0)
            for part in range(2)
        )
        for group in range(GROUPS)
    )
    sums[...] = jnp.zeros_like(sums)

    def adjoint_step(step, carry, previous):
        new = []
        add_re = zero8
        add_im = zero8
        add_gamma = zero8
        for group in range(GROUPS):
            rows = rows_of(group, step)
            b = scan_step(carry[group], spread(keep_next[rows, :]), adjoint[rows, :], 1.0)
            new.append(b)
            adjoint[rows, :] = jnp.concatenate(b, 1)
            u = unpack(proj[rows, :])
            v = previous(group, step)
            mask = spread(keep[rows, :])
            add_re = add_re + mask * (b[0] * v[0] + b[1] * v[1])
            add_im = add_im + mask * (b[0] * v[1] - b[1] * v[0])
            add_gamma = add_gamma + b[0] * u[0] + b[1] * u[1]
        return tuple(new), (add_re, add_im, add_gamma)

    def adjoint_body(index, carry):
        values, totals = carry
        values, added = adjoint_step(
            L - 1 - index, values, lambda group, step: unpack(state[rows_of(group, step - 1), :])
        )
        return values, tuple(total + add for total, add in zip(totals, added))

    values, totals = lax.fori_loop(0, L - 1, adjoint_body, (groups, (zero8, zero8, zero8)))
    inside = entering_groups()
    _, added = adjoint_step(0, values, lambda group, step: inside[group])
    totals = [jnp.sum(total + add, 0, keepdims=True) for total, add in zip(totals, added)]

    d_proj[...] = (adjoint[...] * gamma_signed).astype(BF16)
    grad_in = dot_tn(d_proj[...], normed[...]).astype(BF16)
    if fused:
        r.grad_rates[...] = grad_in
        divide(r.grad_rates, r.in_full)
        in_reduce = Reduce(place, r.in_full, r.in_halves, r.in_eighths, r.in_summed)
        in_reduce.over_cores()
        unit_sums(T - 2)
        out_reduce.sum_plane()
        out_copies = links.send(
            r.out_sums,
            [
                (r.out_summed.at[i], r.out_sums.at[i - 1], (s, lax.rem(t + i, T)))
                for i in range(1, T)
            ],
        )
        in_reduce.over_plane()
        unit_sums(T - 1)
    else:
        r.grad_in[...] = grad_in

    @pl.loop(0, R // BLOCK)
    def _(tile):
        rows = block_rows(tile)
        d_m = d_mixed[rows, :].astype(F32)
        d_n = dot(d_proj[rows, :], w_in[...]) + d_m * skip_row
        c = centred[rows, :]
        sums[0:8, :] += jnp.sum((d_n * c).reshape(BLOCK // 8, 8, D), 0)
        sums[8:16, :] += jnp.sum((d_m * normed[rows, :].astype(F32)).reshape(BLOCK // 8, 8, D), 0)
        d_c = d_n * gain_row
        mean = jnp.mean(d_c, 1, keepdims=True)
        cross = jnp.mean(d_c * c, 1, keepdims=True)
        inv = inv_std[rows, 0:1]
        out = cot_in[rows, :].astype(F32) + inv * (d_c - mean - c * cross)
        high = out.astype(BF16)
        out = dot(turn[...], high) + dot(turn[...], (out - high.astype(F32)).astype(BF16))
        for run, piece in enumerate(pieces(tile)):
            grad_tokens[piece, :] = out[run * SEGMENTS : run * SEGMENTS + SEGMENTS]

    grad_copy = pltpu.make_async_copy(grad_tokens, r.grad_tokens, r.local_sem.at[1])
    grad_copy.start()
    small = r.small
    small_rows = [
        jnp.sum(sums[0:8, :], 0, keepdims=True),
        jnp.sum(sums[8:16, :], 0, keepdims=True),
        jnp.concatenate(totals[:2], 1),
        jnp.concatenate([totals[2] / gamma, jnp.zeros_like(gamma)], 1),
    ]
    if not fused:
        for k, row in enumerate(small_rows):
            small[k : k + 1, :] = row
        small[4:8, :] = jnp.zeros((4, D), F32)
        links.close()
        result_copy.wait()
        grad_copy.wait()
        return

    small_tp, small_seq = (r.small_tp, r.small_seq)
    small_tp[t] = jnp.concatenate([packed(row, D // 128) for row in small_rows], 0)
    small_copies = links.send(
        small_tp.at[pl.ds(0, T - 1)],
        [(small_tp.at[t], small_tp.at[t], (s, peer)) for peer in peers_tp],
    )

    def total_of(own, buffer):
        total = own.astype(F32)
        for k in range(buffer.shape[0]):
            total = total + buffer[k].astype(F32)
        return total.astype(BF16)

    unit_sum, out_sum, in_sum = (r.unit_sum, r.out_sum, r.in_sum)
    unit_copies.arrive()
    unit_sum[0, place.chip, place.core] = total_of(r.unit_summed[0, 0], r.unit_sums.at[:, 0])
    unit_spread = Spread(place, unit_sum)
    unit_spread.over_plane()

    in_reduce.sum_plane()
    in_copies = links.send(
        r.in_sums,
        [(r.in_summed.at[i], r.in_sums.at[i - 1], (s, lax.rem(t + i, T))) for i in range(1, T)],
    )
    out_copies.arrive()
    out_sum[0, place.chip, place.core] = total_of(r.out_summed[0], r.out_sums)
    out_spread = Spread(place, out_sum)
    out_spread.over_plane()

    small_copies.arrive()
    part = small_tp[0]
    for z in range(1, T):
        part = part + small_tp[z]
    small_seq[s] = part
    small_copies = links.send(
        small_seq.at[pl.ds(0, S - 1)],
        [(small_seq.at[s], small_seq.at[s], (peer, t)) for peer in peers_seq],
    )

    unit_spread.over_cores()
    in_copies.arrive()
    in_sum[0, place.chip, place.core] = total_of(r.in_summed[0], r.in_sums)
    in_spread = Spread(place, in_sum)
    in_spread.over_plane()
    out_spread.over_cores()

    unit_spread.finish()
    unit_copy = pltpu.make_async_copy(unit_sum.at[0], r.grad_units, r.local_sem.at[2])
    unit_copy.start()

    small_copies.arrive()
    part = small_seq[0]
    for block in range(1, S):
        part = part + small_seq[block]
    for k in range(4):
        height = D // 128
        small[k : k + 1, :] = unpacked(part[k * height : (k + 1) * height], height)
    small[4:8, :] = jnp.zeros((4, D), F32)

    out_spread.finish()
    out_copy = pltpu.make_async_copy(out_sum.at[0], r.grad_out, r.local_sem.at[3])
    out_copy.start()
    in_spread.over_cores()
    in_spread.finish()
    in_copy = pltpu.make_async_copy(in_sum.at[0], r.grad_in, r.local_sem.at[4])
    in_copy.start()
    for copy in (result_copy, grad_copy, unit_copy, out_copy, in_copy):
        copy.wait()
    links.close()


def finish_kernel(T, names, *refs):
    r = types.SimpleNamespace(**dict(zip(names, refs)))
    copies = [
        pltpu.make_async_copy(source, target, r.local_sem.at[index])
        for index, (source, target) in enumerate(
            ((r.result_in, r.result), (r.grad_tokens_in, r.grad_tokens))
        )
    ]
    for copy in copies:
        copy.start()
    D_rows, lanes = (r.glu.shape[3], r.glu.shape[4])
    r.glu[0] = r.units_in[:, :, 0:D_rows, :lanes].astype(F32)
    r.glu[1] = r.units_in[:, :, 0:D_rows, lanes:].astype(F32)
    r.down[...] = r.units_in[:, :, D_rows:, :].astype(F32)
    r.out[...] = r.out_in[...].astype(F32)
    r.in_[...] = r.in_in[...].astype(F32)
    r.gain[...] = r.small[0:1, :]
    r.skip[...] = r.small[1:2, :]
    n = r.decay_log.shape[1]
    N = T * n
    t = lax.axis_index("tp")

    def mine(row, first):
        own = row[:, first : first + n]
        for z in range(1, T):
            own = jnp.where(t == z, row[:, first + z * n : first + z * n + n], own)
        return own

    lam_re, lam_im, gamma = decay_terms(r.decay_log[...], r.angle[...])
    g_re = mine(r.small[2:3, :], 0)
    g_im = mine(r.small[2:3, :], N)
    g_gamma = mine(r.small[3:4, :], 0)
    rate_step = jnp.exp(r.decay_log[...])
    r.decay[...] = rate_step * (
        g_gamma * (1.0 - fall(2.0 * rate_step)) / gamma - g_re * lam_re - g_im * lam_im
    )
    r.turn[...] = g_im * lam_re - g_re * lam_im
    for copy in copies:
        copy.wait()


def fall(value):
    series = jnp.ones_like(value)
    for order in range(12, 1, -1):
        series = 1.0 - value / order * series
    return jnp.where(value < 0.5, value * series, 1.0 - jnp.exp(-value))


def decay_terms(decay_log, angle):
    rate_step = jnp.exp(decay_log)
    radius = 1.0 - fall(rate_step)
    return (radius * jnp.cos(angle), radius * jnp.sin(angle), jnp.sqrt(fall(2.0 * rate_step)))


def local(
    S,
    T,
    tokens,
    ln_gain,
    in_proj,
    decay_log,
    angle,
    out_proj,
    skip,
    glu_proj,
    down_proj,
    lengths,
    cotangent,
):
    R, D = tokens.shape
    n = in_proj.shape[2]
    N = n * T
    units = down_proj.shape[0]
    C = S // 2
    fused = (
        S == 8
        and T % 2 == 0
        and T > 2
        and 2 * n == 128
        and 2 * units == D
        and all(size % (16 * S) == 0 for size in (D, 2 * n, units))
    )
    vmem = pl.BlockSpec(memory_space=pltpu.VMEM)
    anywhere = pl.BlockSpec(memory_space=pl.ANY)
    hbm = pl.BlockSpec(memory_space=pltpu.HBM)
    ins = dict(
        lengths=(lengths, hbm),
        tokens=(tokens, hbm),
        cot=(cotangent, hbm),
        gain=(ln_gain.reshape(1, D), hbm),
        skip=(skip, hbm),
    )
    outs = dict(
        result=((R, D), BF16, anywhere),
        grad_tokens=((R, D), F32, anywhere),
        small=((8, D), F32, vmem),
    )
    scratch = dict(
        gain_row=((1, D), F32),
        skip_row=((D,), BF16),
        tokens_raw=((R, D), BF16),
        cot_raw=((R, D), BF16),
        turn=((BLOCK, BLOCK), BF16),
        tokens_in=((R, D), BF16),
        cot_in=((R, D), BF16),
        centred=((R, D), F32),
        inv_std=((R, 128), F32),
        normed=((R, D), BF16),
        proj=((R, 2 * N), F32),
        keep=((R, 128), F32),
        keep_next=((R, 128), F32),
        state=((R, 2 * N), F32),
        state_low=((R, 2 * N), BF16),
        act=((R, D), BF16),
        d_gelu=((R, D), F32),
        d_act=((R, D), F32),
        summed=((R, D), F32),
        d_mixed=((R, D), BF16),
        d_proj=((R, 2 * N), BF16),
        hidden=((R, units), BF16),
        d_unit=((R, 2 * units), BF16),
        seg_carry=((SEGMENTS, 2 * N), F32),
        sums=((16, D), F32),
        state_all=((T, S, 2 * N // 128, 128), F32),
        adj_all=((T, S, 2 * N // 128, 128), F32),
    )
    in_rows = in_proj.transpose(0, 2, 1)
    if fused:
        unit_rows = D // S + units // S
        ins.update(
            decay_log=(decay_log.reshape(1, n), hbm),
            angle=(angle.reshape(1, n), hbm),
            in_proj=(in_rows.reshape(C, 2, 2 * n // S, D), hbm),
            out_proj=(out_proj.reshape(C, 2, 2 * n // S, D), hbm),
            glu_proj=(glu_proj.reshape(2, C, 2, D // S, units), hbm),
            down_proj=(down_proj.reshape(C, 2, units // S, D), hbm),
        )
        outs.update(
            grad_in=((C, 2, 2 * n // S, D), BF16, anywhere),
            grad_out=((C, 2, 2 * n // S, D), BF16, anywhere),
            grad_units=((C, 2, unit_rows, D), BF16, anywhere),
        )

        def whole(parts, rows, lead=()):
            return (lead + (parts, C, 2, rows, D), BF16)

        def halves(parts, rows, lead=()):
            return (lead + (parts, C, rows, D), BF16)

        def eighths(parts, rows, lead=()):
            return (lead + (C - 1, parts, rows, D), BF16)

        def own(parts, rows, lead=()):
            return (lead + (parts, rows, D), BF16)

        unit_sizes = (1, unit_rows, (T,))
        rate_sizes = (T, 2 * n // S)
        scratch.update(
            w_in=((2 * N, D), BF16),
            w_out=((2 * N, D), BF16),
            rates_all=((T, 8, 128), F32),
            decay_row=((1, n), F32),
            angle_row=((1, n), F32),
            in_slices=((T, C, 2, 2 * n // S, D), BF16),
            out_slices=((T, C, 2, 2 * n // S, D), BF16),
            unit_slices=((T, C, 2, unit_rows, D), BF16),
            grad_rates=((2 * N, D), BF16),
            small_tp=((T, 16, 128), F32),
            small_seq=((S, 16, 128), F32),
            unit_sums=((T - 1, 1, unit_rows, D), BF16),
            out_sums=((T - 1, 2 * n // S, D), BF16),
            in_sums=((T - 1, 2 * n // S, D), BF16),
            unit_sum=((1, C, 2, unit_rows, D), BF16),
            out_sum=((1, C, 2, 2 * n // S, D), BF16),
            in_sum=((1, C, 2, 2 * n // S, D), BF16),
            unit_full=whole(*unit_sizes),
            unit_halves=halves(*unit_sizes),
            unit_eighths=eighths(*unit_sizes),
            unit_summed=own(*unit_sizes),
            out_full=whole(*rate_sizes),
            out_halves=halves(*rate_sizes),
            out_eighths=eighths(*rate_sizes),
            out_summed=own(*rate_sizes),
            in_full=whole(*rate_sizes),
            in_halves=halves(*rate_sizes),
            in_eighths=eighths(*rate_sizes),
            in_summed=own(*rate_sizes),
        )
        links = 19 + 8 * T
    else:
        w_in = lax.all_gather(in_rows, "tp", axis=1, tiled=True).reshape(2 * N, D)
        w_out = lax.all_gather(out_proj, "tp", axis=1, tiled=True).reshape(2 * N, D)
        glu = lax.all_gather(glu_proj, "tp")
        rates = jnp.stack(
            [lax.all_gather(part, "tp", tiled=True) for part in decay_terms(decay_log, angle)]
            + [jnp.zeros((N,), F32)] * 5
        )
        ins.update(
            rates=(rates, vmem),
            w_in=(w_in, vmem),
            w_out=(w_out, vmem),
            glu=(jnp.concatenate([glu[:, 0], glu[:, 1]], 2), vmem),
            down=(lax.all_gather(down_proj, "tp"), vmem),
        )
        outs.update(
            grad_in=((2 * N, D), BF16, vmem),
            grad_out=((2 * N, D), BF16, vmem),
            grad_glu=((T, D, 2 * units), BF16, vmem),
            grad_down=((T, units, D), BF16, vmem),
        )
        links = 2 * T
    names = [*ins, *outs, *scratch, *dict(counts=0, local_sem=0, send_sem=0, recv_sem=0)]
    results = pl.pallas_call(
        functools.partial(layer_kernel, S, T, fused, names),
        out_shape=tuple(jax.ShapeDtypeStruct(shape, dtype) for shape, dtype, _ in outs.values()),
        in_specs=[spec for _, spec in ins.values()],
        out_specs=tuple(spec for _, _, spec in outs.values()),
        scratch_shapes=[pltpu.VMEM(shape, dtype) for shape, dtype in scratch.values()]
        + [
            pltpu.SMEM(lengths.shape, jnp.int32),
            pltpu.SemaphoreType.DMA((12,)),
            pltpu.SemaphoreType.DMA((links,)),
            pltpu.SemaphoreType.DMA((links,)),
        ],
        compiler_params=pltpu.CompilerParams(
            collective_id=0, has_side_effects=True, vmem_limit_bytes=46 * 2**20
        ),
    )(
        *[
            pltpu.with_memory_space_constraint(value, pltpu.HBM) if spec is hbm else value
            for value, spec in ins.values()
        ]
    )
    if fused:
        result, grad_tokens, small, grad_in, grad_out, grad_units = results
        ins = dict(
            result_in=(pltpu.with_memory_space_constraint(result, pltpu.VMEM), vmem),
            grad_tokens_in=(pltpu.with_memory_space_constraint(grad_tokens, pltpu.VMEM), vmem),
            small=(small, vmem),
            in_in=(grad_in, vmem),
            out_in=(grad_out, vmem),
            units_in=(grad_units, vmem),
            decay_log=(decay_log.reshape(1, n), vmem),
            angle=(angle.reshape(1, n), vmem),
        )
        outs = dict(
            result=((R, D), BF16, anywhere),
            grad_tokens=((R, D), F32, anywhere),
            gain=((1, D), F32, vmem),
            in_=((C, 2, 2 * n // S, D), F32, vmem),
            decay=((1, n), F32, vmem),
            turn=((1, n), F32, vmem),
            out=((C, 2, 2 * n // S, D), F32, vmem),
            skip=((1, D), F32, vmem),
            glu=((2, C, 2, D // S, units), F32, vmem),
            down=((C, 2, units // S, D), F32, vmem),
        )
        names = [*ins, *outs, *dict(local_sem=0)]
        result, grad_tokens, gain, in_, decay, turn, out, skip_sum, glu, down = pl.pallas_call(
            functools.partial(finish_kernel, T, names),
            out_shape=tuple(
                jax.ShapeDtypeStruct(shape, dtype) for shape, dtype, _ in outs.values()
            ),
            in_specs=[spec for _, spec in ins.values()],
            out_specs=tuple(spec for _, _, spec in outs.values()),
            scratch_shapes=[pltpu.SemaphoreType.DMA((2,))],
            compiler_params=pltpu.CompilerParams(vmem_limit_bytes=16 * 2**20),
        )(*[value for value, _ in ins.values()])
        return (
            result,
            grad_tokens,
            gain.reshape(D),
            in_.reshape(2, n, D).transpose(0, 2, 1),
            decay.reshape(n),
            turn.reshape(n),
            out.reshape(2, n, D),
            skip_sum.reshape(D),
            glu.reshape(2, D, units),
            down.reshape(units, D),
        )
    result, grad_tokens, small, grad_in, grad_out, grad_glu, grad_down = results
    small = lax.psum(small, ("seq", "tp"))

    def reduced(part):
        part = lax.psum_scatter(part, "tp", scatter_dimension=0, tiled=True)
        return lax.psum(part, "seq").astype(F32)

    def by_tp(grad):
        return reduced(grad.reshape(2, T, n, D).transpose(1, 0, 2, 3).reshape(T * 2, n, D))

    grad_glu = reduced(grad_glu)[0].reshape(D, 2, units).transpose(1, 0, 2)
    grad_down = reduced(grad_down)[0]

    def mine(row):
        return lax.dynamic_slice_in_dim(row, lax.axis_index("tp") * n, n)

    g_re, g_im, g_gamma = (mine(small[2, :N]), mine(small[2, N:]), mine(small[3, :N]))
    _, pull = jax.vjp(decay_terms, decay_log, angle)
    grad_decay, grad_angle = pull((g_re, g_im, g_gamma))
    return (
        result,
        grad_tokens,
        small[0],
        by_tp(grad_in).transpose(0, 2, 1),
        grad_decay,
        grad_angle,
        by_tp(grad_out),
        small[1],
        grad_glu,
        grad_down,
    )


def solution(mesh):
    in_specs = (
        P(("seq", "tp"), None),
        P(),
        P(None, None, "tp"),
        P("tp"),
        P("tp"),
        P(None, "tp", None),
        P(),
        P(None, None, "tp"),
        P("tp", None),
        P(),
        P(("seq", "tp"), None),
    )
    out_specs = (
        P(("seq", "tp"), None),
        P(("seq", "tp"), None),
        P(),
        P(None, None, "tp"),
        P("tp"),
        P("tp"),
        P(None, "tp", None),
        P(),
        P(None, None, "tp"),
        P("tp", None),
    )
    return jax.shard_map(
        functools.partial(local, mesh.shape["seq"], mesh.shape["tp"]),
        mesh=mesh,
        in_specs=in_specs,
        out_specs=out_specs,
        check_vma=False,
    )
```

```python
import functools
import types
import jax
import jax.numpy as jnp
from jax import lax
from jax.experimental import pallas as pl
from jax.experimental.pallas import tpu as pltpu
from jax.sharding import PartitionSpec as P

epsilon = 1e-05
MESH = pl.DeviceIdType.MESH
F32 = jnp.float32
BF16 = jnp.bfloat16
GROUPS = 2
SEGMENTS = 8 * GROUPS
BLOCK = SEGMENTS * SEGMENTS


def dot(left, right):
    return jnp.dot(left, right, preferred_element_type=F32)


def dot_nt(left, right):
    return lax.dot_general(left, right, (((1,), (1,)), ((), ())), preferred_element_type=F32)


def complex_mul(left_re, left_im, right_re, right_im):
    return (left_re * right_re - left_im * right_im, left_re * right_im + left_im * right_re)


def dot_tn(left, right):
    return lax.dot_general(left, right, (((0,), (0,)), ((), ())), preferred_element_type=F32)


def power(base, exponent):
    result = None
    square = base
    while exponent:
        if exponent & 1:
            result = square if result is None else complex_mul(*result, *square)
        exponent >>= 1
        if exponent:
            square = complex_mul(*square, *square)
    return result


class Links:
    def __init__(self, send_sem, recv_sem):
        self.send_sem = send_sem
        self.recv_sem = recv_sem
        self.groups = []

    def group(self, whole):
        group = Group(self, len(self.groups), whole)
        self.groups.append(group)
        return group

    def send(self, whole, copies):
        group = self.group(whole)
        for source, target, device in copies:
            group.add(source, target, device)
        return group

    def close(self):
        for group in self.groups:
            group.last.wait_send()


class Group:
    def __init__(self, links, index, whole):
        self.links = links
        self.index = index
        self.whole = whole

    def copy(self, source, target, device):
        return pltpu.make_async_remote_copy(
            src_ref=source,
            dst_ref=target,
            send_sem=self.links.send_sem.at[self.index],
            recv_sem=self.links.recv_sem.at[self.index],
            device_id=device,
            device_id_type=MESH,
        )

    def add(self, source, target, device):
        self.copy(source, target, device).start()
        self.last = self.copy(self.whole, self.whole, device)

    def arrive(self):
        self.last.wait_recv()


class Gather:
    def __init__(self, place, buffer, first, last):
        self.place = place
        self.buffer = buffer
        self.slots = range(first, last)
        self.part = buffer.at[pl.ds(first, last - first)]

    def over_tp(self):
        p = self.place
        self.copies = p.links.send(
            self.part.at[:, p.chip, p.core],
            [
                (
                    self.buffer.at[0, p.chip, p.core],
                    self.buffer.at[slot, p.chip, p.core],
                    (p.s, lax.rem(p.t + p.T - slot, p.T)),
                )
                for slot in self.slots
            ],
        )

    def over_plane(self):
        p = self.place
        self.copies.arrive()
        mine = self.part.at[:, p.chip, p.core]
        self.copies = p.links.send(
            self.part.at[:, pl.ds(0, len(p.chips)), p.core],
            [(mine, mine, device) for _, device in p.chips],
        )

    def over_cores(self):
        p = self.place
        self.copies.arrive()
        mine = self.part.at[:, :, p.core]
        self.copies = p.links.send(mine, [(mine, mine, p.sibling)])

    def finish(self):
        self.copies.arrive()


class Reduce:
    def __init__(self, place, full, halves, eighths, summed):
        self.place = place
        self.full = full
        self.halves = halves
        self.eighths = eighths
        self.summed = summed

    def over_cores(self):
        p = self.place
        self.copies = p.links.send(
            self.halves, [(self.full.at[:, :, 1 - p.core], self.halves, p.sibling)]
        )

    def over_plane(self):
        p = self.place
        self.copies.arrive()
        parts, chips = self.halves.shape[:2]

        @pl.loop(0, parts * chips)
        def _(index):
            part, chip = (lax.div(index, chips), lax.rem(index, chips))
            self.halves[part, chip] = (
                self.full[part, chip, p.core].astype(F32) + self.halves[part, chip].astype(F32)
            ).astype(BF16)

        self.copies = p.links.send(
            self.eighths,
            [
                (self.halves.at[:, chip], self.eighths.at[k], device)
                for k, (chip, device) in enumerate(p.chips)
            ],
        )

    def sum_plane(self):
        p = self.place
        self.copies.arrive()

        @pl.loop(0, self.halves.shape[0])
        def _(part):
            total = self.halves[part, p.chip].astype(F32)
            for k in range(len(p.chips)):
                total = total + self.eighths[k, part].astype(F32)
            self.summed[part] = total.astype(BF16)


class Reduce2(Reduce):
    def __init__(self, place, full, halves, eighths, summed):
        super().__init__(place, full, halves, eighths, summed)
        self.rows = halves.shape[2] // 2
        self.ours = halves.at[:, :, pl.ds(0, self.rows)]
        self.theirs = halves.at[:, :, pl.ds(self.rows, self.rows)]

    def sum_cores(self, chip):
        self.halves[0, chip] = (
            self.full[0, chip, self.place.core].astype(F32) + self.halves[0, chip].astype(F32)
        ).astype(BF16)

    def over_plane(self):
        p = self.place
        self.copies.arrive()
        self.sum_cores(p.by_x)
        self.sum_cores(p.by_y)
        self.sum_cores(p.by_xy)
        self.copies = p.links.send(
            self.eighths.at[pl.ds(0, 2)],
            [
                (part.at[0, chip], self.eighths.at[index, 0, rows], device)
                for index, part, chip, rows, device in (
                    (0, self.ours, p.by_x, pl.ds(0, self.rows), p.x_device),
                    (1, self.ours, p.by_xy, pl.ds(0, self.rows), p.x_device),
                    (0, self.theirs, p.by_y, pl.ds(self.rows, self.rows), p.y_device),
                    (1, self.theirs, p.by_xy, pl.ds(self.rows, self.rows), p.y_device),
                )
            ],
        )
        self.sum_cores(p.chip)

    def turn_plane(self):
        p = self.place
        self.copies.arrive()
        n = self.rows
        for index, chip in ((0, p.chip), (1, p.by_y)):
            self.halves[0, chip, 0:n] = (
                self.halves[0, chip, 0:n].astype(F32) + self.eighths[index, 0, 0:n].astype(F32)
            ).astype(BF16)
        for index, chip in ((0, p.chip), (1, p.by_x)):
            self.halves[0, chip, n:] = (
                self.halves[0, chip, n:].astype(F32) + self.eighths[index, 0, n:].astype(F32)
            ).astype(BF16)
        self.copies = p.links.send(
            self.eighths.at[2],
            [
                (self.ours.at[0, p.by_y], self.eighths.at[2, 0, pl.ds(0, n)], p.y_device),
                (self.theirs.at[0, p.by_x], self.eighths.at[2, 0, pl.ds(n, n)], p.x_device),
            ],
        )

    def sum_plane(self):
        p = self.place
        self.copies.arrive()
        self.summed[0] = (
            self.halves[0, p.chip].astype(F32) + self.eighths[2, 0].astype(F32)
        ).astype(BF16)


class Spread:
    def __init__(self, place, buffer):
        self.place = place
        self.buffer = buffer

    def over_plane(self):
        p = self.place
        mine = self.buffer.at[:, p.chip, p.core]
        self.copies = p.links.send(
            self.buffer.at[:, pl.ds(0, len(p.chips)), p.core],
            [(mine, mine, device) for _, device in p.chips],
        )

    def over_cores(self):
        p = self.place
        self.copies.arrive()
        mine = self.buffer.at[:, :, p.core]
        self.copies = p.links.send(mine, [(mine, mine, p.sibling)])

    def finish(self):
        self.copies.arrive()


class Place:
    def __init__(self, S, T, links):
        self.S, self.T, self.links = (S, T, links)
        self.s = lax.axis_index("seq")
        self.t = lax.axis_index("tp")
        C = S // 2
        self.core = lax.rem(self.s, 2)
        self.chip = lax.div(self.s, 2)
        self.sibling = (self.chip * 2 + 1 - self.core, self.t)
        x = lax.rem(self.chip, 2)
        y = lax.div(self.chip, 2)
        self.by_x = y * 2 + 1 - x
        self.by_y = (1 - y) * 2 + x
        self.by_xy = (1 - y) * 2 + 1 - x
        self.x_device = (self.by_x * 2 + self.core, self.t)
        self.y_device = (self.by_y * 2 + self.core, self.t)
        self.chips = []
        for k in range(1, C):
            chip = lax.rem(self.chip + k, C)
            self.chips.append((chip, (chip * 2 + self.core, self.t)))


def layer_kernel(S, T, fused, names, *refs):
    r = types.SimpleNamespace(**dict(zip(names, refs)))
    links = Links(r.send_sem, r.recv_sem)
    place = Place(S, T, links)
    lengths = r.counts
    tokens = r.tokens_raw
    cot = r.cot_raw
    result = r.tokens_raw
    grad_tokens = r.d_gelu
    turn = r.turn
    tokens_in = r.tokens_in
    cot_in = r.cot_in
    centred = r.centred
    inv_std = r.inv_std
    normed = r.normed
    proj = r.proj
    keep = r.keep
    keep_next = r.keep_next
    state = r.state
    state_low = r.state_low
    act = r.act
    d_gelu = r.d_gelu
    d_act = r.d_act
    summed = r.summed
    d_mixed = r.d_mixed
    adjoint = r.summed
    d_proj = r.d_proj
    hidden = r.hidden
    d_unit = r.d_unit
    seg_carry, sums = (r.seg_carry, r.sums)
    w_in, w_out = (r.w_in, r.w_out)
    R, D = tokens.shape
    N = w_in.shape[0] // 2
    n = N // T
    L = R // SEGMENTS
    s = place.s
    t = place.t
    first = (s * T + t) * R

    peers_tp = [lax.rem(t + k, T) for k in range(1, T)]
    peers_seq = [lax.rem(s + k, S) for k in range(1, S)]
    barrier = pltpu.get_barrier_semaphore()
    for peer in peers_tp:
        pl.semaphore_signal(barrier, inc=1, device_id=(s, peer), device_id_type=MESH)
    for peer in peers_seq:
        pl.semaphore_signal(barrier, inc=1, device_id=(peer, t), device_id_type=MESH)

    fetched = [
        pltpu.make_async_copy(source, target, r.local_sem.at[index])
        for index, (source, target) in enumerate(
            ((r.tokens, tokens), (r.cot, cot), (r.gain, r.gain_row), (r.skip, r.skip_row), (r.lengths, r.counts))
        )
    ]
    if fused:
        in_slices, out_slices, unit_slices = (r.in_slices, r.out_slices, r.unit_slices)
        units = r.down_proj.shape[2] * S
        D_rows = r.glu_proj.shape[3]
        gated_rows = unit_slices.at[0, :, :, pl.ds(0, D_rows)]
        weights = [
            pltpu.make_async_copy(source, target, r.local_sem.at[5 + index])
            for index, (source, target) in enumerate(
                (
                    (r.decay_log, r.decay_row),
                    (r.angle, r.angle_row),
                    (r.in_proj, in_slices.at[0]),
                    (r.out_proj, out_slices.at[0]),
                    (r.glu_proj.at[0], gated_rows.at[:, :, :, pl.ds(0, units)]),
                    (r.glu_proj.at[1], gated_rows.at[:, :, :, pl.ds(units, units)]),
                    (r.down_proj, unit_slices.at[0, :, :, pl.ds(D_rows, units // S)]),
                )
            )
        ]
        for copy in weights:
            copy.start()
    for copy in fetched:
        copy.start()
    if fused:
        rates_all = r.rates_all
        rates_all[t] = jnp.zeros(rates_all.shape[1:], F32)
        gather_in = Gather(place, in_slices, 1, T)
        gather_out = Gather(place, out_slices, 1, T)
        gather_units = [Gather(place, unit_slices, slot, slot + 1) for slot in range(1, T)]
        for copy in weights:
            copy.wait()
        for index, row in enumerate(decay_terms(r.decay_row[...], r.angle_row[...])):
            rates_all[t, index : index + 1, 0:n] = row
        pl.semaphore_wait(barrier, T - 1 + S - 1)
        gather_in.over_tp()
        rate_copies = links.send(
            rates_all.at[pl.ds(0, T - 1)],
            [(rates_all.at[t], rates_all.at[t], (s, peer)) for peer in peers_tp],
        )

    for copy in fetched[2:]:
        copy.wait()
    starts = []
    total = jnp.int32(0)
    for index in range(lengths.shape[0]):
        starts.append(total)
        total = total + lengths[index]

    def keeps(position):
        hit = position == starts[0]
        for start in starts[1:]:
            hit = hit | (position == start)
        return jnp.where(hit, 0.0, 1.0)

    def clear(low, high):
        hit = (starts[0] >= low) & (starts[0] < high)
        for start in starts[1:]:
            hit = hit | ((start >= low) & (start < high))
        return jnp.where(hit, 0.0, 1.0)

    gain_row = r.gain_row[...]
    skip_row = r.skip_row[...].astype(F32).reshape(1, D)

    down_index = lax.broadcasted_iota(jnp.int32, (BLOCK, BLOCK), 0)
    across_index = lax.broadcasted_iota(jnp.int32, (BLOCK, BLOCK), 1)
    turned = lax.rem(down_index, SEGMENTS) * SEGMENTS + lax.div(down_index, SEGMENTS)
    turn[...] = jnp.where(turned == across_index, 1.0, 0.0).astype(BF16)

    def pieces(block):
        return [
            pl.ds(pl.multiple_of(run * L + block * SEGMENTS, SEGMENTS), SEGMENTS)
            for run in range(SEGMENTS)
        ]

    def taken(ref, block):
        return dot(turn[...], jnp.concatenate([ref[piece, :] for piece in pieces(block)], 0))

    def block_rows(tile):
        return pl.ds(pl.multiple_of(tile * BLOCK, BLOCK), BLOCK)

    def norm_tile(tile):
        rows = block_rows(tile)
        x = taken(tokens, tile)
        tokens_in[rows, :] = x.astype(BF16)
        mean = jnp.mean(x, 1, keepdims=True)
        inv = lax.rsqrt(jnp.mean(x * x, 1, keepdims=True) - mean * mean + epsilon)
        c = (x - mean) * inv
        centred[rows, :] = c
        inv_std[rows, :] = jnp.broadcast_to(inv, (BLOCK, 128))
        n_rows = (c * gain_row).astype(BF16)
        normed[rows, :] = n_rows

    def cot_tile(tile):
        rows = block_rows(tile)
        cot_rows = taken(cot, tile).astype(BF16)
        cot_in[rows, :] = cot_rows
        index = tile * BLOCK + lax.broadcasted_iota(jnp.int32, (BLOCK, 128), 0)
        position = first + lax.rem(index, SEGMENTS) * L + lax.div(index, SEGMENTS)
        keep[rows, :] = keeps(position)
        keep_next[rows, :] = keeps(position + 1)

    fetched[0].wait()
    pl.loop(0, R // BLOCK)(norm_tile)
    if fused:
        gather_in.over_plane()
        gather_out.over_tp()
        gather_units[0].over_tp()
    fetched[1].wait()
    pl.loop(0, R // BLOCK)(cot_tile)

    def assemble(slices, weight):
        for i in range(T):
            at = lax.rem(t + i, T) * n
            for part in range(2):
                weight[pl.ds(pl.multiple_of(part * N + at, n), n), :] = slices[
                    i, part * (S // 4) : (part + 1) * (S // 4)
                ].reshape(n, D)

    if fused:
        gather_in.over_cores()
        gather_units[1].over_tp()
        rate_copies.arrive()
        half = lax.broadcasted_iota(jnp.int32, (8, 128), 1) < n
        rate_rows = [rates_all[z] for z in range(T)]
        joined = jnp.concatenate(
            [
                jnp.where(half, rate_rows[z], pltpu.roll(rate_rows[z + 1], n, 1))
                for z in range(0, T, 2)
            ],
            1,
        )
        lam_re, lam_im, gamma = (joined[k : k + 1] for k in range(3))
        gather_in.finish()
        for gather in gather_units[2:]:
            gather.over_tp()
        gather_out.over_plane()
        assemble(in_slices, w_in)
    else:
        pl.semaphore_wait(barrier, T - 1 + S - 1)
        lam_re, lam_im, gamma = (r.rates[k : k + 1, :] for k in range(3))
    gamma_signed = jnp.concatenate([gamma, -gamma], 1)

    @pl.loop(0, R // BLOCK)
    def _(tile):
        rows = block_rows(tile)
        proj[rows, :] = dot_nt(normed[rows, :], w_in[...]) * gamma_signed

    low8_re = jnp.broadcast_to(lam_re, (8, N))
    low8_im = jnp.broadcast_to(lam_im, (8, N))

    def rows_of(group, step):
        return pl.ds(pl.multiple_of(step * SEGMENTS + group * 8, 8), 8)

    def spread(row):
        return jnp.concatenate([row] * (N // 128), 1)

    def scan_step(values, mask, add, sign):
        new_re, new_im = complex_mul(low8_re, sign * low8_im, *(value * mask for value in values))
        return (new_re + add[:, :N], new_im + add[:, N:])

    zero8 = jnp.zeros((8, N), F32)
    none = tuple((zero8, zero8) for _ in range(GROUPS))

    def forward_step(step, carry):
        return tuple(
            scan_step(
                carry[group],
                spread(keep[rows_of(group, step), :]),
                proj[rows_of(group, step), :],
                -1.0,
            )
            for group in range(GROUPS)
        )

    def segment_rows(finals):
        return [
            (finals[group][0][sub : sub + 1], finals[group][1][sub : sub + 1])
            for group in range(GROUPS)
            for sub in range(8)
        ]

    def fold(start, factor, items, masks, taken):
        before = []
        carry = start
        for (item_re, item_im), mask, take in zip(items, masks, taken):
            before.append(carry)
            moved = complex_mul(*factor, *carry)
            longer = (moved[0] * mask + item_re, moved[1] * mask + item_im)
            if take is None:
                carry = longer
            else:
                carry = tuple(jnp.where(take, new, old) for new, old in zip(longer, carry))
        return carry, before

    zero1 = (jnp.zeros((1, N), F32), jnp.zeros((1, N), F32))
    lam = (lam_re, lam_im)
    conj = (lam_re, -lam_im)

    def unpack(row):
        return (row[:, :N], row[:, N:])

    def packed(row, height):
        parts = [row[:, at : at + 128] for at in range(0, row.shape[1], 128)]
        return jnp.concatenate(parts + [parts[0]] * (height - len(parts)), 0)

    def unpacked(tile, height):
        return jnp.concatenate([tile[k : k + 1, :] for k in range(height)], 1)

    class Exchange:
        def __init__(self, own, factor, buffer, forward):
            self.forward = forward
            self.shift = 0 if forward else 1
            self.factor = power(factor, R)
            self.buffer = buffer
            buffer[t, s] = packed(jnp.concatenate(own, 1), 2 * N // 128)
            mine = buffer.at[t, s]
            self.copies = [
                links.send(
                    buffer.at[0], [(mine, mine, (peer, peer_tp)) for peer in [s, *peers_seq]]
                )
                for peer_tp in peers_tp
            ]
            self.copies.append(
                links.send(
                    buffer.at[0, pl.ds(0, S - 1)], [(mine, mine, (peer, t)) for peer in peers_seq]
                )
            )

        def carry(self):
            for copies in self.copies:
                copies.arrive()

            def order(count):
                return list(range(count)) if self.forward else list(range(count))[::-1]

            def ahead(block, z):
                mine, other = (s * T + t, block * T + z)
                return other < mine if self.forward else other > mine

            rows = [
                jnp.concatenate(
                    [unpacked(self.buffer[z, block], 2 * N // 128) for block in range(S)], 0
                )
                for z in range(T)
            ]
            block = lax.broadcasted_iota(jnp.int32, (S, N), 0)
            carry = (jnp.zeros((S, N), F32), jnp.zeros((S, N), F32))
            for z in order(T):
                low = (block * T + z) * R + self.shift
                mask = clear(low, low + R)
                item = (rows[z][:, :N], rows[z][:, N:])
                moved = complex_mul(*self.factor, *carry)
                longer = (moved[0] * mask + item[0], moved[1] * mask + item[1])
                mine = block == s
                taken = jnp.logical_or(jnp.logical_not(mine), ahead(s, z))
                carry = tuple(jnp.where(taken, new, old) for new, old in zip(longer, carry))
            result = zero1
            whole = power(self.factor, T)
            for b in order(S):
                low = b * T * R + self.shift
                mask = clear(low, low + T * R)
                moved = complex_mul(*whole, *result)
                longer = (
                    moved[0] * mask + carry[0][b : b + 1],
                    moved[1] * mask + carry[1][b : b + 1],
                )
                earlier = b < s if self.forward else b > s
                result = tuple(jnp.where(earlier, new, old) for new, old in zip(longer, result))
            inside = tuple(
                jnp.sum(jnp.where(block == s, part, 0.0), 0, keepdims=True) for part in carry
            )
            for z in order(T):
                low = (s * T + z) * R + self.shift
                mask = clear(low, low + R)
                moved = complex_mul(*self.factor, *result)
                longer = (moved[0] * mask, moved[1] * mask)
                result = tuple(
                    jnp.where(ahead(s, z), new, old) for new, old in zip(longer, result)
                )
            return (result[0] + inside[0], result[1] + inside[1])

    finals = segment_rows(lax.fori_loop(0, L, forward_step, none))
    seg_masks = [clear(first + index * L, first + (index + 1) * L) for index in range(SEGMENTS)]
    factor_seg = power(conj, L)
    own, _ = fold(zero1, factor_seg, finals, seg_masks, [None] * SEGMENTS)
    exchange = Exchange(own, conj, r.state_all, True)
    if fused:
        gather_units[0].over_plane()
        gather_out.over_cores()
    if fused:
        gather_units[1].over_plane()
        gather_out.finish()
        assemble(out_slices, w_out)
    carry = exchange.carry()
    _, entering = fold(carry, factor_seg, finals, seg_masks, [None] * SEGMENTS)
    for index, (row_re, row_im) in enumerate(entering):
        seg_carry[index : index + 1, :] = jnp.concatenate([row_re, row_im], 1)

    def write_state(step, carry):
        new = forward_step(step, carry)
        for group in range(GROUPS):
            state[rows_of(group, step), :] = jnp.concatenate(new[group], 1)
        return new

    def entering_groups():
        return tuple(
            unpack(seg_carry[group * 8 : group * 8 + 8, :]) for group in range(GROUPS)
        )

    lax.fori_loop(0, L, write_state, entering_groups())
    if fused:
        for gather in gather_units[2:]:
            gather.over_plane()

    @pl.loop(0, R // BLOCK)
    def _(tile):
        rows = block_rows(tile)
        low = state[rows, :].astype(BF16)
        state_low[rows, :] = low
        x = dot(low, w_out[...]) + skip_row * normed[rows, :].astype(F32)
        scale = 0.7978845608028654
        th = jnp.tanh(scale * (x + 0.044715 * x * x * x))
        half = 0.5 * (1.0 + th)
        a = (x * half).astype(BF16)
        act[rows, :] = a
        d_act[rows, :] = x
        summed[rows, :] = half

    if fused:
        reduces = [
            Reduce2(
                place,
                r.unit_full.at[i],
                r.unit_halves.at[i],
                r.unit_eighths.at[i],
                r.unit_summed.at[i],
            )
            for i in range(T)
        ]

    UNIT_ROWS = min(512, R)
    units = hidden.shape[1]
    unit_copies = links.group(r.unit_sums) if fused else None

    def unit_grads(i):
        c = lax.rem(t + i, T)
        gated_grad = dot_tn(act[...], d_unit[...]).astype(BF16)
        down_grad = dot_tn(hidden[...], cot_in[...]).astype(BF16)
        if fused:
            full = r.unit_full
            full[i, 0, :, :, 0:D_rows] = gated_grad.reshape(S // 2, 2, D_rows, 2 * units)
            full[i, 0, :, :, D_rows:] = down_grad.reshape(S // 2, 2, units // S, D)
            reduces[i].over_cores()
        else:
            r.grad_glu[c] = gated_grad
            r.grad_down[c] = down_grad

    def unit_sums(i):
        reduces[i].sum_plane()
        if i > 0:
            unit_copies.add(r.unit_summed.at[i], r.unit_sums.at[i - 1], (s, lax.rem(t + i, T)))

    for i in range(T):
        c = lax.rem(t + i, T)
        if fused:
            if i > 0:
                gather_units[i - 1].finish()
            if i < T - 1:
                gather_units[i].over_cores()
            w_gated = unit_slices[i, :, :, 0:D_rows].reshape(D, 2 * units)
            w_down = unit_slices[i, :, :, D_rows:].reshape(units, D)
        else:
            w_gated = r.glu[c]
            w_down = r.down[c]

        for tile in range(R // UNIT_ROWS):
            rows = slice(tile * UNIT_ROWS, (tile + 1) * UNIT_ROWS)
            both = dot(act[rows, :], w_gated)
            if i == 0:
                x = d_act[rows, :]
                half = summed[rows, :]
                slope = 1.5957691216057308 * (1.0 + 0.134145 * x * x)
                d_gelu[rows, :] = half + x * half * (1.0 - half) * slope
            value, gate = (both[:, :units], both[:, units:])
            sigma = 0.5 * jnp.tanh(0.5 * gate) + 0.5
            gated = value * sigma
            h = gated.astype(BF16)
            hidden[rows, :] = h
            d_h = dot_nt(cot_in[rows, :], w_down)
            d_both = jnp.concatenate(
                [(d_h * sigma).astype(BF16), (d_h * gated * (1.0 - sigma)).astype(BF16)], 1
            )
            d_unit[rows, :] = d_both
            added = dot(h, w_down)
            d_a = dot_nt(d_both, w_gated)
            if i > 0:
                added = added + summed[rows, :]
                d_a = d_a + d_act[rows, :]
            if i < T - 1:
                summed[rows, :] = added
                d_act[rows, :] = d_a
            else:
                d_m = (d_gelu[rows, :] * d_a).astype(BF16)
                d_mixed[rows, :] = d_m
                adjoint[rows, :] = dot_nt(d_m, w_out[...])
                out = (tokens_in[rows, :].astype(F32) + added).astype(BF16)
                for block in range(UNIT_ROWS // BLOCK):
                    turned = dot(turn[...], out[block * BLOCK : block * BLOCK + BLOCK])
                    turned = turned.astype(BF16)
                    for run, piece in enumerate(pieces(tile * (UNIT_ROWS // BLOCK) + block)):
                        result[piece, :] = turned[run * SEGMENTS : run * SEGMENTS + SEGMENTS]

        if fused and i > 0:
            reduces[i - 1].over_plane()
        unit_grads(i)
        if fused and i > 1:
            reduces[i - 2].turn_plane()
        if fused and i > 2:
            unit_sums(i - 3)

    result_copy = pltpu.make_async_copy(result, r.result, r.local_sem.at[0])
    result_copy.start()

    def backward_step(index, carry):
        step = L - 1 - index
        return tuple(
            scan_step(
                carry[group],
                spread(keep_next[rows_of(group, step), :]),
                adjoint[rows_of(group, step), :],
                1.0,
            )
            for group in range(GROUPS)
        )

    finals = segment_rows(lax.fori_loop(0, L, backward_step, none))[::-1]
    seg_masks = [
        clear(first + index * L + 1, first + (index + 1) * L + 1) for index in range(SEGMENTS)
    ][::-1]
    factor_seg = power(lam, L)
    own, _ = fold(zero1, factor_seg, finals, seg_masks, [None] * SEGMENTS)
    exchange = Exchange(own, lam, r.adj_all, False)
    if fused:
        reduces[T - 2].turn_plane()
        reduces[T - 1].over_plane()
    grad_out = dot_tn(state_low[...], d_mixed[...]).astype(BF16)

    def divide(grad, full):
        for i in range(T):
            at = lax.rem(t + i, T) * n
            for part in range(2):
                rows = pl.ds(pl.multiple_of(part * N + at, n), n)
                full[i, part * (S // 4) : (part + 1) * (S // 4)] = grad[rows, :].reshape(
                    S // 4, 2, -1, D
                )

    if fused:
        r.grad_rates[...] = grad_out
        divide(r.grad_rates, r.out_full)
        out_reduce = Reduce(place, r.out_full, r.out_halves, r.out_eighths, r.out_summed)
        out_reduce.over_cores()
        unit_sums(T - 3)
    else:
        r.grad_out[...] = grad_out
    carry = exchange.carry()
    if fused:
        reduces[T - 1].turn_plane()
        out_reduce.over_plane()
        unit_sums(T - 2)
    _, entering = fold(carry, factor_seg, finals, seg_masks, [None] * SEGMENTS)
    entering = entering[::-1]
    groups = tuple(
        tuple(
            jnp.concatenate([entering[group * 8 + sub][part] for sub in range(8)], 0)
            for part in range(2)
        )
        for group in range(GROUPS)
    )
    sums[...] = jnp.zeros_like(sums)

    def adjoint_step(step, carry, previous):
        new = []
        add_re = zero8
        add_im = zero8
        add_gamma = zero8
        for group in range(GROUPS):
            rows = rows_of(group, step)
            b = scan_step(carry[group], spread(keep_next[rows, :]), adjoint[rows, :], 1.0)
            new.append(b)
            adjoint[rows, :] = jnp.concatenate(b, 1)
            u = unpack(proj[rows, :])
            v = previous(group, step)
            mask = spread(keep[rows, :])
            add_re = add_re + mask * (b[0] * v[0] + b[1] * v[1])
            add_im = add_im + mask * (b[0] * v[1] - b[1] * v[0])
            add_gamma = add_gamma + b[0] * u[0] + b[1] * u[1]
        return tuple(new), (add_re, add_im, add_gamma)

    def adjoint_body(index, carry):
        values, totals = carry
        values, added = adjoint_step(
            L - 1 - index, values, lambda group, step: unpack(state[rows_of(group, step - 1), :])
        )
        return values, tuple(total + add for total, add in zip(totals, added))

    values, totals = lax.fori_loop(0, L - 1, adjoint_body, (groups, (zero8, zero8, zero8)))
    inside = entering_groups()
    _, added = adjoint_step(0, values, lambda group, step: inside[group])
    totals = [jnp.sum(total + add, 0, keepdims=True) for total, add in zip(totals, added)]

    d_proj[...] = (adjoint[...] * gamma_signed).astype(BF16)
    grad_in = dot_tn(d_proj[...], normed[...]).astype(BF16)
    if fused:
        r.grad_rates[...] = grad_in
        divide(r.grad_rates, r.in_full)
        in_reduce = Reduce(place, r.in_full, r.in_halves, r.in_eighths, r.in_summed)
        in_reduce.over_cores()
        out_reduce.sum_plane()
        out_copies = links.send(
            r.out_sums,
            [
                (r.out_summed.at[i], r.out_sums.at[i - 1], (s, lax.rem(t + i, T)))
                for i in range(1, T)
            ],
        )
        in_reduce.over_plane()
        unit_sums(T - 1)
    else:
        r.grad_in[...] = grad_in

    @pl.loop(0, R // BLOCK)
    def _(tile):
        rows = block_rows(tile)
        d_m = d_mixed[rows, :].astype(F32)
        d_n = dot(d_proj[rows, :], w_in[...]) + d_m * skip_row
        c = centred[rows, :]
        sums[0:8, :] += jnp.sum((d_n * c).reshape(BLOCK // 8, 8, D), 0)
        sums[8:16, :] += jnp.sum((d_m * normed[rows, :].astype(F32)).reshape(BLOCK // 8, 8, D), 0)
        d_c = d_n * gain_row
        mean = jnp.mean(d_c, 1, keepdims=True)
        cross = jnp.mean(d_c * c, 1, keepdims=True)
        inv = inv_std[rows, 0:1]
        out = cot_in[rows, :].astype(F32) + inv * (d_c - mean - c * cross)
        high = out.astype(BF16)
        out = dot(turn[...], high) + dot(turn[...], (out - high.astype(F32)).astype(BF16))
        for run, piece in enumerate(pieces(tile)):
            grad_tokens[piece, :] = out[run * SEGMENTS : run * SEGMENTS + SEGMENTS]

    grad_copy = pltpu.make_async_copy(grad_tokens, r.grad_tokens, r.local_sem.at[1])
    grad_copy.start()
    small = r.small
    small_rows = [
        jnp.sum(sums[0:8, :], 0, keepdims=True),
        jnp.sum(sums[8:16, :], 0, keepdims=True),
        jnp.concatenate(totals[:2], 1),
        jnp.concatenate([totals[2] / gamma, jnp.zeros_like(gamma)], 1),
    ]
    if not fused:
        for k, row in enumerate(small_rows):
            small[k : k + 1, :] = row
        small[4:8, :] = jnp.zeros((4, D), F32)
        links.close()
        result_copy.wait()
        grad_copy.wait()
        return

    small_tp, small_seq = (r.small_tp, r.small_seq)
    small_tp[t] = jnp.concatenate([packed(row, D // 128) for row in small_rows], 0)
    small_copies = links.send(
        small_tp.at[pl.ds(0, T - 1)],
        [(small_tp.at[t], small_tp.at[t], (s, peer)) for peer in peers_tp],
    )

    def total_of(own, buffer):
        total = own.astype(F32)
        for k in range(buffer.shape[0]):
            total = total + buffer[k].astype(F32)
        return total.astype(BF16)

    unit_sum, out_sum, in_sum = (r.unit_sum, r.out_sum, r.in_sum)
    unit_copies.arrive()
    unit_sum[0, place.chip, place.core] = total_of(r.unit_summed[0, 0], r.unit_sums.at[:, 0])
    unit_spread = Spread(place, unit_sum)
    unit_spread.over_plane()

    in_reduce.sum_plane()
    in_copies = links.send(
        r.in_sums,
        [(r.in_summed.at[i], r.in_sums.at[i - 1], (s, lax.rem(t + i, T))) for i in range(1, T)],
    )
    out_copies.arrive()
    out_sum[0, place.chip, place.core] = total_of(r.out_summed[0], r.out_sums)
    out_spread = Spread(place, out_sum)
    out_spread.over_plane()

    small_copies.arrive()
    part = small_tp[0]
    for z in range(1, T):
        part = part + small_tp[z]
    small_seq[s] = part
    small_copies = links.send(
        small_seq.at[pl.ds(0, S - 1)],
        [(small_seq.at[s], small_seq.at[s], (peer, t)) for peer in peers_seq],
    )

    unit_spread.over_cores()
    in_copies.arrive()
    in_sum[0, place.chip, place.core] = total_of(r.in_summed[0], r.in_sums)
    in_spread = Spread(place, in_sum)
    in_spread.over_plane()
    out_spread.over_cores()

    unit_spread.finish()
    unit_copy = pltpu.make_async_copy(unit_sum.at[0], r.grad_units, r.local_sem.at[2])
    unit_copy.start()

    small_copies.arrive()
    part = small_seq[0]
    for block in range(1, S):
        part = part + small_seq[block]
    for k in range(4):
        height = D // 128
        small[k : k + 1, :] = unpacked(part[k * height : (k + 1) * height], height)
    small[4:8, :] = jnp.zeros((4, D), F32)

    out_spread.finish()
    out_copy = pltpu.make_async_copy(out_sum.at[0], r.grad_out, r.local_sem.at[3])
    out_copy.start()
    in_spread.over_cores()
    in_spread.finish()
    in_copy = pltpu.make_async_copy(in_sum.at[0], r.grad_in, r.local_sem.at[4])
    in_copy.start()
    for copy in (result_copy, grad_copy, unit_copy, out_copy, in_copy):
        copy.wait()
    links.close()


def finish_kernel(T, names, *refs):
    r = types.SimpleNamespace(**dict(zip(names, refs)))
    copies = [
        pltpu.make_async_copy(source, target, r.local_sem.at[index])
        for index, (source, target) in enumerate(
            ((r.result_in, r.result), (r.grad_tokens_in, r.grad_tokens))
        )
    ]
    for copy in copies:
        copy.start()
    D_rows, lanes = (r.glu.shape[3], r.glu.shape[4])
    r.glu[0] = r.units_in[:, :, 0:D_rows, :lanes].astype(F32)
    r.glu[1] = r.units_in[:, :, 0:D_rows, lanes:].astype(F32)
    r.down[...] = r.units_in[:, :, D_rows:, :].astype(F32)
    r.out[...] = r.out_in[...].astype(F32)
    r.in_[...] = r.in_in[...].astype(F32)
    r.gain[...] = r.small[0:1, :]
    r.skip[...] = r.small[1:2, :]
    n = r.decay_log.shape[1]
    N = T * n
    t = lax.axis_index("tp")

    def mine(row, first):
        own = row[:, first : first + n]
        for z in range(1, T):
            own = jnp.where(t == z, row[:, first + z * n : first + z * n + n], own)
        return own

    lam_re, lam_im, gamma = decay_terms(r.decay_log[...], r.angle[...])
    g_re = mine(r.small[2:3, :], 0)
    g_im = mine(r.small[2:3, :], N)
    g_gamma = mine(r.small[3:4, :], 0)
    rate_step = jnp.exp(r.decay_log[...])
    r.decay[...] = rate_step * (
        g_gamma * (1.0 - fall(2.0 * rate_step)) / gamma - g_re * lam_re - g_im * lam_im
    )
    r.turn[...] = g_im * lam_re - g_re * lam_im
    for copy in copies:
        copy.wait()


def fall(value):
    series = jnp.ones_like(value)
    for order in range(12, 1, -1):
        series = 1.0 - value / order * series
    return jnp.where(value < 0.5, value * series, 1.0 - jnp.exp(-value))


def decay_terms(decay_log, angle):
    rate_step = jnp.exp(decay_log)
    radius = 1.0 - fall(rate_step)
    return (radius * jnp.cos(angle), radius * jnp.sin(angle), jnp.sqrt(fall(2.0 * rate_step)))


def local(
    S,
    T,
    tokens,
    ln_gain,
    in_proj,
    decay_log,
    angle,
    out_proj,
    skip,
    glu_proj,
    down_proj,
    lengths,
    cotangent,
):
    R, D = tokens.shape
    n = in_proj.shape[2]
    N = n * T
    units = down_proj.shape[0]
    C = S // 2
    fused = (
        S == 8
        and T % 2 == 0
        and T > 2
        and 2 * n == 128
        and 2 * units == D
        and all(size % (16 * S) == 0 for size in (D, 2 * n, units))
    )
    vmem = pl.BlockSpec(memory_space=pltpu.VMEM)
    anywhere = pl.BlockSpec(memory_space=pl.ANY)
    hbm = pl.BlockSpec(memory_space=pltpu.HBM)
    ins = dict(
        lengths=(lengths, hbm),
        tokens=(tokens, hbm),
        cot=(cotangent, hbm),
        gain=(ln_gain.reshape(1, D), hbm),
        skip=(skip, hbm),
    )
    outs = dict(
        result=((R, D), BF16, anywhere),
        grad_tokens=((R, D), F32, anywhere),
        small=((8, D), F32, vmem),
    )
    scratch = dict(
        gain_row=((1, D), F32),
        skip_row=((D,), BF16),
        tokens_raw=((R, D), BF16),
        cot_raw=((R, D), BF16),
        turn=((BLOCK, BLOCK), BF16),
        tokens_in=((R, D), BF16),
        cot_in=((R, D), BF16),
        centred=((R, D), F32),
        inv_std=((R, 128), F32),
        normed=((R, D), BF16),
        proj=((R, 2 * N), F32),
        keep=((R, 128), F32),
        keep_next=((R, 128), F32),
        state=((R, 2 * N), F32),
        state_low=((R, 2 * N), BF16),
        act=((R, D), BF16),
        d_gelu=((R, D), F32),
        d_act=((R, D), F32),
        summed=((R, D), F32),
        d_mixed=((R, D), BF16),
        d_proj=((R, 2 * N), BF16),
        hidden=((R, units), BF16),
        d_unit=((R, 2 * units), BF16),
        seg_carry=((SEGMENTS, 2 * N), F32),
        sums=((16, D), F32),
        state_all=((T, S, 2 * N // 128, 128), F32),
        adj_all=((T, S, 2 * N // 128, 128), F32),
    )
    in_rows = in_proj.transpose(0, 2, 1)
    if fused:
        unit_rows = D // S + units // S
        ins.update(
            decay_log=(decay_log.reshape(1, n), hbm),
            angle=(angle.reshape(1, n), hbm),
            in_proj=(in_rows.reshape(C, 2, 2 * n // S, D), hbm),
            out_proj=(out_proj.reshape(C, 2, 2 * n // S, D), hbm),
            glu_proj=(glu_proj.reshape(2, C, 2, D // S, units), hbm),
            down_proj=(down_proj.reshape(C, 2, units // S, D), hbm),
        )
        outs.update(
            grad_in=((C, 2, 2 * n // S, D), BF16, anywhere),
            grad_out=((C, 2, 2 * n // S, D), BF16, anywhere),
            grad_units=((C, 2, unit_rows, D), BF16, anywhere),
        )

        def whole(parts, rows, lead=()):
            return (lead + (parts, C, 2, rows, D), BF16)

        def halves(parts, rows, lead=()):
            return (lead + (parts, C, rows, D), BF16)

        def eighths(parts, rows, lead=()):
            return (lead + (C - 1, parts, rows, D), BF16)

        def own(parts, rows, lead=()):
            return (lead + (parts, rows, D), BF16)

        unit_sizes = (1, unit_rows, (T,))
        rate_sizes = (T, 2 * n // S)
        scratch.update(
            w_in=((2 * N, D), BF16),
            w_out=((2 * N, D), BF16),
            rates_all=((T, 8, 128), F32),
            decay_row=((1, n), F32),
            angle_row=((1, n), F32),
            in_slices=((T, C, 2, 2 * n // S, D), BF16),
            out_slices=((T, C, 2, 2 * n // S, D), BF16),
            unit_slices=((T, C, 2, unit_rows, D), BF16),
            grad_rates=((2 * N, D), BF16),
            small_tp=((T, 16, 128), F32),
            small_seq=((S, 16, 128), F32),
            unit_sums=((T - 1, 1, unit_rows, D), BF16),
            out_sums=((T - 1, 2 * n // S, D), BF16),
            in_sums=((T - 1, 2 * n // S, D), BF16),
            unit_sum=((1, C, 2, unit_rows, D), BF16),
            out_sum=((1, C, 2, 2 * n // S, D), BF16),
            in_sum=((1, C, 2, 2 * n // S, D), BF16),
            unit_full=whole(*unit_sizes),
            unit_halves=halves(*unit_sizes),
            unit_eighths=eighths(*unit_sizes),
            unit_summed=own(*unit_sizes),
            out_full=whole(*rate_sizes),
            out_halves=halves(*rate_sizes),
            out_eighths=eighths(*rate_sizes),
            out_summed=own(*rate_sizes),
            in_full=whole(*rate_sizes),
            in_halves=halves(*rate_sizes),
            in_eighths=eighths(*rate_sizes),
            in_summed=own(*rate_sizes),
        )
        links = 19 + 8 * T
    else:
        w_in = lax.all_gather(in_rows, "tp", axis=1, tiled=True).reshape(2 * N, D)
        w_out = lax.all_gather(out_proj, "tp", axis=1, tiled=True).reshape(2 * N, D)
        glu = lax.all_gather(glu_proj, "tp")
        rates = jnp.stack(
            [lax.all_gather(part, "tp", tiled=True) for part in decay_terms(decay_log, angle)]
            + [jnp.zeros((N,), F32)] * 5
        )
        ins.update(
            rates=(rates, vmem),
            w_in=(w_in, vmem),
            w_out=(w_out, vmem),
            glu=(jnp.concatenate([glu[:, 0], glu[:, 1]], 2), vmem),
            down=(lax.all_gather(down_proj, "tp"), vmem),
        )
        outs.update(
            grad_in=((2 * N, D), BF16, vmem),
            grad_out=((2 * N, D), BF16, vmem),
            grad_glu=((T, D, 2 * units), BF16, vmem),
            grad_down=((T, units, D), BF16, vmem),
        )
        links = 2 * T
    names = [*ins, *outs, *scratch, *dict(counts=0, local_sem=0, send_sem=0, recv_sem=0)]
    results = pl.pallas_call(
        functools.partial(layer_kernel, S, T, fused, names),
        out_shape=tuple(jax.ShapeDtypeStruct(shape, dtype) for shape, dtype, _ in outs.values()),
        in_specs=[spec for _, spec in ins.values()],
        out_specs=tuple(spec for _, _, spec in outs.values()),
        scratch_shapes=[pltpu.VMEM(shape, dtype) for shape, dtype in scratch.values()]
        + [
            pltpu.SMEM(lengths.shape, jnp.int32),
            pltpu.SemaphoreType.DMA((12,)),
            pltpu.SemaphoreType.DMA((links,)),
            pltpu.SemaphoreType.DMA((links,)),
        ],
        compiler_params=pltpu.CompilerParams(
            collective_id=0, has_side_effects=True, vmem_limit_bytes=46 * 2**20
        ),
    )(
        *[
            pltpu.with_memory_space_constraint(value, pltpu.HBM) if spec is hbm else value
            for value, spec in ins.values()
        ]
    )
    if fused:
        result, grad_tokens, small, grad_in, grad_out, grad_units = results
        ins = dict(
            result_in=(pltpu.with_memory_space_constraint(result, pltpu.VMEM), vmem),
            grad_tokens_in=(pltpu.with_memory_space_constraint(grad_tokens, pltpu.VMEM), vmem),
            small=(small, vmem),
            in_in=(grad_in, vmem),
            out_in=(grad_out, vmem),
            units_in=(grad_units, vmem),
            decay_log=(decay_log.reshape(1, n), vmem),
            angle=(angle.reshape(1, n), vmem),
        )
        outs = dict(
            result=((R, D), BF16, anywhere),
            grad_tokens=((R, D), F32, anywhere),
            gain=((1, D), F32, vmem),
            in_=((C, 2, 2 * n // S, D), F32, vmem),
            decay=((1, n), F32, vmem),
            turn=((1, n), F32, vmem),
            out=((C, 2, 2 * n // S, D), F32, vmem),
            skip=((1, D), F32, vmem),
            glu=((2, C, 2, D // S, units), F32, vmem),
            down=((C, 2, units // S, D), F32, vmem),
        )
        names = [*ins, *outs, *dict(local_sem=0)]
        result, grad_tokens, gain, in_, decay, turn, out, skip_sum, glu, down = pl.pallas_call(
            functools.partial(finish_kernel, T, names),
            out_shape=tuple(
                jax.ShapeDtypeStruct(shape, dtype) for shape, dtype, _ in outs.values()
            ),
            in_specs=[spec for _, spec in ins.values()],
            out_specs=tuple(spec for _, _, spec in outs.values()),
            scratch_shapes=[pltpu.SemaphoreType.DMA((2,))],
            compiler_params=pltpu.CompilerParams(vmem_limit_bytes=16 * 2**20),
        )(*[value for value, _ in ins.values()])
        return (
            result,
            grad_tokens,
            gain.reshape(D),
            in_.reshape(2, n, D).transpose(0, 2, 1),
            decay.reshape(n),
            turn.reshape(n),
            out.reshape(2, n, D),
            skip_sum.reshape(D),
            glu.reshape(2, D, units),
            down.reshape(units, D),
        )
    result, grad_tokens, small, grad_in, grad_out, grad_glu, grad_down = results
    small = lax.psum(small, ("seq", "tp"))

    def reduced(part):
        part = lax.psum_scatter(part, "tp", scatter_dimension=0, tiled=True)
        return lax.psum(part, "seq").astype(F32)

    def by_tp(grad):
        return reduced(grad.reshape(2, T, n, D).transpose(1, 0, 2, 3).reshape(T * 2, n, D))

    grad_glu = reduced(grad_glu)[0].reshape(D, 2, units).transpose(1, 0, 2)
    grad_down = reduced(grad_down)[0]

    def mine(row):
        return lax.dynamic_slice_in_dim(row, lax.axis_index("tp") * n, n)

    g_re, g_im, g_gamma = (mine(small[2, :N]), mine(small[2, N:]), mine(small[3, :N]))
    _, pull = jax.vjp(decay_terms, decay_log, angle)
    grad_decay, grad_angle = pull((g_re, g_im, g_gamma))
    return (
        result,
        grad_tokens,
        small[0],
        by_tp(grad_in).transpose(0, 2, 1),
        grad_decay,
        grad_angle,
        by_tp(grad_out),
        small[1],
        grad_glu,
        grad_down,
    )


def solution(mesh):
    in_specs = (
        P(("seq", "tp"), None),
        P(),
        P(None, None, "tp"),
        P("tp"),
        P("tp"),
        P(None, "tp", None),
        P(),
        P(None, None, "tp"),
        P("tp", None),
        P(),
        P(("seq", "tp"), None),
    )
    out_specs = (
        P(("seq", "tp"), None),
        P(("seq", "tp"), None),
        P(),
        P(None, None, "tp"),
        P("tp"),
        P("tp"),
        P(None, "tp", None),
        P(),
        P(None, None, "tp"),
        P("tp", None),
    )
    return jax.shard_map(
        functools.partial(local, mesh.shape["seq"], mesh.shape["tp"]),
        mesh=mesh,
        in_specs=in_specs,
        out_specs=out_specs,
        check_vma=False,
    )
```
